32 devices in a mesh: seq: 4 (over z), tp: 2 (over x), rows: 4 (over y, core).
Axes of the slice: x: 2, y: 2, z: 4, core: 2. Of those that a mesh axis runs over, the one named last changes fastest.
Arguments:
- inputs: bfloat16 [8, 1024, 1024], P('rows', 'seq'), may hold values from -6 to 6
- norm_gain_one: float32 [1024], replicated, may hold values from 0.5 to 1.5
- norm_bias_one: float32 [1024], replicated, may hold values from -1.75 to 1.75
- query_one: bfloat16 [1024, 1024], P(None, 'tp'), may hold values from -0.375 to 0.375
- key_one: bfloat16 [1024, 1024], P(None, 'tp'), may hold values from -0.1875 to 0.1875
- value_one: bfloat16 [1024, 1024], P(None, 'tp'), may hold values from -0.1875 to 0.1875
- output_one: bfloat16 [1024, 1024], P('tp'), may hold values from -0.75 to 0.75
- up_one: bfloat16 [1024, 4096], P(None, 'tp'), may hold values from -0.1875 to 0.1875
- up_bias_one: float32 [4096], P('tp'), may hold values from -3 to 3
- down_one: bfloat16 [4096, 1024], P('tp'), may hold values from -0.09375 to 0.09375
- down_bias_one: float32 [1024], replicated, may hold values from -3.5 to 3.5
- norm_gain_two: float32 [1024], replicated, may hold values from 0.5 to 1.5
- norm_bias_two: float32 [1024], replicated, may hold values from -1.75 to 1.75
- query_two: bfloat16 [1024, 1024], P(None, 'tp'), may hold values from -0.375 to 0.375
- key_two: bfloat16 [1024, 1024], P(None, 'tp'), may hold values from -0.1875 to 0.1875
- value_two: bfloat16 [1024, 1024], P(None, 'tp'), may hold values from -0.1875 to 0.1875
- output_two: bfloat16 [1024, 1024], P('tp'), may hold values from -0.75 to 0.75
- up_two: bfloat16 [1024, 4096], P(None, 'tp'), may hold values from -0.1875 to 0.1875
- up_bias_two: float32 [4096], P('tp'), may hold values from -3 to 3
- down_two: bfloat16 [4096, 1024], P('tp'), may hold values from -0.09375 to 0.09375
- down_bias_two: float32 [1024], replicated, may hold values from -3.5 to 3.5
- cotangent: bfloat16 [8, 1024, 1024], P('rows', 'seq'), may hold values from -6 to 6
Outputs:
- outputs: bfloat16 [8, 1024, 1024], P('rows', 'seq')
- input_grad: bfloat16 [8, 1024, 1024], P('rows', 'seq')
- grad_norm_gain_one: float32 [1024], P(('seq', 'rows'))
- grad_norm_bias_one: float32 [1024], P(('seq', 'rows'))
- grad_query_one: float32 [1024, 1024], P(('seq', 'rows'), 'tp')
- grad_key_one: float32 [1024, 1024], P(('seq', 'rows'), 'tp')
- grad_value_one: float32 [1024, 1024], P(('seq', 'rows'), 'tp')
- grad_output_one: float32 [1024, 1024], P('tp', ('seq', 'rows'))
- grad_up_one: float32 [1024, 4096], P(('seq', 'rows'), 'tp')
- grad_up_bias_one: float32 [4096], P(('tp', 'seq', 'rows'))
- grad_down_one: float32 [4096, 1024], P('tp', ('seq', 'rows'))
- grad_down_bias_one: float32 [1024], P(('seq', 'rows'))
- grad_norm_gain_two: float32 [1024], P(('seq', 'rows'))
- grad_norm_bias_two: float32 [1024], P(('seq', 'rows'))
- grad_query_two: float32 [1024, 1024], P(('seq', 'rows'), 'tp')
- grad_key_two: float32 [1024, 1024], P(('seq', 'rows'), 'tp')
- grad_value_two: float32 [1024, 1024], P(('seq', 'rows'), 'tp')
- grad_output_two: float32 [1024, 1024], P('tp', ('seq', 'rows'))
- grad_up_two: float32 [1024, 4096], P(('seq', 'rows'), 'tp')
- grad_up_bias_two: float32 [4096], P(('tp', 'seq', 'rows'))
- grad_down_two: float32 [4096, 1024], P('tp', ('seq', 'rows'))
- grad_down_bias_two: float32 [1024], P(('seq', 'rows'))
The draws below stay inside these ranges and needn't reach their ends.
All inputs are finite; a program needn't handle non-finite values.
Results may differ from the reference program's by a relative error of at most 0.04.
Values may be sent and summed in bfloat16 or wider, within the bound.
No kernel may reach another device: no remote copies, remote signals or barrier semaphores. Data moves between devices by JAX's collectives and lax.ppermute only.
A program may use at most 256 MiB of HBM per device.

```python
import math
import jax
import jax.numpy as jnp
from jax import lax

D = 1024
HEADS = 16
HDIM = 64
ROT = 32
FF = 4096
LENGTH = 1024
ROWS = 8


def shard_levels(rng, shape, shards, smallest, largest):
    loudness, own = 1.0, jax.random.fold_in(rng, 6)
    for dim, shards_of in shards:
        heights = jnp.exp(jax.random.uniform(jax.random.fold_in(own, dim), (shards_of,), jnp.float32, smallest / len(shards), largest / len(shards)))
        loudness = loudness * jnp.repeat(heights, shape[dim] // shards_of).reshape([-1 if axis == dim else 1 for axis in range(len(shape))])
    return loudness


def bell_draw(own_key, extent, spread, limit, pieces=(), kind=jnp.bfloat16):
    values = spread * jax.random.normal(own_key, extent, jnp.float32)
    if pieces:
        values = values * shard_levels(own_key, extent, pieces, -0.22, 0.18)
    return jnp.clip(values, -limit, limit).astype(kind)


def setup_inputs(seed: int = 0) -> dict:
    streams_of = jax.random.split(jax.random.key(seed), 23)
    inputs = bell_draw(streams_of[0], (ROWS, LENGTH, D), 1.0, 6.0, ((0, 4), (1, 4)))
    norm_gain_one = jnp.clip(1.0 + 0.1 * jax.random.normal(streams_of[1], (D,), jnp.float32), 0.5, 1.5)
    norm_bias_one = bell_draw(streams_of[2], (D,), 0.3, 1.75, (), jnp.float32)
    query_one = bell_draw(streams_of[3], (D, HEADS * HDIM), (D // 4) ** -0.5, 0.375, ((1, 2),))
    key_one = bell_draw(streams_of[4], (D, HEADS * HDIM), D ** -0.5, 0.1875, ((1, 2),))
    value_one = bell_draw(streams_of[5], (D, HEADS * HDIM), D ** -0.5, 0.1875, ((1, 2),))
    output_one = bell_draw(streams_of[6], (HEADS * HDIM, D), (HEADS * HDIM // 16) ** -0.5, 0.75, ((0, 2),))
    up_one = bell_draw(streams_of[7], (D, FF), D ** -0.5, 0.1875, ((1, 2),))
    up_bias_one = bell_draw(streams_of[8], (FF,), 0.5, 3.0, ((0, 2),), jnp.float32)
    down_one = bell_draw(streams_of[9], (FF, D), FF ** -0.5, 0.09375, ((0, 2),))
    down_bias_one = bell_draw(streams_of[10], (D,), 0.6, 3.5, (), jnp.float32)
    norm_gain_two = jnp.clip(1.0 + 0.1 * jax.random.normal(streams_of[11], (D,), jnp.float32), 0.5, 1.5)
    norm_bias_two = bell_draw(streams_of[12], (D,), 0.3, 1.75, (), jnp.float32)
    query_two = bell_draw(streams_of[13], (D, HEADS * HDIM), (D // 4) ** -0.5, 0.375, ((1, 2),))
    key_two = bell_draw(streams_of[14], (D, HEADS * HDIM), D ** -0.5, 0.1875, ((1, 2),))
    value_two = bell_draw(streams_of[15], (D, HEADS * HDIM), D ** -0.5, 0.1875, ((1, 2),))
    output_two = bell_draw(streams_of[16], (HEADS * HDIM, D), (HEADS * HDIM // 16) ** -0.5, 0.75, ((0, 2),))
    up_two = bell_draw(streams_of[17], (D, FF), D ** -0.5, 0.1875, ((1, 2),))
    up_bias_two = bell_draw(streams_of[18], (FF,), 0.5, 3.0, ((0, 2),), jnp.float32)
    down_two = bell_draw(streams_of[19], (FF, D), FF ** -0.5, 0.09375, ((0, 2),))
    down_bias_two = bell_draw(streams_of[20], (D,), 0.6, 3.5, (), jnp.float32)
    cotangent = bell_draw(streams_of[21], (ROWS, LENGTH, D), 1.0, 6.0, ((0, 4), (1, 4)))
    return dict(inputs=inputs, norm_gain_one=norm_gain_one, norm_bias_one=norm_bias_one, query_one=query_one, key_one=key_one, value_one=value_one, output_one=output_one, up_one=up_one, up_bias_one=up_bias_one, down_one=down_one, down_bias_one=down_bias_one, norm_gain_two=norm_gain_two, norm_bias_two=norm_bias_two, query_two=query_two, key_two=key_two, value_two=value_two, output_two=output_two, up_two=up_two, up_bias_two=up_bias_two, down_two=down_two, down_bias_two=down_bias_two, cotangent=cotangent)


@jax.custom_vjp
def low(v):
    return lax.optimization_barrier(v.astype(jnp.bfloat16)).astype(jnp.float32)

@jax.custom_vjp
def low_back(v):
    return v

def low_keep(v):
    return (low(v), None)

def low_pass(kept, grad):
    return (grad,)

def back_keep(v):
    return (v, None)

def back_low(kept, grad):
    return (low(grad),)
low.defvjp(low_keep, low_pass)
low_back.defvjp(back_keep, back_low)
epsilon = 1e-05
negative = -1e+30
highest = lax.Precision.HIGHEST

def tables(position, length):
    positions = (position + jnp.arange(length, dtype=jnp.int32)).astype(jnp.float32)
    ladder = jnp.arange(ROT // 2, dtype=jnp.float32)
    frequency = jnp.exp(ladder * (-2.0 * math.log(10000.0) / ROT))
    angles = positions[:, None] * frequency[None, :]
    return (jnp.cos(angles), jnp.sin(angles))

def rotate(flat_rows, cos_table, sin_table):
    old_shape = flat_rows.shape
    headed = flat_rows.reshape(old_shape[:-1] + (old_shape[-1] // HDIM, HDIM))
    turned = headed[..., :ROT].reshape(headed.shape[:-1] + (ROT // 2, 2))
    even_part = turned[..., 0]
    odd_part = turned[..., 1]
    cos_wide = cos_table[:, None, :]
    sin_wide = sin_table[:, None, :]
    new_even = even_part * cos_wide - odd_part * sin_wide
    new_odd = odd_part * cos_wide + even_part * sin_wide
    joined = jnp.stack([new_even, new_odd], -1).reshape(headed.shape[:-1] + (ROT,))
    return jnp.concatenate([joined, headed[..., ROT:]], -1).reshape(old_shape)

def normalize(residual, gain, bias):
    centered = residual - lax.optimization_barrier(jnp.mean(residual, -1, keepdims=True))
    variance = lax.optimization_barrier(jnp.mean(centered * centered, -1, keepdims=True))
    return centered * lax.rsqrt(variance + epsilon) * gain + bias

def multiply(operand, weight):
    return jnp.dot(operand, weight, precision=highest)

def attend(queries, key_rows, value_rows):
    length = queries.shape[0]
    headed_q = queries.reshape(length, HEADS, HDIM)
    headed_k = key_rows.reshape(length, HEADS, HDIM)
    headed_v = value_rows.reshape(length, HEADS, HDIM)
    scores = jnp.einsum('qhd,khd->hqk', headed_q, headed_k, precision=highest) * (1.0 / math.sqrt(HDIM))
    scores = low_back(scores)
    allowed = jnp.arange(length)[:, None] >= jnp.arange(length)[None, :]
    attn_weights = low(jax.nn.softmax(jnp.where(allowed, scores, negative), axis=-1))
    context = jnp.einsum('hqk,khd->qhd', attn_weights, headed_v, precision=highest)
    return context.reshape(length, HEADS * HDIM)

def layer(residual, params, cos_table, sin_table):
    norm_gain, norm_bias, w_query, w_key, w_value, w_out, w_up, b_up, w_down, b_down = params
    normed = low(normalize(residual, norm_gain, norm_bias))
    queries = low(rotate(low_back(multiply(normed, w_query)), cos_table, sin_table))
    key_rows = low(rotate(low_back(multiply(normed, w_key)), cos_table, sin_table))
    value_rows = low(low_back(multiply(normed, w_value)))
    context = low(low_back(jax.checkpoint(attend)(queries, key_rows, value_rows)))
    preact = low_back(multiply(normed, w_up)) + b_up
    hidden = low(jax.nn.gelu(preact, approximate=True))
    attn_branch = low_back(multiply(context, w_out))
    ffn_branch = low_back(multiply(hidden, w_down))
    return residual + attn_branch + ffn_branch + b_down

def reference(inputs, norm_gain_one, norm_bias_one, query_one, key_one, value_one, output_one, up_one, up_bias_one, down_one, down_bias_one, norm_gain_two, norm_bias_two, query_two, key_two, value_two, output_two, up_two, up_bias_two, down_two, down_bias_two, cotangent):
    params = tuple((argument.astype(jnp.float32) for argument in (norm_gain_one, norm_bias_one, query_one, key_one, value_one, output_one, up_one, up_bias_one, down_one, down_bias_one, norm_gain_two, norm_bias_two, query_two, key_two, value_two, output_two, up_two, up_bias_two, down_two, down_bias_two)))
    cos_table, sin_table = tables(0, LENGTH)

    def forward(residual, weights):
        middle = layer(residual, weights[:10], cos_table, sin_table)
        return layer(middle, weights[10:], cos_table, sin_table)

    def one_row(accum_grads, row_pair):
        row_input, row_cot = row_pair
        result, pullback = jax.vjp(forward, row_input.astype(jnp.float32), params)
        grad_row, grad_params = pullback(row_cot.astype(jnp.float32))
        accum_grads = jax.tree.map(jnp.add, accum_grads, grad_params)
        return (accum_grads, (result.astype(jnp.bfloat16), grad_row.astype(jnp.bfloat16)))
    initial = jax.tree.map(jnp.zeros_like, params)
    accum, (outputs, input_grad) = lax.scan(one_row, initial, (inputs, cotangent))
    return (outputs, input_grad, accum[0], accum[1], accum[2], accum[3], accum[4], accum[5], accum[6], accum[7], accum[8], accum[9], accum[10], accum[11], accum[12], accum[13], accum[14], accum[15], accum[16], accum[17], accum[18], accum[19])
```

```python
import functools
import math

import jax
import jax.numpy as jnp
from jax import lax
from jax.experimental import pallas as pl
from jax.experimental.pallas import tpu as pltpu
from jax.sharding import PartitionSpec as P

HDIM = 64
ROT = 32


epsilon = 1e-05
negative = -1e30


def tables(position, length):
    positions = (position + jnp.arange(length, dtype=jnp.int32)).astype(jnp.float32)
    ladder = jnp.arange(ROT // 2, dtype=jnp.float32)
    frequency = jnp.exp(ladder * (-2.0 * math.log(10000.0) / ROT))
    angles = positions[:, None] * frequency[None, :]
    return (jnp.cos(angles), jnp.sin(angles))


def rotate(flat_rows, cos_table, sin_table):
    old_shape = flat_rows.shape
    headed = flat_rows.reshape(old_shape[:-1] + (old_shape[-1] // HDIM, HDIM))
    turned = headed[..., :ROT].reshape(headed.shape[:-1] + (ROT // 2, 2))
    even_part = turned[..., 0]
    odd_part = turned[..., 1]
    cos_wide = cos_table[:, None, :]
    sin_wide = sin_table[:, None, :]
    new_even = even_part * cos_wide - odd_part * sin_wide
    new_odd = odd_part * cos_wide + even_part * sin_wide
    joined = jnp.stack([new_even, new_odd], -1).reshape(headed.shape[:-1] + (ROT,))
    return jnp.concatenate([joined, headed[..., ROT:]], -1).reshape(old_shape)


def normalize(residual, gain, bias):
    centered = residual - jnp.mean(residual, -1, keepdims=True)
    inverse_std = lax.rsqrt(jnp.mean(centered * centered, -1, keepdims=True) + epsilon)
    unit_rows = centered * inverse_std
    return (unit_rows * gain + bias, unit_rows, inverse_std)


def normed_rows(residual, gain, bias):
    normed, unit_rows, inverse_std = normalize(residual, gain, bias)
    normed_low = normed.astype(jnp.bfloat16)
    return (normed_low, unit_rows, inverse_std)


def project(operand, weight):
    return jnp.dot(operand, weight, preferred_element_type=jnp.float32)


def back_project(operand, weight):
    return lax.dot_general(
        operand, weight, (((2,), (1,)), ((), ())), preferred_element_type=jnp.float32
    )


def outer(left_rows, right_rows):
    return lax.dot_general(
        left_rows, right_rows, (((0, 1), (0, 1)), ((), ())), preferred_element_type=jnp.float32
    )


def token_sum(operand):
    return jnp.sum(operand, axis=(0, 1))


def gelu_tanh(argument):
    return jax.nn.gelu(argument, approximate=True)


def headed_view(flat_rows):
    return flat_rows.reshape(flat_rows.shape[:-1] + (flat_rows.shape[-1] // HDIM, HDIM))


def allowed_mask(position, query_count, key_start, key_count):
    query_places = position + jnp.arange(query_count, dtype=jnp.int32)
    key_places = key_start + jnp.arange(key_count, dtype=jnp.int32)
    return query_places[:, None] >= key_places[None, :]


def block_scores(queries, key_rows, position, key_start):
    scaling = 1.0 / math.sqrt(HDIM)
    scores = (
        jnp.einsum(
            "bqhd,bkhd->bhqk",
            headed_view(queries),
            headed_view(key_rows),
            preferred_element_type=jnp.float32,
        )
        * scaling
    )
    allowed = allowed_mask(position, queries.shape[1], key_start, key_rows.shape[1])
    return (jnp.where(allowed, scores, negative), allowed)


def start_stats(queries):
    batch, query_count, width = queries.shape
    head_count = width // HDIM
    highest = jnp.full((batch, head_count, query_count), negative, jnp.float32)
    summed = jnp.zeros((batch, head_count, query_count), jnp.float32)
    return (highest, summed)


def start_values(queries):
    batch, query_count, width = queries.shape
    return jnp.zeros((batch, query_count, width // HDIM, HDIM), jnp.float32)


def stats_block(running, pieces, key_start, queries, position):
    highest, summed = running
    masked, allowed = block_scores(queries, pieces[0], position, key_start)
    new_high = jnp.maximum(highest, jnp.max(masked, -1))
    expo = jnp.where(allowed, jnp.exp(masked - new_high[..., None]), 0.0)
    summed = jnp.sum(expo, -1)
    return (new_high, summed)


def value_block(pieces, key_start, queries, position, log_total):
    masked, allowed = block_scores(queries, pieces[0], position, key_start)
    attn_low = jnp.where(allowed, jnp.exp(masked - log_total[..., None]), 0.0).astype(jnp.bfloat16)
    return jnp.einsum(
        "bhqk,bkhd->bqhd", attn_low, headed_view(pieces[1]), preferred_element_type=jnp.float32
    )


def fold_history(key_rows, value_rows, fold_fn, initial):
    return fold_fn(
        initial,
        (
            lax.all_gather(key_rows, "seq", axis=1, tiled=True),
            lax.all_gather(value_rows, "seq", axis=1, tiled=True),
        ),
        jnp.int32(0),
    )


def attend_fold(queries, key_rows, value_rows, position):

    def stats_piece(running, pieces, key_start):
        return stats_block(running, pieces, key_start, queries, position)

    highest, summed = fold_history(key_rows, value_rows, stats_piece, start_stats(queries))
    log_total = highest + jnp.log(summed)

    def value_piece(accumulated, pieces, key_start):
        return value_block(pieces, key_start, queries, position, log_total)

    accumulated = fold_history(key_rows, value_rows, value_piece, start_values(queries))
    return (accumulated.reshape(queries.shape), log_total)


def attend_back(queries, grad_context, log_total, row_delta, key_all, value_all, position):
    batch, block_size, width = queries.shape
    head_count = width // HDIM
    block_count = key_all.shape[1] // block_size
    scaling = 1.0 / math.sqrt(HDIM)
    headed_q = headed_view(queries)
    headed_g = headed_view(grad_context)

    def back_block(grad_query, block_index):
        offset = block_index * block_size
        key_rows = headed_view(lax.dynamic_slice_in_dim(key_all, offset, block_size, 1))
        value_rows = headed_view(lax.dynamic_slice_in_dim(value_all, offset, block_size, 1))
        scores = (
            jnp.einsum("bqhd,bkhd->bhqk", headed_q, key_rows, preferred_element_type=jnp.float32)
            * scaling
        )
        allowed = allowed_mask(position, block_size, offset, block_size)
        masked = jnp.where(allowed, scores, negative)
        attn_weights = jnp.where(allowed, jnp.exp(masked - log_total[..., None]), 0.0)
        grad_weights = jnp.einsum(
            "bqhd,bkhd->bhqk", headed_g, value_rows, preferred_element_type=jnp.float32
        )
        grad_score = (attn_weights * (grad_weights - row_delta[..., None])).astype(jnp.bfloat16)
        grad_query = (
            grad_query
            + jnp.einsum(
                "bhqk,bkhd->bqhd", grad_score, key_rows, preferred_element_type=jnp.float32
            )
            * scaling
        )
        grad_key = (
            jnp.einsum("bhqk,bqhd->bkhd", grad_score, headed_q, preferred_element_type=jnp.float32)
            * scaling
        )
        grad_value = jnp.einsum(
            "bhqk,bqhd->bkhd",
            attn_weights.astype(jnp.bfloat16),
            headed_g,
            preferred_element_type=jnp.float32,
        )
        return (
            grad_query,
            (
                grad_key.reshape(batch, block_size, width),
                grad_value.reshape(batch, block_size, width),
            ),
        )

    initial = jnp.zeros((batch, block_size, head_count, HDIM), jnp.float32)
    grad_query, key_terms = lax.scan(back_block, initial, jnp.arange(block_count, dtype=jnp.int32))
    return (grad_query.reshape(batch, block_size, width), key_terms)


def layer_forward(residual, params, cos_table, sin_table, position):
    norm_gain, norm_bias, w_query, w_key, w_value, w_out, w_up, b_up, w_down, b_down = params
    normed_low, unit_rows, inverse_std = normed_rows(residual, norm_gain, norm_bias)
    queries = rotate(project(normed_low, w_query), cos_table, sin_table).astype(jnp.bfloat16)
    key_rows = rotate(project(normed_low, w_key), cos_table, sin_table).astype(jnp.bfloat16)
    value_rows = project(normed_low, w_value).astype(jnp.bfloat16)
    context, log_total = attend_fold(queries, key_rows, value_rows, position)
    attn_branch = project(context.astype(jnp.bfloat16), w_out)
    preact = project(normed_low, w_up) + b_up
    hidden_low = gelu_tanh(preact).astype(jnp.bfloat16)
    branches = attn_branch + project(hidden_low, w_down)
    combined = lax.psum(branches, "tp")
    return (residual + combined + b_down, (context, log_total, None))


def layer_backward(residual, params, cos_table, sin_table, position, stashed, grad_out, grad_low):
    norm_gain, norm_bias, w_query, w_key, w_value, w_out, w_up, b_up, w_down, b_down = params
    context, log_total, gathered = stashed
    normed_low, unit_rows, inverse_std = normed_rows(residual, norm_gain, norm_bias)
    queries = rotate(project(normed_low, w_query), cos_table, sin_table).astype(jnp.bfloat16)
    key_rows = rotate(project(normed_low, w_key), cos_table, sin_table).astype(jnp.bfloat16)
    value_rows = project(normed_low, w_value).astype(jnp.bfloat16)
    key_all, value_all = (
        lax.all_gather(key_rows, "seq", axis=1, tiled=True),
        lax.all_gather(value_rows, "seq", axis=1, tiled=True),
    )
    grad_context = back_project(grad_low, w_out).astype(jnp.bfloat16)
    batch, block_size, width = queries.shape
    products = (grad_context.astype(jnp.float32) * context).reshape(
        batch, block_size, width // HDIM, HDIM
    )
    row_delta = jnp.transpose(jnp.sum(products, -1), (0, 2, 1))
    grad_query, key_terms = attend_back(
        queries, grad_context, log_total, row_delta, key_all, value_all, position
    )
    summed_keys, summed_values = (
        lax.psum_scatter(key_terms[0], "seq", scatter_dimension=0, tiled=True),
        lax.psum_scatter(key_terms[1], "seq", scatter_dimension=0, tiled=True),
    )
    own_keys = summed_keys[0]
    own_values = summed_values[0]
    grad_query_low = rotate(grad_query, cos_table, -sin_table).astype(jnp.bfloat16)
    grad_key_low = rotate(own_keys, cos_table, -sin_table).astype(jnp.bfloat16)
    grad_value_low = own_values.astype(jnp.bfloat16)
    preact = project(normed_low, w_up) + b_up
    hidden, gelu_pull = jax.vjp(gelu_tanh, preact)
    hidden_low = hidden.astype(jnp.bfloat16)
    grad_preact = gelu_pull(back_project(grad_low, w_down))[0]
    grad_preact_low = grad_preact.astype(jnp.bfloat16)
    partial_value = back_project(grad_query_low, w_query) + back_project(grad_key_low, w_key)
    partial_value = (
        partial_value + back_project(grad_value_low, w_value) + back_project(grad_preact_low, w_up)
    )
    grad_normed = lax.psum(partial_value, "tp")
    grad_unit = grad_normed * norm_gain
    centered_grad = grad_unit - jnp.mean(grad_unit, -1, keepdims=True)
    centered_grad = centered_grad - unit_rows * jnp.mean(grad_unit * unit_rows, -1, keepdims=True)
    grad_input = grad_out + inverse_std * centered_grad
    small = (token_sum(grad_normed * unit_rows), token_sum(grad_normed), token_sum(grad_out))
    gradients = (
        small[0],
        small[1],
        outer(normed_low, grad_query_low),
        outer(normed_low, grad_key_low),
        outer(normed_low, grad_value_low),
        outer(context.astype(jnp.bfloat16), grad_low),
        outer(normed_low, grad_preact_low),
        token_sum(grad_preact),
        outer(hidden_low, grad_low),
        small[2],
    )
    return (grad_input, gradients)


def general_body(
    inputs,
    norm_gain_one,
    norm_bias_one,
    query_one,
    key_one,
    value_one,
    output_one,
    up_one,
    up_bias_one,
    down_one,
    down_bias_one,
    norm_gain_two,
    norm_bias_two,
    query_two,
    key_two,
    value_two,
    output_two,
    up_two,
    up_bias_two,
    down_two,
    down_bias_two,
    cotangent,
):
    first_params = (
        norm_gain_one,
        norm_bias_one,
        query_one,
        key_one,
        value_one,
        output_one,
        up_one,
        up_bias_one,
        down_one,
        down_bias_one,
    )
    second_params = (
        norm_gain_two,
        norm_bias_two,
        query_two,
        key_two,
        value_two,
        output_two,
        up_two,
        up_bias_two,
        down_two,
        down_bias_two,
    )
    block_size = inputs.shape[1]
    position = lax.axis_index("seq") * block_size
    cos_table, sin_table = tables(position, block_size)
    start_rows = inputs.astype(jnp.float32)
    cot_rows = cotangent.astype(jnp.float32)
    middle, first_stash = layer_forward(start_rows, first_params, cos_table, sin_table, position)
    result, second_stash = layer_forward(middle, second_params, cos_table, sin_table, position)
    result_low = result.astype(jnp.bfloat16)
    middle_grad, second_grads = layer_backward(
        middle, second_params, cos_table, sin_table, position, second_stash, cot_rows, cotangent
    )
    middle_low = middle_grad.astype(jnp.bfloat16)
    start_grad, first_grads = layer_backward(
        start_rows,
        first_params,
        cos_table,
        sin_table,
        position,
        first_stash,
        middle_grad,
        middle_low,
    )
    start_low = start_grad.astype(jnp.bfloat16)
    everything = (
        lax.psum_scatter(first_grads[0], ("seq", "rows"), scatter_dimension=0, tiled=True),
        lax.psum_scatter(first_grads[1], ("seq", "rows"), scatter_dimension=0, tiled=True),
        lax.psum_scatter(first_grads[2], ("seq", "rows"), scatter_dimension=0, tiled=True),
        lax.psum_scatter(first_grads[3], ("seq", "rows"), scatter_dimension=0, tiled=True),
        lax.psum_scatter(first_grads[4], ("seq", "rows"), scatter_dimension=0, tiled=True),
        lax.psum_scatter(first_grads[5], ("seq", "rows"), scatter_dimension=1, tiled=True),
        lax.psum_scatter(first_grads[6], ("seq", "rows"), scatter_dimension=0, tiled=True),
        lax.psum_scatter(first_grads[7], ("seq", "rows"), scatter_dimension=0, tiled=True),
        lax.psum_scatter(first_grads[8], ("seq", "rows"), scatter_dimension=1, tiled=True),
        lax.psum_scatter(first_grads[9], ("seq", "rows"), scatter_dimension=0, tiled=True),
        lax.psum_scatter(second_grads[0], ("seq", "rows"), scatter_dimension=0, tiled=True),
        lax.psum_scatter(second_grads[1], ("seq", "rows"), scatter_dimension=0, tiled=True),
        lax.psum_scatter(second_grads[2], ("seq", "rows"), scatter_dimension=0, tiled=True),
        lax.psum_scatter(second_grads[3], ("seq", "rows"), scatter_dimension=0, tiled=True),
        lax.psum_scatter(second_grads[4], ("seq", "rows"), scatter_dimension=0, tiled=True),
        lax.psum_scatter(second_grads[5], ("seq", "rows"), scatter_dimension=1, tiled=True),
        lax.psum_scatter(second_grads[6], ("seq", "rows"), scatter_dimension=0, tiled=True),
        lax.psum_scatter(second_grads[7], ("seq", "rows"), scatter_dimension=0, tiled=True),
        lax.psum_scatter(second_grads[8], ("seq", "rows"), scatter_dimension=1, tiled=True),
        lax.psum_scatter(second_grads[9], ("seq", "rows"), scatter_dimension=0, tiled=True),
    )
    return (result_low, start_low) + tuple(everything)


BLOCKS = 4
SLOTS = 4
low_type = jnp.bfloat16
wide_type = jnp.float32
NT = (((1,), (1,)), ((), ()))
NN = (((1,), (0,)), ((), ()))
TN = (((0,), (0,)), ((), ()))


def swap_x(v):
    return lax.ppermute(v, "tp", [(0, 1), (1, 0)])


def swap_c(v):
    return lax.ppermute(v, "rows", [(0, 1), (1, 0), (2, 3), (3, 2)])


def swap_y(v):
    return lax.ppermute(v, "rows", [(0, 2), (2, 0), (1, 3), (3, 1)])


def swap_z(v, k):
    return lax.ppermute(v, "seq", [(i, i ^ k) for i in range(4)])


def low(v):
    return v.astype(low_type)


def wide(v):
    return v.astype(wide_type)


def dot(a, b, dims=NN):
    return lax.dot_general(a, b, dims, preferred_element_type=wide_type)


def pick(v, index, axis=0):
    return lax.dynamic_index_in_dim(v, index, axis, keepdims=False)


def part(v, index, count, axis):
    size = v.shape[axis] // count
    return lax.dynamic_slice_in_dim(v, index * size, size, axis)


def in_order(first, a, b, axis):
    return jnp.where(first, jnp.concatenate([a, b], axis), jnp.concatenate([b, a], axis))


def xor_order(pieces, z):
    a = jnp.stack(pieces)
    a = jnp.where((z & 1) == 1, a[jnp.array([1, 0, 3, 2])], a)
    return jnp.where((z & 2) == 2, a[jnp.array([2, 3, 0, 1])], a)


def own_tokens(local, place):
    x, c, y, z = place
    rows, tokens, width = local.shape
    sub = tokens // SLOTS
    mine = part(local.reshape(rows, SLOTS, sub, width), x, 2, 1)
    got = swap_c(pick(mine, 1 - c, 1))
    whole = in_order(c == 0, pick(mine, c, 1), got, 0)
    pieces = [pick(whole, z)] + [swap_z(pick(whole, z ^ k), k) for k in (1, 2, 3)]
    return xor_order(pieces, z).reshape(BLOCKS * sub, width)


def local_rows(own, place):
    x, c, y, z = place
    sub = own.shape[0] // BLOCKS
    width = own.shape[1]
    blocks = own.reshape(BLOCKS, sub, width)
    pieces = [pick(blocks, z)] + [swap_z(pick(blocks, z ^ k), k) for k in (1, 2, 3)]
    rows = xor_order(pieces, z)
    got = swap_c(part(rows, 1 - c, 2, 0))
    both = in_order(c == 0, part(rows, c, 2, 0)[:, None], got[:, None], 1)
    other = swap_x(both)
    full = in_order(x == 0, both[:, None], other[:, None], 1)
    return full.reshape(2, SLOTS * sub, width)


def whole_row(own):
    two = jnp.concatenate([own, swap_x(own)], 0)
    return jnp.concatenate([two, swap_c(two)], 0)


def sum_to_own(product, count):
    got = swap_c(low(product(count // 2, count)))
    kept = product(0, count // 2) + wide(got)
    half = count // 4
    return kept[:half] + wide(swap_x(low(kept[half:])))


def slot_places(owner, index, sub):
    slot = index // sub
    return (owner ^ (((slot & 1) << 1) | (slot >> 1))) * sub + (index - slot * sub)


def row_positions(owner, sub):
    index = jnp.arange(SLOTS * BLOCKS * sub, dtype=jnp.int32)
    slot = index // (BLOCKS * sub)
    block = (index // sub) % BLOCKS
    own_place = (owner ^ (((slot & 1) << 1) | (slot >> 1))) * sub
    return block * SLOTS * sub + own_place + index % sub


def lane_tables(positions):
    lane = jnp.arange(128, dtype=jnp.int32) % HDIM
    frequency = jnp.exp((lane // 2).astype(wide_type) * (-2.0 * math.log(10000.0) / ROT))
    angles = positions.astype(wide_type)[:, None] * frequency[None, :]
    turned = (lane < ROT)[None, :]
    even = (lane % 2 == 0)[None, :]
    sines = jnp.sin(angles)
    return (
        jnp.where(turned, jnp.cos(angles), 1.0),
        jnp.where(turned & even, -sines, 0.0),
        jnp.where(turned & ~even, sines, 0.0),
    )


def turn_lanes(v, cosines, to_even, to_odd):
    return v * cosines + pltpu.roll(v, 127, 1) * to_even + pltpu.roll(v, 1, 1) * to_odd


def take_block(ref, block, sub):
    starts = [(slot * BLOCKS + block) * sub for slot in range(SLOTS)]
    return jnp.concatenate([ref[at : at + sub, :] for at in starts], 0)


def put_block(ref, block, sub, value):
    for slot in range(SLOTS):
        at = (slot * BLOCKS + block) * sub
        ref[at : at + sub, :] = value[slot * sub : (slot + 1) * sub]


def block_allowed(owner, size, sub):
    key_place = slot_places(owner, lax.broadcasted_iota(jnp.int32, (size, size), 0), sub)
    query_place = slot_places(owner, lax.broadcasted_iota(jnp.int32, (size, size), 1), sub)
    return query_place >= key_place


def add(a, b):
    return b if a is None else a + b


def attend_kernel(sub, owner, q_ref, k_ref, v_ref, cos_ref, even_ref, odd_ref, q_out, k_out, v_out, c_out, log_out):
    scaling = 1.0 / math.sqrt(HDIM)
    size = SLOTS * sub
    allowed = block_allowed(owner[0], size, sub)
    lane = lax.broadcasted_iota(jnp.int32, (1, 128), 1)
    queries, keys, values = [], [], []
    for block in range(BLOCKS):
        turns = [take_block(ref, block, sub) for ref in (cos_ref, even_ref, odd_ref)]
        queries.append(low(turn_lanes(take_block(q_ref, block, sub), *turns)))
        keys.append(low(turn_lanes(take_block(k_ref, block, sub), *turns)))
        value_rows = low(take_block(v_ref, block, sub))
        values.append(value_rows.T)
        put_block(q_out, block, sub, queries[block])
        put_block(k_out, block, sub, keys[block])
        put_block(v_out, block, sub, value_rows)
    for j in range(BLOCKS):
        contexts = []
        for head in range(128 // HDIM):
            of_head = lane // HDIM == head
            query = jnp.where(of_head, queries[j], jnp.zeros_like(queries[j]))
            scores = [dot(keys[i], query, NT) for i in range(j + 1)]
            scores[j] = jnp.where(allowed, scores[j], negative)
            tops = [jnp.max(s, 0, keepdims=True) for s in scores]
            top = functools.reduce(jnp.maximum, tops)
            weights = [jnp.exp((s - top) * scaling) for s in scores]
            total = functools.reduce(jnp.add, [jnp.sum(w, 0, keepdims=True) for w in weights])
            context = None
            for i in range(j + 1):
                rows = values[i][head * HDIM : (head + 1) * HDIM]
                context = add(context, dot(rows, low(weights[i])))
            contexts.append(context * (1.0 / total))
            log_out[0, head : head + 1, j * size : (j + 1) * size] = top * scaling + jnp.log(total)
        put_block(c_out, j, sub, low(jnp.concatenate(contexts, 0).T))


def attend(joined, turns, owner):
    rows = joined.shape[0]
    groups = joined.shape[1] // (3 * 128)
    width = groups * 128
    column = lambda shift: pl.BlockSpec((rows, 128), lambda g: (0, shift * groups + g))
    same = pl.BlockSpec((rows, 128), lambda g: (0, 0))
    logs = pl.BlockSpec((1, 2, rows), lambda g: (g, 0, 0))
    return pl.pallas_call(
        functools.partial(attend_kernel, rows // (BLOCKS * SLOTS)),
        grid=(groups,),
        in_specs=[pl.BlockSpec(memory_space=pltpu.SMEM), column(0), column(1), column(2)] + [same] * 3,
        out_specs=[column(0)] * 4 + [logs],
        out_shape=[jax.ShapeDtypeStruct((rows, width), low_type)] * 4
        + [jax.ShapeDtypeStruct((groups, 2, rows), wide_type)],
        compiler_params=pltpu.CompilerParams(vmem_limit_bytes=48 * 2**20),
        cost_estimate=pl.CostEstimate(
            flops=8 * groups * rows * rows * 128, bytes_accessed=rows * width * 24, transcendentals=groups * rows * rows
        ),
        name="attend",
    )(owner, joined, joined, joined, *turns)


def attend_back_kernel(
    sub, owner, q_ref, k_ref, v_ref, g_ref, log_ref, cos_ref, even_ref, odd_ref, dq_out, dk_out, dv_out
):
    scaling = 1.0 / math.sqrt(HDIM)
    size = SLOTS * sub
    allowed = block_allowed(owner[0], size, sub)
    lane = lax.broadcasted_iota(jnp.int32, (1, 128), 1)
    queries, keys, values, grads = [
        [take_block(ref, block, sub) for block in range(BLOCKS)] for ref in (q_ref, k_ref, v_ref, g_ref)
    ]
    turns = []
    for block in range(BLOCKS):
        cosines, to_even, to_odd = [take_block(ref, block, sub) for ref in (cos_ref, even_ref, odd_ref)]
        turns.append((cosines, -to_even, -to_odd))
    flat_keys = [k.T for k in keys]
    grad_keys = [None] * BLOCKS
    grad_values = [None] * BLOCKS
    for j in range(BLOCKS):
        grad_query = []
        for head in range(128 // HDIM):
            of_head = lane // HDIM == head
            query = jnp.where(of_head, queries[j], jnp.zeros_like(queries[j]))
            grad = jnp.where(of_head, grads[j], jnp.zeros_like(grads[j]))
            log_total = log_ref[0, head : head + 1, j * size : (j + 1) * size]
            probs, grad_probs, delta = [], [], None
            for i in range(j + 1):
                weights = jnp.exp(dot(keys[i], query, NT) * scaling - log_total)
                if i == j:
                    weights = jnp.where(allowed, weights, 0.0)
                back = dot(values[i], grad, NT)
                delta = add(delta, jnp.sum(weights * back, 0, keepdims=True))
                probs.append(weights)
                grad_probs.append(back)
            flat = None
            for i in range(j + 1):
                grad_scores = low(probs[i] * (grad_probs[i] - delta))
                grad_values[i] = add(grad_values[i], dot(low(probs[i]), grad))
                grad_keys[i] = add(grad_keys[i], dot(grad_scores, query))
                flat = add(flat, dot(flat_keys[i][head * HDIM : (head + 1) * HDIM], grad_scores))
            grad_query.append(flat)
        turned = jnp.concatenate(grad_query, 0).T * scaling
        put_block(dq_out, j, sub, low(turn_lanes(turned, *turns[j])))
    for i in range(BLOCKS):
        put_block(dk_out, i, sub, low(turn_lanes(grad_keys[i] * scaling, *turns[i])))
        put_block(dv_out, i, sub, low(grad_values[i]))


def attend_back_call(queries, keys, values, grad_context, logs, turns, owner):
    rows, width = queries.shape
    groups = width // 128
    column = pl.BlockSpec((rows, 128), lambda g: (0, g))
    same = pl.BlockSpec((rows, 128), lambda g: (0, 0))
    log_spec = pl.BlockSpec((1, 2, rows), lambda g: (g, 0, 0))
    return pl.pallas_call(
        functools.partial(attend_back_kernel, rows // (BLOCKS * SLOTS)),
        grid=(groups,),
        in_specs=[pl.BlockSpec(memory_space=pltpu.SMEM)] + [column] * 4 + [log_spec] + [same] * 3,
        out_specs=[column] * 3,
        out_shape=[jax.ShapeDtypeStruct((rows, width), low_type)] * 3,
        compiler_params=pltpu.CompilerParams(vmem_limit_bytes=48 * 2**20),
        cost_estimate=pl.CostEstimate(
            flops=20 * groups * rows * rows * 128, bytes_accessed=rows * width * 24, transcendentals=groups * rows * rows
        ),
        name="attend_back",
    )(owner, queries, keys, values, grad_context, logs, *turns)


def gelu_and_slope(u):
    root = math.sqrt(2.0 / math.pi)
    square = u * u
    bend = jnp.tanh(root * u * (1.0 + 0.044715 * square))
    half = 0.5 * (1.0 + bend)
    slope = half + 0.5 * u * (1.0 - bend * bend) * (root * (1.0 + 3.0 * 0.044715 * square))
    return (u * half, slope)


def split_rows(v, place):
    x, c, y, z = place
    cut = v.reshape(v.shape[0], 4, 2, v.shape[1] // 8)
    flat = lambda index: pick(cut, index, 2).reshape(v.shape[0], v.shape[1] // 2)
    return (flat(y), flat(1 - y))


def reduce_rows(halves, right, place):
    x, c, y, z = place
    kept, sent = halves
    width = right.shape[1]
    got = swap_y(low(dot(sent, right, TN)))
    total = dot(kept, right, TN) + wide(got)
    total = total.reshape(2, 2, -1, width)
    total = pick(total, z & 1, 1) + wide(swap_z(low(pick(total, 1 - (z & 1), 1)), 1))
    total = pick(total, z >> 1) + wide(swap_z(low(pick(total, 1 - (z >> 1))), 2))
    total = total.reshape(2, -1, width)
    own = pick(total, c)
    other = wide(swap_c(low(pick(total, 1 - c))))
    return (jnp.where(c == 0, own, other), jnp.where(c == 0, other, own))


def reduce_small(shared, hidden_sums, place):
    x, c, y, z = place
    zeros = jnp.zeros_like(hidden_sums)
    both = in_order(c == 0, hidden_sums, zeros, 0)
    shared = shared + swap_x(shared)
    total = jnp.concatenate([shared, both], 0)
    total = total + swap_c(total)
    total = total + swap_y(total)
    total = total + swap_z(total, 1)
    total = total + swap_z(total, 2)
    index = z * 4 + y * 2 + c
    count = shared.shape[0] // 3
    cut = [part(total[i * count : (i + 1) * count], index, 16, 0) for i in range(3)]
    return cut + [part(total[3 * count :], index, 16, 0)]


def quad_forward(own, params, turns, owner, want_result):
    gain, bias, w_join, w_out, w_up, b_up, w_down, b_down = params
    normed, unit_rows, inverse_std = normalize(own, gain, bias)
    full = whole_row(low(normed))
    queries, keys, values, context, logs = attend(dot(full, w_join), turns, owner)
    hidden, slope = gelu_and_slope(dot(full, w_up) + b_up)
    hidden = low(hidden)
    stash = (full, unit_rows, inverse_std, queries, keys, values, context, logs, hidden, low(slope))

    def product(start, stop):
        return dot(context[start:stop], w_out) + dot(hidden[start:stop], w_down)

    result = own + sum_to_own(product, full.shape[0]) + b_down
    return (result, stash)


def quad_backward(grad_own, grad_full, params, stash, turns, owner, place):
    gain, bias, w_join, w_out, w_up, b_up, w_down, b_down = params
    full, unit_rows, inverse_std, queries, keys, values, context, logs, hidden, slope = stash
    grad_context = low(dot(grad_full, w_out, NT))
    grad_preact = dot(grad_full, w_down, NT) * wide(slope)
    grad_hidden = low(grad_preact)
    grads = attend_back_call(queries, keys, values, grad_context, logs, turns, owner)
    joined = jnp.concatenate(grads, 1)

    def product(start, stop):
        return dot(joined[start:stop], w_join, NT) + dot(grad_hidden[start:stop], w_up, NT)

    grad_normed = sum_to_own(product, full.shape[0])
    grad_unit = grad_normed * gain
    centered = grad_unit - jnp.mean(grad_unit, -1, keepdims=True)
    centered = centered - unit_rows * jnp.mean(grad_unit * unit_rows, -1, keepdims=True)
    grad_input = grad_own + inverse_std * centered
    shared = jnp.concatenate(
        [jnp.sum(grad_normed * unit_rows, 0), jnp.sum(grad_normed, 0), jnp.sum(grad_own, 0)], 0
    )
    small = reduce_small(shared, jnp.sum(grad_preact, 0), place)
    left = split_rows(grad_full, place)
    right = split_rows(full, place)
    down = reduce_rows(left, jnp.concatenate([context, hidden], 1), place)
    up = reduce_rows(right, grad_hidden, place)
    heads = reduce_rows(right, joined, place)
    wide_head = context.shape[1]
    side = lambda pair, start, stop: jnp.concatenate([p[:, start:stop] for p in pair], 1)
    gradients = (
        small[0],
        small[1],
        side(heads, 0, wide_head),
        side(heads, wide_head, 2 * wide_head),
        side(heads, 2 * wide_head, 3 * wide_head),
        side(down, 0, wide_head).T,
        side(up, 0, None),
        small[3],
        side(down, wide_head, None).T,
        small[2],
    )
    return (grad_input, gradients)


def quad_body(inputs, *rest):
    cotangent = rest[-1]
    r = lax.axis_index("rows")
    place = (lax.axis_index("tp"), r % 2, r // 2, lax.axis_index("seq"))
    x, c, y, z = place
    owner = 2 * x + c
    sub = inputs.shape[1] // SLOTS
    turns = lane_tables(row_positions(owner, sub))
    owner_ref = jnp.reshape(owner, (1,)).astype(jnp.int32)
    layers = []
    for raw in (rest[:10], rest[10:20]):
        gain, bias, w_query, w_key, w_value, w_out, w_up, b_up, w_down, b_down = raw
        w_join = jnp.concatenate([part(w, c, 2, 1) for w in (w_query, w_key, w_value)], 1)
        layers.append(
            (gain, bias, w_join, part(w_out, c, 2, 0), part(w_up, c, 2, 1), part(b_up, c, 2, 0), part(w_down, c, 2, 0), b_down)
        )
    start = wide(own_tokens(inputs, place))
    cot_own = own_tokens(cotangent, place)
    middle, first_stash = quad_forward(start, layers[0], turns, owner_ref, True)
    cot_full = whole_row(cot_own)
    result, second_stash = quad_forward(middle, layers[1], turns, owner_ref, True)
    outputs = local_rows(low(result), place)
    middle_grad, second = quad_backward(wide(cot_own), cot_full, layers[1], second_stash, turns, owner_ref, place)
    middle_full = whole_row(low(middle_grad))
    start_grad, first = quad_backward(middle_grad, middle_full, layers[0], first_stash, turns, owner_ref, place)
    input_grad = local_rows(low(start_grad), place)
    return (outputs, input_grad) + first + second


def solution(mesh):
    in_specs = (
        P("rows", "seq", None),
        P(),
        P(),
        P(None, "tp"),
        P(None, "tp"),
        P(None, "tp"),
        P("tp", None),
        P(None, "tp"),
        P("tp"),
        P("tp", None),
        P(),
        P(),
        P(),
        P(None, "tp"),
        P(None, "tp"),
        P(None, "tp"),
        P("tp", None),
        P(None, "tp"),
        P("tp"),
        P("tp", None),
        P(),
        P("rows", "seq", None),
    )
    out_specs = (
        P("rows", "seq", None),
        P("rows", "seq", None),
        P(("seq", "rows")),
        P(("seq", "rows")),
        P(("seq", "rows"), "tp"),
        P(("seq", "rows"), "tp"),
        P(("seq", "rows"), "tp"),
        P("tp", ("seq", "rows")),
        P(("seq", "rows"), "tp"),
        P(("tp", "seq", "rows")),
        P("tp", ("seq", "rows")),
        P(("seq", "rows")),
        P(("seq", "rows")),
        P(("seq", "rows")),
        P(("seq", "rows"), "tp"),
        P(("seq", "rows"), "tp"),
        P(("seq", "rows"), "tp"),
        P("tp", ("seq", "rows")),
        P(("seq", "rows"), "tp"),
        P(("tp", "seq", "rows")),
        P("tp", ("seq", "rows")),
        P(("seq", "rows")),
    )
    fits = (mesh.shape["seq"], mesh.shape["tp"], mesh.shape["rows"]) == (4, 2, 4)
    body = quad_body if fits else general_body
    return jax.shard_map(body, mesh=mesh, in_specs=in_specs, out_specs=out_specs, check_vma=False)
```

```python
import functools
import math

import jax
import jax.numpy as jnp
from jax import lax
from jax.experimental import pallas as pl
from jax.experimental.pallas import tpu as pltpu
from jax.sharding import PartitionSpec as P

HDIM = 64
ROT = 32


epsilon = 1e-05
negative = -1e30


def tables(position, length):
    positions = (position + jnp.arange(length, dtype=jnp.int32)).astype(jnp.float32)
    ladder = jnp.arange(ROT // 2, dtype=jnp.float32)
    frequency = jnp.exp(ladder * (-2.0 * math.log(10000.0) / ROT))
    angles = positions[:, None] * frequency[None, :]
    return (jnp.cos(angles), jnp.sin(angles))


def rotate(flat_rows, cos_table, sin_table):
    old_shape = flat_rows.shape
    headed = flat_rows.reshape(old_shape[:-1] + (old_shape[-1] // HDIM, HDIM))
    turned = headed[..., :ROT].reshape(headed.shape[:-1] + (ROT // 2, 2))
    even_part = turned[..., 0]
    odd_part = turned[..., 1]
    cos_wide = cos_table[:, None, :]
    sin_wide = sin_table[:, None, :]
    new_even = even_part * cos_wide - odd_part * sin_wide
    new_odd = odd_part * cos_wide + even_part * sin_wide
    joined = jnp.stack([new_even, new_odd], -1).reshape(headed.shape[:-1] + (ROT,))
    return jnp.concatenate([joined, headed[..., ROT:]], -1).reshape(old_shape)


def normalize(residual, gain, bias):
    centered = residual - jnp.mean(residual, -1, keepdims=True)
    inverse_std = lax.rsqrt(jnp.mean(centered * centered, -1, keepdims=True) + epsilon)
    unit_rows = centered * inverse_std
    return (unit_rows * gain + bias, unit_rows, inverse_std)


def normed_rows(residual, gain, bias):
    normed, unit_rows, inverse_std = normalize(residual, gain, bias)
    normed_low = normed.astype(jnp.bfloat16)
    return (normed_low, unit_rows, inverse_std)


def project(operand, weight):
    return jnp.dot(operand, weight, preferred_element_type=jnp.float32)


def back_project(operand, weight):
    return lax.dot_general(
        operand, weight, (((2,), (1,)), ((), ())), preferred_element_type=jnp.float32
    )


def outer(left_rows, right_rows):
    return lax.dot_general(
        left_rows, right_rows, (((0, 1), (0, 1)), ((), ())), preferred_element_type=jnp.float32
    )


def token_sum(operand):
    return jnp.sum(operand, axis=(0, 1))


def gelu_tanh(argument):
    return jax.nn.gelu(argument, approximate=True)


def headed_view(flat_rows):
    return flat_rows.reshape(flat_rows.shape[:-1] + (flat_rows.shape[-1] // HDIM, HDIM))


def allowed_mask(position, query_count, key_start, key_count):
    query_places = position + jnp.arange(query_count, dtype=jnp.int32)
    key_places = key_start + jnp.arange(key_count, dtype=jnp.int32)
    return query_places[:, None] >= key_places[None, :]


def block_scores(queries, key_rows, position, key_start):
    scaling = 1.0 / math.sqrt(HDIM)
    scores = (
        jnp.einsum(
            "bqhd,bkhd->bhqk",
            headed_view(queries),
            headed_view(key_rows),
            preferred_element_type=jnp.float32,
        )
        * scaling
    )
    allowed = allowed_mask(position, queries.shape[1], key_start, key_rows.shape[1])
    return (jnp.where(allowed, scores, negative), allowed)


def start_stats(queries):
    batch, query_count, width = queries.shape
    head_count = width // HDIM
    highest = jnp.full((batch, head_count, query_count), negative, jnp.float32)
    summed = jnp.zeros((batch, head_count, query_count), jnp.float32)
    return (highest, summed)


def start_values(queries):
    batch, query_count, width = queries.shape
    return jnp.zeros((batch, query_count, width // HDIM, HDIM), jnp.float32)


def stats_block(running, pieces, key_start, queries, position):
    highest, summed = running
    masked, allowed = block_scores(queries, pieces[0], position, key_start)
    new_high = jnp.maximum(highest, jnp.max(masked, -1))
    expo = jnp.where(allowed, jnp.exp(masked - new_high[..., None]), 0.0)
    summed = jnp.sum(expo, -1)
    return (new_high, summed)


def value_block(pieces, key_start, queries, position, log_total):
    masked, allowed = block_scores(queries, pieces[0], position, key_start)
    attn_low = jnp.where(allowed, jnp.exp(masked - log_total[..., None]), 0.0).astype(jnp.bfloat16)
    return jnp.einsum(
        "bhqk,bkhd->bqhd", attn_low, headed_view(pieces[1]), preferred_element_type=jnp.float32
    )


def fold_history(key_rows, value_rows, fold_fn, initial):
    return fold_fn(
        initial,
        (
            lax.all_gather(key_rows, "seq", axis=1, tiled=True),
            lax.all_gather(value_rows, "seq", axis=1, tiled=True),
        ),
        jnp.int32(0),
    )


def attend_fold(queries, key_rows, value_rows, position):

    def stats_piece(running, pieces, key_start):
        return stats_block(running, pieces, key_start, queries, position)

    highest, summed = fold_history(key_rows, value_rows, stats_piece, start_stats(queries))
    log_total = highest + jnp.log(summed)

    def value_piece(accumulated, pieces, key_start):
        return value_block(pieces, key_start, queries, position, log_total)

    accumulated = fold_history(key_rows, value_rows, value_piece, start_values(queries))
    return (accumulated.reshape(queries.shape), log_total)


def attend_back(queries, grad_context, log_total, row_delta, key_all, value_all, position):
    batch, block_size, width = queries.shape
    head_count = width // HDIM
    block_count = key_all.shape[1] // block_size
    scaling = 1.0 / math.sqrt(HDIM)
    headed_q = headed_view(queries)
    headed_g = headed_view(grad_context)

    def back_block(grad_query, block_index):
        offset = block_index * block_size
        key_rows = headed_view(lax.dynamic_slice_in_dim(key_all, offset, block_size, 1))
        value_rows = headed_view(lax.dynamic_slice_in_dim(value_all, offset, block_size, 1))
        scores = (
            jnp.einsum("bqhd,bkhd->bhqk", headed_q, key_rows, preferred_element_type=jnp.float32)
            * scaling
        )
        allowed = allowed_mask(position, block_size, offset, block_size)
        masked = jnp.where(allowed, scores, negative)
        attn_weights = jnp.where(allowed, jnp.exp(masked - log_total[..., None]), 0.0)
        grad_weights = jnp.einsum(
            "bqhd,bkhd->bhqk", headed_g, value_rows, preferred_element_type=jnp.float32
        )
        grad_score = (attn_weights * (grad_weights - row_delta[..., None])).astype(jnp.bfloat16)
        grad_query = (
            grad_query
            + jnp.einsum(
                "bhqk,bkhd->bqhd", grad_score, key_rows, preferred_element_type=jnp.float32
            )
            * scaling
        )
        grad_key = (
            jnp.einsum("bhqk,bqhd->bkhd", grad_score, headed_q, preferred_element_type=jnp.float32)
            * scaling
        )
        grad_value = jnp.einsum(
            "bhqk,bqhd->bkhd",
            attn_weights.astype(jnp.bfloat16),
            headed_g,
            preferred_element_type=jnp.float32,
        )
        return (
            grad_query,
            (
                grad_key.reshape(batch, block_size, width),
                grad_value.reshape(batch, block_size, width),
            ),
        )

    initial = jnp.zeros((batch, block_size, head_count, HDIM), jnp.float32)
    grad_query, key_terms = lax.scan(back_block, initial, jnp.arange(block_count, dtype=jnp.int32))
    return (grad_query.reshape(batch, block_size, width), key_terms)


def layer_forward(residual, params, cos_table, sin_table, position):
    norm_gain, norm_bias, w_query, w_key, w_value, w_out, w_up, b_up, w_down, b_down = params
    normed_low, unit_rows, inverse_std = normed_rows(residual, norm_gain, norm_bias)
    queries = rotate(project(normed_low, w_query), cos_table, sin_table).astype(jnp.bfloat16)
    key_rows = rotate(project(normed_low, w_key), cos_table, sin_table).astype(jnp.bfloat16)
    value_rows = project(normed_low, w_value).astype(jnp.bfloat16)
    context, log_total = attend_fold(queries, key_rows, value_rows, position)
    attn_branch = project(context.astype(jnp.bfloat16), w_out)
    preact = project(normed_low, w_up) + b_up
    hidden_low = gelu_tanh(preact).astype(jnp.bfloat16)
    branches = attn_branch + project(hidden_low, w_down)
    combined = lax.psum(branches, "tp")
    return (residual + combined + b_down, (context, log_total, None))


def layer_backward(residual, params, cos_table, sin_table, position, stashed, grad_out, grad_low):
    norm_gain, norm_bias, w_query, w_key, w_value, w_out, w_up, b_up, w_down, b_down = params
    context, log_total, gathered = stashed
    normed_low, unit_rows, inverse_std = normed_rows(residual, norm_gain, norm_bias)
    queries = rotate(project(normed_low, w_query), cos_table, sin_table).astype(jnp.bfloat16)
    key_rows = rotate(project(normed_low, w_key), cos_table, sin_table).astype(jnp.bfloat16)
    value_rows = project(normed_low, w_value).astype(jnp.bfloat16)
    key_all, value_all = (
        lax.all_gather(key_rows, "seq", axis=1, tiled=True),
        lax.all_gather(value_rows, "seq", axis=1, tiled=True),
    )
    grad_context = back_project(grad_low, w_out).astype(jnp.bfloat16)
    batch, block_size, width = queries.shape
    products = (grad_context.astype(jnp.float32) * context).reshape(
        batch, block_size, width // HDIM, HDIM
    )
    row_delta = jnp.transpose(jnp.sum(products, -1), (0, 2, 1))
    grad_query, key_terms = attend_back(
        queries, grad_context, log_total, row_delta, key_all, value_all, position
    )
    summed_keys, summed_values = (
        lax.psum_scatter(key_terms[0], "seq", scatter_dimension=0, tiled=True),
        lax.psum_scatter(key_terms[1], "seq", scatter_dimension=0, tiled=True),
    )
    own_keys = summed_keys[0]
    own_values = summed_values[0]
    grad_query_low = rotate(grad_query, cos_table, -sin_table).astype(jnp.bfloat16)
    grad_key_low = rotate(own_keys, cos_table, -sin_table).astype(jnp.bfloat16)
    grad_value_low = own_values.astype(jnp.bfloat16)
    preact = project(normed_low, w_up) + b_up
    hidden, gelu_pull = jax.vjp(gelu_tanh, preact)
    hidden_low = hidden.astype(jnp.bfloat16)
    grad_preact = gelu_pull(back_project(grad_low, w_down))[0]
    grad_preact_low = grad_preact.astype(jnp.bfloat16)
    partial_value = back_project(grad_query_low, w_query) + back_project(grad_key_low, w_key)
    partial_value = (
        partial_value + back_project(grad_value_low, w_value) + back_project(grad_preact_low, w_up)
    )
    grad_normed = lax.psum(partial_value, "tp")
    grad_unit = grad_normed * norm_gain
    centered_grad = grad_unit - jnp.mean(grad_unit, -1, keepdims=True)
    centered_grad = centered_grad - unit_rows * jnp.mean(grad_unit * unit_rows, -1, keepdims=True)
    grad_input = grad_out + inverse_std * centered_grad
    small = (token_sum(grad_normed * unit_rows), token_sum(grad_normed), token_sum(grad_out))
    gradients = (
        small[0],
        small[1],
        outer(normed_low, grad_query_low),
        outer(normed_low, grad_key_low),
        outer(normed_low, grad_value_low),
        outer(context.astype(jnp.bfloat16), grad_low),
        outer(normed_low, grad_preact_low),
        token_sum(grad_preact),
        outer(hidden_low, grad_low),
        small[2],
    )
    return (grad_input, gradients)


def general_body(
    inputs,
    norm_gain_one,
    norm_bias_one,
    query_one,
    key_one,
    value_one,
    output_one,
    up_one,
    up_bias_one,
    down_one,
    down_bias_one,
    norm_gain_two,
    norm_bias_two,
    query_two,
    key_two,
    value_two,
    output_two,
    up_two,
    up_bias_two,
    down_two,
    down_bias_two,
    cotangent,
):
    first_params = (
        norm_gain_one,
        norm_bias_one,
        query_one,
        key_one,
        value_one,
        output_one,
        up_one,
        up_bias_one,
        down_one,
        down_bias_one,
    )
    second_params = (
        norm_gain_two,
        norm_bias_two,
        query_two,
        key_two,
        value_two,
        output_two,
        up_two,
        up_bias_two,
        down_two,
        down_bias_two,
    )
    block_size = inputs.shape[1]
    position = lax.axis_index("seq") * block_size
    cos_table, sin_table = tables(position, block_size)
    start_rows = inputs.astype(jnp.float32)
    cot_rows = cotangent.astype(jnp.float32)
    middle, first_stash = layer_forward(start_rows, first_params, cos_table, sin_table, position)
    result, second_stash = layer_forward(middle, second_params, cos_table, sin_table, position)
    result_low = result.astype(jnp.bfloat16)
    middle_grad, second_grads = layer_backward(
        middle, second_params, cos_table, sin_table, position, second_stash, cot_rows, cotangent
    )
    middle_low = middle_grad.astype(jnp.bfloat16)
    start_grad, first_grads = layer_backward(
        start_rows,
        first_params,
        cos_table,
        sin_table,
        position,
        first_stash,
        middle_grad,
        middle_low,
    )
    start_low = start_grad.astype(jnp.bfloat16)
    everything = (
        lax.psum_scatter(first_grads[0], ("seq", "rows"), scatter_dimension=0, tiled=True),
        lax.psum_scatter(first_grads[1], ("seq", "rows"), scatter_dimension=0, tiled=True),
        lax.psum_scatter(first_grads[2], ("seq", "rows"), scatter_dimension=0, tiled=True),
        lax.psum_scatter(first_grads[3], ("seq", "rows"), scatter_dimension=0, tiled=True),
        lax.psum_scatter(first_grads[4], ("seq", "rows"), scatter_dimension=0, tiled=True),
        lax.psum_scatter(first_grads[5], ("seq", "rows"), scatter_dimension=1, tiled=True),
        lax.psum_scatter(first_grads[6], ("seq", "rows"), scatter_dimension=0, tiled=True),
        lax.psum_scatter(first_grads[7], ("seq", "rows"), scatter_dimension=0, tiled=True),
        lax.psum_scatter(first_grads[8], ("seq", "rows"), scatter_dimension=1, tiled=True),
        lax.psum_scatter(first_grads[9], ("seq", "rows"), scatter_dimension=0, tiled=True),
        lax.psum_scatter(second_grads[0], ("seq", "rows"), scatter_dimension=0, tiled=True),
        lax.psum_scatter(second_grads[1], ("seq", "rows"), scatter_dimension=0, tiled=True),
        lax.psum_scatter(second_grads[2], ("seq", "rows"), scatter_dimension=0, tiled=True),
        lax.psum_scatter(second_grads[3], ("seq", "rows"), scatter_dimension=0, tiled=True),
        lax.psum_scatter(second_grads[4], ("seq", "rows"), scatter_dimension=0, tiled=True),
        lax.psum_scatter(second_grads[5], ("seq", "rows"), scatter_dimension=1, tiled=True),
        lax.psum_scatter(second_grads[6], ("seq", "rows"), scatter_dimension=0, tiled=True),
        lax.psum_scatter(second_grads[7], ("seq", "rows"), scatter_dimension=0, tiled=True),
        lax.psum_scatter(second_grads[8], ("seq", "rows"), scatter_dimension=1, tiled=True),
        lax.psum_scatter(second_grads[9], ("seq", "rows"), scatter_dimension=0, tiled=True),
    )
    return (result_low, start_low) + tuple(everything)


BLOCKS = 4
SLOTS = 4
low_type = jnp.bfloat16
wide_type = jnp.float32
NT = (((1,), (1,)), ((), ()))
NN = (((1,), (0,)), ((), ()))
TN = (((0,), (0,)), ((), ()))
SCALARS = pl.BlockSpec(memory_space=pltpu.SMEM)
HERE = pl.BlockSpec(memory_space=pltpu.VMEM)
ANYWHERE = pl.BlockSpec(memory_space=pl.ANY)


def swap_x(v):
    return lax.ppermute(v, "tp", [(0, 1), (1, 0)])


def swap_c(v):
    return lax.ppermute(v, "rows", [(0, 1), (1, 0), (2, 3), (3, 2)])


def swap_y(v):
    return lax.ppermute(v, "rows", [(0, 2), (2, 0), (1, 3), (3, 1)])


def swap_z(v, k):
    return lax.ppermute(v, "seq", [(i, i ^ k) for i in range(4)])


def low(v):
    return v.astype(low_type)


def wide(v):
    return v.astype(wide_type)


def shape(kind, *dims):
    return jax.ShapeDtypeStruct(dims, kind)


def dot(a, b, dims=NN):
    return lax.dot_general(a, b, dims, preferred_element_type=wide_type)


def add(a, b):
    return b if a is None else a + b


def pick(v, index, axis=0):
    return lax.dynamic_index_in_dim(v, index, axis, keepdims=False)


def part(v, index, count, axis):
    size = v.shape[axis] // count
    return lax.dynamic_slice_in_dim(v, index * size, size, axis)


def in_order(first, a, b, axis):
    return jnp.where(first, jnp.concatenate([a, b], axis), jnp.concatenate([b, a], axis))


def xor_order(pieces, z):
    odd = (z & 1) == 1
    high = (z & 2) == 2
    a, b, c, d = pieces
    a, b, c, d = jnp.where(odd, b, a), jnp.where(odd, a, b), jnp.where(odd, d, c), jnp.where(odd, c, d)
    a, b, c, d = jnp.where(high, c, a), jnp.where(high, d, b), jnp.where(high, a, c), jnp.where(high, b, d)
    return jnp.stack([a, b, c, d])


class Chain:
    def __init__(self, scalars):
        self.scalars = scalars
        self.token = None

    def __call__(self, name, kernel, args, outs, us=1, spec=HERE, limit=8):
        before = () if self.token is None else (self.token,)
        count = len(args)

        def with_token(*refs):
            outs_at = 1 + count + len(before)
            refs[outs_at][...] = jnp.zeros((8, 128), wide_type)
            kernel(*refs[: 1 + count], *refs[outs_at + 1 :])

        made = pl.pallas_call(
            with_token,
            in_specs=[SCALARS] + [spec] * count + [HERE] * len(before),
            out_specs=[HERE] * (1 + len(outs)),
            out_shape=[shape(wide_type, 8, 128), *outs],
            compiler_params=pltpu.CompilerParams(vmem_limit_bytes=limit * 2**20),
            cost_estimate=pl.CostEstimate(flops=int(us * 1.1e9), bytes_accessed=100000, transcendentals=0),
            name=name,
        )(self.scalars, *args, *before)
        self.token = made[0]
        return made[1:]


def core_rows(local, place):
    x, c, y, z = place
    rows, tokens, width = local.shape
    mine = part(local.reshape(rows, SLOTS, tokens // SLOTS, width), x, 2, 1)
    return in_order(c == 0, pick(mine, c, 1), swap_c(pick(mine, 1 - c, 1)), 0)


def own_tokens(whole, place):
    z = place[3]
    pieces = [pick(whole, z)] + [swap_z(pick(whole, z ^ k), k) for k in (1, 2, 3)]
    return xor_order(pieces, z).reshape(-1, whole.shape[2])


def rows_over_z(own, place):
    z = place[3]
    blocks = own.reshape(BLOCKS, own.shape[0] // BLOCKS, own.shape[1])
    pieces = [pick(blocks, z)] + [swap_z(pick(blocks, z ^ k), k) for k in (1, 2, 3)]
    return xor_order(pieces, z)


def local_rows(rows, place):
    x, c, y, z = place
    got = swap_c(part(rows, 1 - c, 2, 0))
    both = in_order(c == 0, part(rows, c, 2, 0)[:, None], got[:, None], 1)
    other = swap_x(both)
    full = in_order(x == 0, both[:, None], other[:, None], 1)
    return full.reshape(2, SLOTS * rows.shape[1], rows.shape[2])


def row_pieces(own):
    across = swap_x(own)
    return (own, across, swap_c(own), swap_c(across))


def half(ref, axis, c):
    size = ref.shape[axis] // 2
    at = pl.ds(pl.multiple_of(c * size, size), size)
    return ref[at, :] if axis == 0 else ref[:, at]


def slot_places(owner, index, sub):
    slot = index // sub
    return (owner ^ (((slot & 1) << 1) | (slot >> 1))) * sub + (index - slot * sub)


def row_positions(owner, sub):
    index = jnp.arange(SLOTS * BLOCKS * sub, dtype=jnp.int32)
    slot = index // (BLOCKS * sub)
    block = (index // sub) % BLOCKS
    own_place = (owner ^ (((slot & 1) << 1) | (slot >> 1))) * sub
    return block * SLOTS * sub + own_place + index % sub


def lane_tables(positions):
    lane = jnp.arange(128, dtype=jnp.int32) % HDIM
    frequency = jnp.exp((lane // 2).astype(wide_type) * (-2.0 * math.log(10000.0) / ROT))
    angles = positions.astype(wide_type)[:, None] * frequency[None, :]
    turned = (lane < ROT)[None, :]
    even = (lane % 2 == 0)[None, :]
    sines = jnp.sin(angles)
    return (
        jnp.where(turned, jnp.cos(angles), 1.0),
        jnp.where(turned & even, -sines, 0.0),
        jnp.where(turned & ~even, sines, 0.0),
    )


def turn_lanes(v, cosines, to_even, to_odd):
    return v * cosines + pltpu.roll(v, 127, 1) * to_even + pltpu.roll(v, 1, 1) * to_odd


def take_block(ref, block, sub, group):
    starts = [(slot * BLOCKS + block) * sub for slot in range(SLOTS)]
    return jnp.concatenate([ref[at : at + sub, group * 128 : (group + 1) * 128] for at in starts], 0)


def put_block(ref, block, sub, group, value):
    for slot in range(SLOTS):
        at = (slot * BLOCKS + block) * sub
        ref[at : at + sub, group * 128 : (group + 1) * 128] = value[slot * sub : (slot + 1) * sub]


def block_allowed(owner, size, sub):
    key_place = slot_places(owner, lax.broadcasted_iota(jnp.int32, (size, size), 0), sub)
    query_place = slot_places(owner, lax.broadcasted_iota(jnp.int32, (size, size), 1), sub)
    return query_place >= key_place


def normed_of(residual, gain_ref, bias_ref):
    centered = residual - jnp.mean(residual, -1, keepdims=True)
    inverse_std = lax.rsqrt(jnp.mean(centered * centered, -1, keepdims=True) + epsilon)
    return low(centered * inverse_std * gain_ref[...] + bias_ref[...])


def first_kernel(scalars, own_ref, gain_ref, bias_ref, normed_out):
    normed_out[...] = normed_of(wide(own_ref[...]), gain_ref, bias_ref)


def first_norm(own, params, run):
    args = (own, params[0][None], params[1][None])
    return run("first_norm", first_kernel, args, (shape(low_type, *own.shape),))[0]


def settle_kernel(scalars, kept_ref, got_ref, residual_ref, shift_ref, gain_ref, bias_ref, middle_out, normed_out):
    middle = wide(residual_ref[...]) + (kept_ref[...] + wide(got_ref[...])) + shift_ref[...]
    middle_out[...] = middle
    normed_out[...] = normed_of(middle, gain_ref, bias_ref)


def settle(kept, got, residual, shift, gain, bias, run):
    args = (kept, got, residual, shift[None], gain[None], bias[None])
    outs = (shape(wide_type, *kept.shape), shape(low_type, *kept.shape))
    return run("settle", settle_kernel, args, outs)


def result_kernel(scalars, kept_ref, got_ref, residual_ref, shift_ref, out):
    out[...] = low(residual_ref[...] + (kept_ref[...] + wide(got_ref[...])) + shift_ref[...])


def final_result(kept, got, residual, shift, run):
    args = (kept, got, residual, shift[None])
    return run("result", result_kernel, args, (shape(low_type, *kept.shape),))[0]


def settle_back_kernel(scalars, kept_ref, got_ref, grad_ref, residual_ref, gain_ref, grad_out, low_out, shared_out):
    grad_normed = kept_ref[...] + wide(got_ref[...])
    grad_own = wide(grad_ref[...])
    residual = wide(residual_ref[...])
    centered = residual - jnp.mean(residual, -1, keepdims=True)
    inverse_std = lax.rsqrt(jnp.mean(centered * centered, -1, keepdims=True) + epsilon)
    unit_rows = centered * inverse_std
    grad_unit = grad_normed * gain_ref[...]
    pulled = grad_unit - jnp.mean(grad_unit, -1, keepdims=True)
    pulled = pulled - unit_rows * jnp.mean(grad_unit * unit_rows, -1, keepdims=True)
    grad_input = grad_own + inverse_std * pulled
    grad_out[...] = grad_input
    low_out[...] = low(grad_input)
    shared_out[0:1] = jnp.sum(grad_normed * unit_rows, 0, keepdims=True)
    shared_out[1:2] = jnp.sum(grad_normed, 0, keepdims=True)
    shared_out[2:3] = jnp.sum(grad_own, 0, keepdims=True)


def settle_back(kept, got, grad_own, residual, gain, run):
    args = (kept, got, grad_own, residual, gain[None])
    outs = (shape(wide_type, *kept.shape), shape(low_type, *kept.shape), shape(wide_type, 3, kept.shape[1]))
    return run("settle_back", settle_back_kernel, args, outs)


def gelu_and_slope(u):
    root = math.sqrt(2.0 / math.pi)
    square = u * u
    bend = jnp.tanh(root * u * (1.0 + 0.044715 * square))
    half = 0.5 * (1.0 + bend)
    slope = half + 0.5 * u * (1.0 - bend * bend) * (root * (1.0 + 3.0 * 0.044715 * square))
    return (u * half, slope)


def project_kernel(
    with_back, scalars, p0, p1, p2, p3, wq_ref, wk_ref, wv_ref, wu_ref, bu_ref, cos_ref, even_ref, odd_ref, *refs
):
    if with_back:
        back_ref, full_out, q_out, k_out, v_out, hidden_out, slope_out, sum_out = refs
    else:
        full_out, q_out, k_out, v_out, hidden_out, slope_out = refs
    c = scalars[1]
    tile = p0.shape[0]
    shift = half(bu_ref, 1, c)
    for i, piece in enumerate((p0, p1, p2, p3)):
        here = slice(i * tile, (i + 1) * tile)
        rows = piece[...]
        full_out[here] = rows
        turns = (cos_ref[here], even_ref[here], odd_ref[here])
        for w_ref, out in ((wq_ref, q_out), (wk_ref, k_out)):
            product = dot(rows, half(w_ref, 1, c))
            for at in range(0, product.shape[1], 128):
                out[here, at : at + 128] = low(turn_lanes(product[:, at : at + 128], *turns))
        v_out[here] = low(dot(rows, half(wv_ref, 1, c)))
        preact = dot(rows, half(wu_ref, 1, c)) + shift
        hidden, slope = gelu_and_slope(preact)
        hidden_out[here] = low(hidden)
        if with_back:
            grad = wide(back_ref[here]) * slope
            slope_out[here] = low(grad)
            column = jnp.sum(grad, 0, keepdims=True)
            sum_out[...] = column if i == 0 else sum_out[...] + column
        else:
            slope_out[here] = low(slope)


def project_row(pieces, params, turns, run, back=None):
    w_query, w_key, w_value, w_up, b_up = (params[i] for i in (2, 3, 4, 6, 7))
    rows, width = SLOTS * pieces[0].shape[0], pieces[0].shape[1]
    heads, units = w_query.shape[1] // 2, w_up.shape[1] // 2
    outs = [shape(low_type, rows, width)] + [shape(low_type, rows, heads)] * 3 + [shape(low_type, rows, units)] * 2
    args = (*pieces, w_query, w_key, w_value, w_up, b_up[None], *turns)
    if back is not None:
        args += (back,)
        outs.append(shape(wide_type, 1, units))
    return run("project", functools.partial(project_kernel, back is not None), args, outs, 7.5)


def attend_kernel(sub, scalars, q_ref, k_ref, v_ref, c_out, log_out):
    scaling = 1.0 / math.sqrt(HDIM)
    size = SLOTS * sub
    allowed = block_allowed(scalars[0], size, sub)
    lane = lax.broadcasted_iota(jnp.int32, (1, 128), 1)
    for group in range(q_ref.shape[1] // 128):
        queries = [take_block(q_ref, block, sub, group) for block in range(BLOCKS)]
        keys = [take_block(k_ref, block, sub, group) for block in range(BLOCKS)]
        values = [take_block(v_ref, block, sub, group).T for block in range(BLOCKS)]
        for j in range(BLOCKS):
            contexts = []
            for head in range(128 // HDIM):
                of_head = lane // HDIM == head
                query = jnp.where(of_head, queries[j], jnp.zeros_like(queries[j]))
                scores = [dot(keys[i], query, NT) for i in range(j + 1)]
                scores[j] = jnp.where(allowed, scores[j], negative)
                tops = [jnp.max(s, 0, keepdims=True) for s in scores]
                top = functools.reduce(jnp.maximum, tops)
                weights = [jnp.exp((s - top) * scaling) for s in scores]
                total = functools.reduce(jnp.add, [jnp.sum(w, 0, keepdims=True) for w in weights])
                context = None
                for i in range(j + 1):
                    rows = values[i][head * HDIM : (head + 1) * HDIM]
                    context = add(context, dot(rows, low(weights[i])))
                contexts.append(context * (1.0 / total))
                log_row = group * (128 // HDIM) + head
                log_out[log_row : log_row + 1, j * size : (j + 1) * size] = top * scaling + jnp.log(total)
            put_block(c_out, j, sub, group, low(jnp.concatenate(contexts, 0).T))


def attend(queries, keys, values, run):
    rows, width = queries.shape
    kernel = functools.partial(attend_kernel, rows // (BLOCKS * SLOTS))
    outs = (shape(low_type, rows, width), shape(wide_type, width // HDIM, rows))
    return run("attend", kernel, (queries, keys, values), outs, 7.5)


def attend_back_kernel(
    sub, scalars, q_ref, k_ref, v_ref, g_ref, log_ref, cos_ref, even_ref, odd_ref, dq_out, dk_out, dv_out
):
    scaling = 1.0 / math.sqrt(HDIM)
    size = SLOTS * sub
    allowed = block_allowed(scalars[0], size, sub)
    lane = lax.broadcasted_iota(jnp.int32, (1, 128), 1)
    turns = []
    for block in range(BLOCKS):
        cosines, to_even, to_odd = [take_block(ref, block, sub, 0) for ref in (cos_ref, even_ref, odd_ref)]
        turns.append((cosines, -to_even, -to_odd))
    for group in range(q_ref.shape[1] // 128):
        queries, keys, values, grads = [
            [take_block(ref, block, sub, group) for block in range(BLOCKS)] for ref in (q_ref, k_ref, v_ref, g_ref)
        ]
        flat_keys = [k.T for k in keys]
        grad_keys = [None] * BLOCKS
        grad_values = [None] * BLOCKS
        for j in range(BLOCKS):
            grad_query = []
            for head in range(128 // HDIM):
                of_head = lane // HDIM == head
                query = jnp.where(of_head, queries[j], jnp.zeros_like(queries[j]))
                grad = jnp.where(of_head, grads[j], jnp.zeros_like(grads[j]))
                log_row = group * (128 // HDIM) + head
                log_total = log_ref[log_row : log_row + 1, j * size : (j + 1) * size]
                probs, grad_probs, delta = [], [], None
                for i in range(j + 1):
                    weights = jnp.exp(dot(keys[i], query, NT) * scaling - log_total)
                    if i == j:
                        weights = jnp.where(allowed, weights, 0.0)
                    back = dot(values[i], grad, NT)
                    delta = add(delta, jnp.sum(weights * back, 0, keepdims=True))
                    probs.append(weights)
                    grad_probs.append(back)
                flat = None
                for i in range(j + 1):
                    grad_scores = low(probs[i] * (grad_probs[i] - delta))
                    grad_values[i] = add(grad_values[i], dot(low(probs[i]), grad))
                    grad_keys[i] = add(grad_keys[i], dot(grad_scores, query))
                    flat = add(flat, dot(flat_keys[i][head * HDIM : (head + 1) * HDIM], grad_scores))
                grad_query.append(flat)
            turned = jnp.concatenate(grad_query, 0).T * scaling
            put_block(dq_out, j, sub, group, low(turn_lanes(turned, *turns[j])))
        for i in range(BLOCKS):
            put_block(dk_out, i, sub, group, low(turn_lanes(grad_keys[i] * scaling, *turns[i])))
            put_block(dv_out, i, sub, group, low(grad_values[i]))


def attend_back_call(queries, keys, values, grad_context, logs, turns, run):
    rows, width = queries.shape
    kernel = functools.partial(attend_back_kernel, rows // (BLOCKS * SLOTS))
    args = (queries, keys, values, grad_context, logs, *turns)
    return run("attend_back", kernel, args, [shape(low_type, rows, width)] * 3, 10.5, limit=16)


def products(terms, weights, axis, c, start, stop):
    total = None
    for a_ref, w_ref in zip(terms, weights, strict=True):
        total = add(total, dot(a_ref[start:stop], half(w_ref, axis, c), NT if axis else NN))
    return total


def sent_kernel(axis, count, scalars, *refs):
    rows = refs[0].shape[0]
    refs[-1][...] = low(products(refs[:count], refs[count:-1], axis, scalars[1], rows // 2, rows))


def kept_kernel(axis, count, scalars, *refs):
    got_ref, kept_out, sent_out = refs[-3:]
    rows = refs[0].shape[0]
    tile = rows // SLOTS
    total = products(refs[:count], refs[count:-3], axis, scalars[1], 0, rows // 2) + wide(got_ref[...])
    sent_out[...] = low(total[tile:])
    kept_out[...] = total[:tile]


def send_part(terms, weights, axis, run):
    rows = terms[0].shape[0]
    width = weights[0].shape[1 - axis]
    kernel = functools.partial(sent_kernel, axis, len(terms))
    (sent,) = run("sent", kernel, (*terms, *weights), (shape(low_type, rows // 2, width),), 2.5)
    return swap_c(sent)


def keep_part(terms, weights, axis, got, run):
    tile = terms[0].shape[0] // SLOTS
    kernel = functools.partial(kept_kernel, axis, len(terms))
    outs = (shape(wide_type, tile, got.shape[1]), shape(low_type, tile, got.shape[1]))
    kept, sent = run("kept", kernel, (*terms, *weights, got), outs, 2.5)
    return (kept, swap_x(sent))


def raw_back_kernel(scalars, p0, p1, p2, p3, wo_ref, wd_ref, full_out, context_out, raw_out):
    tile = p0.shape[0]
    for i, piece in enumerate((p0, p1, p2, p3)):
        here = slice(i * tile, (i + 1) * tile)
        rows = piece[...]
        full_out[here] = rows
        context_out[here] = low(dot(rows, half(wo_ref, 0, scalars[1]), NT))
        raw_out[here] = low(dot(rows, half(wd_ref, 0, scalars[1]), NT))


def raw_back(pieces, params, run):
    w_out, w_down = params[5], params[8]
    rows, width = SLOTS * pieces[0].shape[0], pieces[0].shape[1]
    outs = [shape(low_type, rows, n) for n in (width, w_out.shape[0] // 2, w_down.shape[0] // 2)]
    return run("raw_back", raw_back_kernel, (*pieces, w_out, w_down), outs, 3.5)


def slopes_kernel(scalars, p0, p1, p2, p3, wo_ref, wd_ref, slope_ref, full_out, context_out, hidden_out, sum_out):
    tile = p0.shape[0]
    for i, piece in enumerate((p0, p1, p2, p3)):
        here = slice(i * tile, (i + 1) * tile)
        rows = piece[...]
        full_out[here] = rows
        context_out[here] = low(dot(rows, half(wo_ref, 0, scalars[1]), NT))
        grad = dot(rows, half(wd_ref, 0, scalars[1]), NT) * wide(slope_ref[here])
        hidden_out[here] = low(grad)
        column = jnp.sum(grad, 0, keepdims=True)
        sum_out[...] = column if i == 0 else sum_out[...] + column


def slopes(pieces, params, slope, run):
    w_out, w_down = params[5], params[8]
    rows, width = SLOTS * pieces[0].shape[0], pieces[0].shape[1]
    units = w_down.shape[0] // 2
    outs = [shape(low_type, rows, n) for n in (width, w_out.shape[0] // 2, units)] + [shape(wide_type, 1, units)]
    return run("slopes", slopes_kernel, (*pieces, w_out, w_down, slope), outs, 3.5)


def outer_kernel(counts, scalars, *refs):
    c, y, z = scalars[1], scalars[2], scalars[3]
    kept_out, sent_out = refs[-2:]
    at = 0
    refs = list(refs[:-2])
    for count in counts:
        left_ref = refs.pop(0)
        rights = [refs.pop(0) for _ in range(count)]
        tile = left_ref.shape[1] // 4
        piece = tile // 4
        total = sum(right.shape[1] for right in rights)
        for i in range(4):
            block = ((i >> 1) ^ (z & 1)) + 2 * ((i & 1) ^ (z >> 1))
            left = left_ref[:, pl.ds(pl.multiple_of(block * tile, tile), tile)]
            start = at
            for right_ref in rights:
                columns = slice(start, start + right_ref.shape[1])
                value = low(dot(left, right_ref[...], TN))
                a, b, d, e = [value[k * piece : (k + 1) * piece] for k in range(4)]
                a, b = jnp.where(c == 0, a, b), jnp.where(c == 0, b, a)
                d, e = jnp.where(c == 0, d, e), jnp.where(c == 0, e, d)
                for k, (upper, lower) in enumerate(((a, d), (b, e))):
                    rows = slice((2 * i + k) * piece, (2 * i + k + 1) * piece)
                    kept_out[rows, columns] = jnp.where(y == 0, upper, lower)
                    sent_out[rows, columns] = jnp.where(y == 0, lower, upper)
                start += right_ref.shape[1]
        at += total


class Reduction:
    hops = (swap_y, lambda v: swap_z(v, 1), lambda v: swap_z(v, 2), swap_c)

    def __init__(self, pairs, run):
        self.run = run
        self.at = 0
        total = sum(right.shape[1] for _, rights in pairs for right in rights)
        out = shape(low_type, pairs[0][0].shape[1] // 2, total)
        kernel = functools.partial(outer_kernel, [len(rights) for _, rights in pairs])
        args = [v for left, rights in pairs for v in (left, *rights)]
        self.kept, sent = run("outer", kernel, args, (out, out), 3 * total / 1024)
        self.got = self.hops[0](sent)

    def hop(self):
        out = shape(low_type, self.kept.shape[0] // 2, self.kept.shape[1])
        self.kept, sent = self.run("fold", fold_kernel, (self.kept, self.got), (out, out))
        self.at += 1
        self.got = self.hops[self.at](sent)

    def finish(self, cuts, outs):
        kernel = functools.partial(finish_kernel, cuts)
        return self.run("finish", kernel, (self.kept, self.got), [shape(wide_type, *dims) for dims in outs])


def finish_kernel(cuts, scalars, kept_ref, got_ref, *outs):
    first = scalars[1] == 0
    start = 0
    for stop, out in zip(cuts, outs, strict=True):
        own, other = wide(kept_ref[:, start:stop]), wide(got_ref[:, start:stop])
        rows = own.shape[0]
        if out.shape[0] == rows and out.shape[1] == own.shape[1]:
            out[...] = own + other
        else:
            both = jnp.concatenate([jnp.where(first, own, other), jnp.where(first, other, own)], 1)
            out[...] = both if out.shape[0] == rows else both.T
        start = stop


def fold_kernel(scalars, kept_ref, got_ref, kept_out, sent_out):
    half = kept_out.shape[0]
    kept_out[...] = low(wide(kept_ref[:half]) + wide(got_ref[:half]))
    sent_out[...] = low(wide(kept_ref[half:]) + wide(got_ref[half:]))


def small_rows(shared, hidden_sums, c):
    rows = [jnp.concatenate(shared, 0)]
    for sums in hidden_sums:
        whole = in_order(c == 0, sums, jnp.zeros_like(sums), 1).reshape(16, 2, -1)
        rows += [whole[:, i].reshape(1, -1) for i in (0, 1)]
    used = 10
    return low(jnp.concatenate(rows + [jnp.zeros((16 - used, shared[0].shape[1]), wide_type)], 0))


def wait_kernel(scalars, *refs):
    pass


def hold(run, *arrays):
    run("wait", wait_kernel, arrays, (), 0.5, ANYWHERE)


def quad_body(inputs, *rest):
    cotangent = rest[-1]
    r = lax.axis_index("rows")
    place = (lax.axis_index("tp"), r % 2, r // 2, lax.axis_index("seq"))
    x, c, y, z = place
    owner = 2 * x + c
    sub = inputs.shape[1] // SLOTS
    run = Chain(jnp.stack([owner, c, y, z]).astype(jnp.int32))
    one, two = rest[:10], rest[10:20]

    start = own_tokens(core_rows(inputs, place), place)
    turns = lane_tables(row_positions(owner, sub))
    normed = first_norm(start, one, run)
    pieces = row_pieces(normed)
    cot_own = own_tokens(core_rows(cotangent, place), place)
    full_one, q1, k1, v1, hidden_one, slope_one = project_row(pieces, one, turns, run)
    hold(run, cot_own)
    context_one, logs_one = attend(q1, k1, v1, run)
    cot_pieces = row_pieces(cot_own)
    branch = ((context_one, hidden_one), (one[5], one[8]), 0)
    got = send_part(*branch, run)
    hold(run, *cot_pieces)
    kept, got = keep_part(*branch, got, run)
    cot_full, grad_context, raw = raw_back(cot_pieces, two, run)
    middle, normed = settle(kept, got, start, one[9], two[0], two[1], run)

    full_two, q2, k2, v2, hidden_two, grad_hidden, sums_two = project_row(row_pieces(normed), two, turns, run, raw)
    down_two = Reduction([(cot_full, (hidden_two,))], run)
    up_two = Reduction([(full_two, (grad_hidden,))], run)
    context_two, logs_two = attend(q2, k2, v2, run)
    grads = attend_back_call(q2, k2, v2, grad_context, logs_two, turns, run)
    down_two.hop()
    back = ((*grads, grad_hidden), (*two[2:5], two[6]), 1)
    got = send_part(*back, run)
    heads_two = Reduction([(cot_full, (context_two,)), (full_two, grads)], run)
    kept, got = keep_part(*back, got, run)
    down_two.hop()
    branch = ((context_two, hidden_two), (two[5], two[8]), 0)
    res_got = send_part(*branch, run)
    grad_middle, grad_low, shared_two = settle_back(kept, got, cot_own, middle, two[0], run)
    pieces = row_pieces(grad_low)
    up_two.hop()
    down_two.hop()

    grad_full, grad_context, grad_hidden, sums_one = slopes(pieces, one, slope_one, run)
    down_one = Reduction([(grad_full, (hidden_one,))], run)
    heads_two.hop()
    up_two.hop()
    up_one = Reduction([(full_one, (grad_hidden,))], run)
    res_kept, res_got = keep_part(*branch, res_got, run)
    grads = attend_back_call(q1, k1, v1, grad_context, logs_one, turns, run)
    up_two.hop()
    down_one.hop()
    back = ((*grads, grad_hidden), (*one[2:5], one[6]), 1)
    got = send_part(*back, run)
    heads_two.hop()
    result = final_result(res_kept, res_got, middle, two[9], run)
    kept, got = keep_part(*back, got, run)
    out_rows = rows_over_z(result, place)
    heads_one = Reduction([(full_one, grads)], run)
    down_one.hop()
    heads_two.hop()
    up_one.hop()
    grad_start, start_low, shared_one = settle_back(kept, got, grad_middle, start, one[0], run)
    in_rows = rows_over_z(start_low, place)
    shared = jnp.concatenate([shared_one, shared_two], 0)
    shared = shared + swap_x(shared)
    width, units = q1.shape[1], hidden_one.shape[1]
    head_cut = [width, 2 * width, 3 * width, 4 * width]
    head_dims = (sub, 2 * width)
    wo_two, wq_two, wk_two, wv_two = heads_two.finish(head_cut, [head_dims[::-1]] + [head_dims] * 3)
    (wd_two,) = down_two.finish([units], [(2 * units, sub)])
    (wu_two,) = up_two.finish([units], [(sub, 2 * units)])
    hold(run, out_rows)
    outputs = local_rows(out_rows, place)
    down_one.hop()
    up_one.hop()
    heads_one.hop()
    small = small_rows([shared], [sums_one, sums_two], c)
    last = Reduction([(grad_full, (context_one,)), (small, (jnp.eye(16, 128, dtype=low_type),))], run)
    hold(run, in_rows)
    input_grad = local_rows(in_rows, place)
    up_one.hop()
    heads_one.hop()
    (wd_one,) = down_one.finish([units], [(2 * units, sub)])
    (wu_one,) = up_one.finish([units], [(sub, 2 * units)])
    last.hop()
    heads_one.hop()
    last.hop()
    wq_one, wk_one, wv_one = heads_one.finish(head_cut[:3], [head_dims] * 3)
    last.hop()
    wo_one, tail = last.finish([width, width + 128], [head_dims[::-1], (sub, 128)])
    columns = tail.T
    hidden_one, hidden_two = (columns[i : i + 2].reshape(-1) for i in (6, 8))
    return (
        outputs, input_grad,
        columns[0], columns[1], wq_one, wk_one, wv_one, wo_one, wu_one, hidden_one, wd_one, columns[2],
        columns[3], columns[4], wq_two, wk_two, wv_two, wo_two, wu_two, hidden_two, wd_two, columns[5],
    )


def solution(mesh):
    in_specs = (
        P("rows", "seq", None),
        P(),
        P(),
        P(None, "tp"),
        P(None, "tp"),
        P(None, "tp"),
        P("tp", None),
        P(None, "tp"),
        P("tp"),
        P("tp", None),
        P(),
        P(),
        P(),
        P(None, "tp"),
        P(None, "tp"),
        P(None, "tp"),
        P("tp", None),
        P(None, "tp"),
        P("tp"),
        P("tp", None),
        P(),
        P("rows", "seq", None),
    )
    out_specs = (
        P("rows", "seq", None),
        P("rows", "seq", None),
        P(("seq", "rows")),
        P(("seq", "rows")),
        P(("seq", "rows"), "tp"),
        P(("seq", "rows"), "tp"),
        P(("seq", "rows"), "tp"),
        P("tp", ("seq", "rows")),
        P(("seq", "rows"), "tp"),
        P(("tp", "seq", "rows")),
        P("tp", ("seq", "rows")),
        P(("seq", "rows")),
        P(("seq", "rows")),
        P(("seq", "rows")),
        P(("seq", "rows"), "tp"),
        P(("seq", "rows"), "tp"),
        P(("seq", "rows"), "tp"),
        P("tp", ("seq", "rows")),
        P(("seq", "rows"), "tp"),
        P(("tp", "seq", "rows")),
        P("tp", ("seq", "rows")),
        P(("seq", "rows")),
    )
    fits = (mesh.shape["seq"], mesh.shape["tp"], mesh.shape["rows"]) == (4, 2, 4)
    body = quad_body if fits else general_body
    return jax.shard_map(body, mesh=mesh, in_specs=in_specs, out_specs=out_specs, check_vma=False)
```

```python
import functools
import math

import jax
import jax.numpy as jnp
from jax import lax
from jax.experimental import pallas as pl
from jax.experimental.pallas import tpu as pltpu
from jax.sharding import PartitionSpec as P

HDIM = 64
ROT = 32


epsilon = 1e-05
negative = -1e30


def tables(position, length):
    positions = (position + jnp.arange(length, dtype=jnp.int32)).astype(jnp.float32)
    ladder = jnp.arange(ROT // 2, dtype=jnp.float32)
    frequency = jnp.exp(ladder * (-2.0 * math.log(10000.0) / ROT))
    angles = positions[:, None] * frequency[None, :]
    return (jnp.cos(angles), jnp.sin(angles))


def rotate(flat_rows, cos_table, sin_table):
    old_shape = flat_rows.shape
    headed = flat_rows.reshape(old_shape[:-1] + (old_shape[-1] // HDIM, HDIM))
    turned = headed[..., :ROT].reshape(headed.shape[:-1] + (ROT // 2, 2))
    even_part = turned[..., 0]
    odd_part = turned[..., 1]
    cos_wide = cos_table[:, None, :]
    sin_wide = sin_table[:, None, :]
    new_even = even_part * cos_wide - odd_part * sin_wide
    new_odd = odd_part * cos_wide + even_part * sin_wide
    joined = jnp.stack([new_even, new_odd], -1).reshape(headed.shape[:-1] + (ROT,))
    return jnp.concatenate([joined, headed[..., ROT:]], -1).reshape(old_shape)


def normalize(residual, gain, bias):
    centered = residual - jnp.mean(residual, -1, keepdims=True)
    inverse_std = lax.rsqrt(jnp.mean(centered * centered, -1, keepdims=True) + epsilon)
    unit_rows = centered * inverse_std
    return (unit_rows * gain + bias, unit_rows, inverse_std)


def normed_rows(residual, gain, bias):
    normed, unit_rows, inverse_std = normalize(residual, gain, bias)
    normed_low = normed.astype(jnp.bfloat16)
    return (normed_low, unit_rows, inverse_std)


def project(operand, weight):
    return jnp.dot(operand, weight, preferred_element_type=jnp.float32)


def back_project(operand, weight):
    return lax.dot_general(
        operand, weight, (((2,), (1,)), ((), ())), preferred_element_type=jnp.float32
    )


def outer(left_rows, right_rows):
    return lax.dot_general(
        left_rows, right_rows, (((0, 1), (0, 1)), ((), ())), preferred_element_type=jnp.float32
    )


def token_sum(operand):
    return jnp.sum(operand, axis=(0, 1))


def gelu_tanh(argument):
    return jax.nn.gelu(argument, approximate=True)


def headed_view(flat_rows):
    return flat_rows.reshape(flat_rows.shape[:-1] + (flat_rows.shape[-1] // HDIM, HDIM))


def allowed_mask(position, query_count, key_start, key_count):
    query_places = position + jnp.arange(query_count, dtype=jnp.int32)
    key_places = key_start + jnp.arange(key_count, dtype=jnp.int32)
    return query_places[:, None] >= key_places[None, :]


def block_scores(queries, key_rows, position, key_start):
    scaling = 1.0 / math.sqrt(HDIM)
    scores = (
        jnp.einsum(
            "bqhd,bkhd->bhqk",
            headed_view(queries),
            headed_view(key_rows),
            preferred_element_type=jnp.float32,
        )
        * scaling
    )
    allowed = allowed_mask(position, queries.shape[1], key_start, key_rows.shape[1])
    return (jnp.where(allowed, scores, negative), allowed)


def start_stats(queries):
    batch, query_count, width = queries.shape
    head_count = width // HDIM
    highest = jnp.full((batch, head_count, query_count), negative, jnp.float32)
    summed = jnp.zeros((batch, head_count, query_count), jnp.float32)
    return (highest, summed)


def start_values(queries):
    batch, query_count, width = queries.shape
    return jnp.zeros((batch, query_count, width // HDIM, HDIM), jnp.float32)


def stats_block(running, pieces, key_start, queries, position):
    highest, summed = running
    masked, allowed = block_scores(queries, pieces[0], position, key_start)
    new_high = jnp.maximum(highest, jnp.max(masked, -1))
    expo = jnp.where(allowed, jnp.exp(masked - new_high[..., None]), 0.0)
    summed = jnp.sum(expo, -1)
    return (new_high, summed)


def value_block(pieces, key_start, queries, position, log_total):
    masked, allowed = block_scores(queries, pieces[0], position, key_start)
    attn_low = jnp.where(allowed, jnp.exp(masked - log_total[..., None]), 0.0).astype(jnp.bfloat16)
    return jnp.einsum(
        "bhqk,bkhd->bqhd", attn_low, headed_view(pieces[1]), preferred_element_type=jnp.float32
    )


def fold_history(key_rows, value_rows, fold_fn, initial):
    return fold_fn(
        initial,
        (
            lax.all_gather(key_rows, "seq", axis=1, tiled=True),
            lax.all_gather(value_rows, "seq", axis=1, tiled=True),
        ),
        jnp.int32(0),
    )


def attend_fold(queries, key_rows, value_rows, position):

    def stats_piece(running, pieces, key_start):
        return stats_block(running, pieces, key_start, queries, position)

    highest, summed = fold_history(key_rows, value_rows, stats_piece, start_stats(queries))
    log_total = highest + jnp.log(summed)

    def value_piece(accumulated, pieces, key_start):
        return value_block(pieces, key_start, queries, position, log_total)

    accumulated = fold_history(key_rows, value_rows, value_piece, start_values(queries))
    return (accumulated.reshape(queries.shape), log_total)


def attend_back(queries, grad_context, log_total, row_delta, key_all, value_all, position):
    batch, block_size, width = queries.shape
    head_count = width // HDIM
    block_count = key_all.shape[1] // block_size
    scaling = 1.0 / math.sqrt(HDIM)
    headed_q = headed_view(queries)
    headed_g = headed_view(grad_context)

    def back_block(grad_query, block_index):
        offset = block_index * block_size
        key_rows = headed_view(lax.dynamic_slice_in_dim(key_all, offset, block_size, 1))
        value_rows = headed_view(lax.dynamic_slice_in_dim(value_all, offset, block_size, 1))
        scores = (
            jnp.einsum("bqhd,bkhd->bhqk", headed_q, key_rows, preferred_element_type=jnp.float32)
            * scaling
        )
        allowed = allowed_mask(position, block_size, offset, block_size)
        masked = jnp.where(allowed, scores, negative)
        attn_weights = jnp.where(allowed, jnp.exp(masked - log_total[..., None]), 0.0)
        grad_weights = jnp.einsum(
            "bqhd,bkhd->bhqk", headed_g, value_rows, preferred_element_type=jnp.float32
        )
        grad_score = (attn_weights * (grad_weights - row_delta[..., None])).astype(jnp.bfloat16)
        grad_query = (
            grad_query
            + jnp.einsum(
                "bhqk,bkhd->bqhd", grad_score, key_rows, preferred_element_type=jnp.float32
            )
            * scaling
        )
        grad_key = (
            jnp.einsum("bhqk,bqhd->bkhd", grad_score, headed_q, preferred_element_type=jnp.float32)
            * scaling
        )
        grad_value = jnp.einsum(
            "bhqk,bqhd->bkhd",
            attn_weights.astype(jnp.bfloat16),
            headed_g,
            preferred_element_type=jnp.float32,
        )
        return (
            grad_query,
            (
                grad_key.reshape(batch, block_size, width),
                grad_value.reshape(batch, block_size, width),
            ),
        )

    initial = jnp.zeros((batch, block_size, head_count, HDIM), jnp.float32)
    grad_query, key_terms = lax.scan(back_block, initial, jnp.arange(block_count, dtype=jnp.int32))
    return (grad_query.reshape(batch, block_size, width), key_terms)


def layer_forward(residual, params, cos_table, sin_table, position):
    norm_gain, norm_bias, w_query, w_key, w_value, w_out, w_up, b_up, w_down, b_down = params
    normed_low, unit_rows, inverse_std = normed_rows(residual, norm_gain, norm_bias)
    queries = rotate(project(normed_low, w_query), cos_table, sin_table).astype(jnp.bfloat16)
    key_rows = rotate(project(normed_low, w_key), cos_table, sin_table).astype(jnp.bfloat16)
    value_rows = project(normed_low, w_value).astype(jnp.bfloat16)
    context, log_total = attend_fold(queries, key_rows, value_rows, position)
    attn_branch = project(context.astype(jnp.bfloat16), w_out)
    preact = project(normed_low, w_up) + b_up
    hidden_low = gelu_tanh(preact).astype(jnp.bfloat16)
    branches = attn_branch + project(hidden_low, w_down)
    combined = lax.psum(branches, "tp")
    return (residual + combined + b_down, (context, log_total, None))


def layer_backward(residual, params, cos_table, sin_table, position, stashed, grad_out, grad_low):
    norm_gain, norm_bias, w_query, w_key, w_value, w_out, w_up, b_up, w_down, b_down = params
    context, log_total, gathered = stashed
    normed_low, unit_rows, inverse_std = normed_rows(residual, norm_gain, norm_bias)
    queries = rotate(project(normed_low, w_query), cos_table, sin_table).astype(jnp.bfloat16)
    key_rows = rotate(project(normed_low, w_key), cos_table, sin_table).astype(jnp.bfloat16)
    value_rows = project(normed_low, w_value).astype(jnp.bfloat16)
    key_all, value_all = (
        lax.all_gather(key_rows, "seq", axis=1, tiled=True),
        lax.all_gather(value_rows, "seq", axis=1, tiled=True),
    )
    grad_context = back_project(grad_low, w_out).astype(jnp.bfloat16)
    batch, block_size, width = queries.shape
    products = (grad_context.astype(jnp.float32) * context).reshape(
        batch, block_size, width // HDIM, HDIM
    )
    row_delta = jnp.transpose(jnp.sum(products, -1), (0, 2, 1))
    grad_query, key_terms = attend_back(
        queries, grad_context, log_total, row_delta, key_all, value_all, position
    )
    summed_keys, summed_values = (
        lax.psum_scatter(key_terms[0], "seq", scatter_dimension=0, tiled=True),
        lax.psum_scatter(key_terms[1], "seq", scatter_dimension=0, tiled=True),
    )
    own_keys = summed_keys[0]
    own_values = summed_values[0]
    grad_query_low = rotate(grad_query, cos_table, -sin_table).astype(jnp.bfloat16)
    grad_key_low = rotate(own_keys, cos_table, -sin_table).astype(jnp.bfloat16)
    grad_value_low = own_values.astype(jnp.bfloat16)
    preact = project(normed_low, w_up) + b_up
    hidden, gelu_pull = jax.vjp(gelu_tanh, preact)
    hidden_low = hidden.astype(jnp.bfloat16)
    grad_preact = gelu_pull(back_project(grad_low, w_down))[0]
    grad_preact_low = grad_preact.astype(jnp.bfloat16)
    partial_value = back_project(grad_query_low, w_query) + back_project(grad_key_low, w_key)
    partial_value = (
        partial_value + back_project(grad_value_low, w_value) + back_project(grad_preact_low, w_up)
    )
    grad_normed = lax.psum(partial_value, "tp")
    grad_unit = grad_normed * norm_gain
    centered_grad = grad_unit - jnp.mean(grad_unit, -1, keepdims=True)
    centered_grad = centered_grad - unit_rows * jnp.mean(grad_unit * unit_rows, -1, keepdims=True)
    grad_input = grad_out + inverse_std * centered_grad
    small = (token_sum(grad_normed * unit_rows), token_sum(grad_normed), token_sum(grad_out))
    gradients = (
        small[0],
        small[1],
        outer(normed_low, grad_query_low),
        outer(normed_low, grad_key_low),
        outer(normed_low, grad_value_low),
        outer(context.astype(jnp.bfloat16), grad_low),
        outer(normed_low, grad_preact_low),
        token_sum(grad_preact),
        outer(hidden_low, grad_low),
        small[2],
    )
    return (grad_input, gradients)


def general_body(
    inputs,
    norm_gain_one,
    norm_bias_one,
    query_one,
    key_one,
    value_one,
    output_one,
    up_one,
    up_bias_one,
    down_one,
    down_bias_one,
    norm_gain_two,
    norm_bias_two,
    query_two,
    key_two,
    value_two,
    output_two,
    up_two,
    up_bias_two,
    down_two,
    down_bias_two,
    cotangent,
):
    first_params = (
        norm_gain_one,
        norm_bias_one,
        query_one,
        key_one,
        value_one,
        output_one,
        up_one,
        up_bias_one,
        down_one,
        down_bias_one,
    )
    second_params = (
        norm_gain_two,
        norm_bias_two,
        query_two,
        key_two,
        value_two,
        output_two,
        up_two,
        up_bias_two,
        down_two,
        down_bias_two,
    )
    block_size = inputs.shape[1]
    position = lax.axis_index("seq") * block_size
    cos_table, sin_table = tables(position, block_size)
    start_rows = inputs.astype(jnp.float32)
    cot_rows = cotangent.astype(jnp.float32)
    middle, first_stash = layer_forward(start_rows, first_params, cos_table, sin_table, position)
    result, second_stash = layer_forward(middle, second_params, cos_table, sin_table, position)
    result_low = result.astype(jnp.bfloat16)
    middle_grad, second_grads = layer_backward(
        middle, second_params, cos_table, sin_table, position, second_stash, cot_rows, cotangent
    )
    middle_low = middle_grad.astype(jnp.bfloat16)
    start_grad, first_grads = layer_backward(
        start_rows,
        first_params,
        cos_table,
        sin_table,
        position,
        first_stash,
        middle_grad,
        middle_low,
    )
    start_low = start_grad.astype(jnp.bfloat16)
    everything = (
        lax.psum_scatter(first_grads[0], ("seq", "rows"), scatter_dimension=0, tiled=True),
        lax.psum_scatter(first_grads[1], ("seq", "rows"), scatter_dimension=0, tiled=True),
        lax.psum_scatter(first_grads[2], ("seq", "rows"), scatter_dimension=0, tiled=True),
        lax.psum_scatter(first_grads[3], ("seq", "rows"), scatter_dimension=0, tiled=True),
        lax.psum_scatter(first_grads[4], ("seq", "rows"), scatter_dimension=0, tiled=True),
        lax.psum_scatter(first_grads[5], ("seq", "rows"), scatter_dimension=1, tiled=True),
        lax.psum_scatter(first_grads[6], ("seq", "rows"), scatter_dimension=0, tiled=True),
        lax.psum_scatter(first_grads[7], ("seq", "rows"), scatter_dimension=0, tiled=True),
        lax.psum_scatter(first_grads[8], ("seq", "rows"), scatter_dimension=1, tiled=True),
        lax.psum_scatter(first_grads[9], ("seq", "rows"), scatter_dimension=0, tiled=True),
        lax.psum_scatter(second_grads[0], ("seq", "rows"), scatter_dimension=0, tiled=True),
        lax.psum_scatter(second_grads[1], ("seq", "rows"), scatter_dimension=0, tiled=True),
        lax.psum_scatter(second_grads[2], ("seq", "rows"), scatter_dimension=0, tiled=True),
        lax.psum_scatter(second_grads[3], ("seq", "rows"), scatter_dimension=0, tiled=True),
        lax.psum_scatter(second_grads[4], ("seq", "rows"), scatter_dimension=0, tiled=True),
        lax.psum_scatter(second_grads[5], ("seq", "rows"), scatter_dimension=1, tiled=True),
        lax.psum_scatter(second_grads[6], ("seq", "rows"), scatter_dimension=0, tiled=True),
        lax.psum_scatter(second_grads[7], ("seq", "rows"), scatter_dimension=0, tiled=True),
        lax.psum_scatter(second_grads[8], ("seq", "rows"), scatter_dimension=1, tiled=True),
        lax.psum_scatter(second_grads[9], ("seq", "rows"), scatter_dimension=0, tiled=True),
    )
    return (result_low, start_low) + tuple(everything)


BLOCKS = 4
SLOTS = 4
low_type = jnp.bfloat16
wide_type = jnp.float32
NT = (((1,), (1,)), ((), ()))
NN = (((1,), (0,)), ((), ()))
TN = (((0,), (0,)), ((), ()))
SCALARS = pl.BlockSpec(memory_space=pltpu.SMEM)
HERE = pl.BlockSpec(memory_space=pltpu.VMEM)
ANYWHERE = pl.BlockSpec(memory_space=pl.ANY)


def swap_x(v):
    return lax.ppermute(v, "tp", [(0, 1), (1, 0)])


def swap_c(v):
    return lax.ppermute(v, "rows", [(0, 1), (1, 0), (2, 3), (3, 2)])


def swap_y(v):
    return lax.ppermute(v, "rows", [(0, 2), (2, 0), (1, 3), (3, 1)])


def swap_z(v, k):
    return lax.ppermute(v, "seq", [(i, i ^ k) for i in range(4)])


def low(v):
    return v.astype(low_type)


def wide(v):
    return v.astype(wide_type)


def shape(kind, *dims):
    return jax.ShapeDtypeStruct(dims, kind)


def dot(a, b, dims=NN):
    return lax.dot_general(a, b, dims, preferred_element_type=wide_type)


def add(a, b):
    return b if a is None else a + b


def pick(v, index, axis=0):
    return lax.dynamic_index_in_dim(v, index, axis, keepdims=False)


def part(v, index, count, axis):
    size = v.shape[axis] // count
    return lax.dynamic_slice_in_dim(v, index * size, size, axis)


def in_order(first, a, b, axis):
    return jnp.where(first, jnp.concatenate([a, b], axis), jnp.concatenate([b, a], axis))


def xor_order(pieces, z):
    odd = (z & 1) == 1
    high = (z & 2) == 2
    a, b, c, d = pieces
    a, b, c, d = jnp.where(odd, b, a), jnp.where(odd, a, b), jnp.where(odd, d, c), jnp.where(odd, c, d)
    a, b, c, d = jnp.where(high, c, a), jnp.where(high, d, b), jnp.where(high, a, c), jnp.where(high, b, d)
    return jnp.stack([a, b, c, d])


class Chain:
    def __init__(self, scalars):
        self.scalars = scalars
        self.token = None
        self.weight = 1.1e9

    def __call__(self, name, kernel, args, outs, us=1, spec=HERE, limit=8):
        before = () if self.token is None else (self.token,)
        count = len(args)

        def with_token(*refs):
            outs_at = 1 + count + len(before)
            refs[outs_at][...] = jnp.zeros((8, 128), wide_type)
            kernel(*refs[: 1 + count], *refs[outs_at + 1 :])

        made = pl.pallas_call(
            with_token,
            in_specs=[SCALARS] + [spec] * count + [HERE] * len(before),
            out_specs=[HERE] * (1 + len(outs)),
            out_shape=[shape(wide_type, 8, 128), *outs],
            compiler_params=pltpu.CompilerParams(vmem_limit_bytes=limit * 2**20),
            cost_estimate=pl.CostEstimate(flops=int(us * self.weight), bytes_accessed=1000, transcendentals=0),
            name=name,
        )(self.scalars, *args, *before)
        self.token = made[0]
        return made[1:]


def across_part(local, x):
    rows, tokens, width = local.shape
    return part(local.reshape(rows, SLOTS, tokens // SLOTS, width), x, 2, 1)


def core_rows(kept, sent, c):
    return in_order(c == 0, kept, swap_c(sent), 0)


def own_tokens(whole, place):
    z = place[3]
    pieces = [pick(whole, z)] + [swap_z(pick(whole, z ^ k), k) for k in (1, 2, 3)]
    return xor_order(pieces, z).reshape(-1, whole.shape[2])


def rows_over_z(own, place):
    z = place[3]
    blocks = own.reshape(BLOCKS, own.shape[0] // BLOCKS, own.shape[1])
    pieces = [pick(blocks, z)] + [swap_z(pick(blocks, z ^ k), k) for k in (1, 2, 3)]
    return xor_order(pieces, z)


def place_kernel(scalars, own_ref, core_ref, across_ref, last_ref, out):
    owner = scalars[0]
    for i, ref in enumerate((own_ref, core_ref, across_ref, last_ref)):
        out[:, owner ^ i] = ref[...]


def local_rows(rows, place, run):
    x, c, y, z = place
    own = part(rows, c, 2, 0)
    across = swap_x(own)
    core = swap_c(part(rows, 1 - c, 2, 0))
    last = swap_x(core)

    def assemble():
        count, sub, width = own.shape
        (full,) = run("place", place_kernel, (own, core, across, last), (shape(rows.dtype, count, SLOTS, sub, width),))
        return full.reshape(count, SLOTS * sub, width)

    return assemble


def row_pieces(own):
    across = [swap_x(piece) for piece in own]
    return [list(own), across, [swap_c(piece) for piece in own], [swap_c(piece) for piece in across]]


def flat(pieces):
    return [piece for slot in pieces for piece in slot]


def stacked(refs):
    return refs[0][...] if len(refs) == 1 else jnp.concatenate([ref[...] for ref in refs], 0)


def slots_of(refs):
    count = len(refs) // SLOTS
    return [stacked(refs[i * count : (i + 1) * count]) for i in range(SLOTS)]


def put_pieces(refs, value):
    rows = refs[0].shape[0]
    for i, ref in enumerate(refs):
        ref[...] = value[i * rows : (i + 1) * rows]


PIECES = 2


def piece_shapes(kind, rows, width, count=PIECES):
    return [shape(kind, rows // count, width)] * count


def half(ref, axis, c):
    size = ref.shape[axis] // 2
    at = pl.ds(pl.multiple_of(c * size, size), size)
    return ref[at, :] if axis == 0 else ref[:, at]


def slot_places(owner, index, sub):
    slot = index // sub
    return (owner ^ (((slot & 1) << 1) | (slot >> 1))) * sub + (index - slot * sub)


def row_positions(owner, sub):
    index = jnp.arange(SLOTS * BLOCKS * sub, dtype=jnp.int32)
    slot = index // (BLOCKS * sub)
    block = (index // sub) % BLOCKS
    own_place = (owner ^ (((slot & 1) << 1) | (slot >> 1))) * sub
    return block * SLOTS * sub + own_place + index % sub


def lane_tables(positions):
    lane = jnp.arange(128, dtype=jnp.int32) % HDIM
    frequency = jnp.exp((lane // 2).astype(wide_type) * (-2.0 * math.log(10000.0) / ROT))
    angles = positions.astype(wide_type)[:, None] * frequency[None, :]
    turned = (lane < ROT)[None, :]
    even = (lane % 2 == 0)[None, :]
    sines = jnp.sin(angles)
    return (
        jnp.where(turned, jnp.cos(angles), 1.0),
        jnp.where(turned & even, -sines, 0.0),
        jnp.where(turned & ~even, sines, 0.0),
    )


def turn_lanes(v, cosines, to_even, to_odd):
    return v * cosines + pltpu.roll(v, 127, 1) * to_even + pltpu.roll(v, 1, 1) * to_odd


def take_block(ref, block, sub, group):
    starts = [(slot * BLOCKS + block) * sub for slot in range(SLOTS)]
    return jnp.concatenate([ref[at : at + sub, group * 128 : (group + 1) * 128] for at in starts], 0)


def put_block(ref, block, sub, group, value):
    for slot in range(SLOTS):
        at = (slot * BLOCKS + block) * sub
        ref[at : at + sub, group * 128 : (group + 1) * 128] = value[slot * sub : (slot + 1) * sub]


def block_allowed(owner, size, sub):
    key_place = slot_places(owner, lax.broadcasted_iota(jnp.int32, (size, size), 0), sub)
    query_place = slot_places(owner, lax.broadcasted_iota(jnp.int32, (size, size), 1), sub)
    return query_place >= key_place


def normed_of(residual, gain_ref, bias_ref):
    centered = residual - jnp.mean(residual, -1, keepdims=True)
    inverse_std = lax.rsqrt(jnp.mean(centered * centered, -1, keepdims=True) + epsilon)
    return low(centered * inverse_std * gain_ref[...] + bias_ref[...])


def first_kernel(scalars, own_ref, gain_ref, bias_ref, cot_ref, kept_out, sent_out, *normed_outs):
    put_pieces(normed_outs, normed_of(wide(own_ref[...]), gain_ref, bias_ref))
    kept_out[...] = cot_ref[:, scalars[1]]
    sent_out[...] = cot_ref[:, 1 - scalars[1]]


def first_norm(own, params, cot, run):
    args = (own, params[0][None], params[1][None], cot)
    half_cot = shape(cot.dtype, cot.shape[0], *cot.shape[2:])
    kept, sent, *normed = run("first_norm", first_kernel, args, [half_cot] * 2 + piece_shapes(low_type, *own.shape))
    return (normed, kept, sent)


def settle_kernel(count, scalars, kept_ref, *refs):
    residual_ref, shift_ref, gain_ref, bias_ref, middle_out = refs[count : count + 5]
    middle = wide(residual_ref[...]) + (kept_ref[...] + wide(stacked(refs[:count]))) + shift_ref[...]
    middle_out[...] = middle
    put_pieces(refs[count + 5 :], normed_of(middle, gain_ref, bias_ref))


def settle(kept, got, residual, shift, gain, bias, run):
    args = (kept, *got, residual, shift[None], gain[None], bias[None])
    outs = [shape(wide_type, *kept.shape)] + piece_shapes(low_type, *kept.shape)
    middle, *normed = run("settle", functools.partial(settle_kernel, len(got)), args, outs)
    return (middle, normed)


def result_kernel(count, scalars, kept_ref, *refs):
    residual_ref, shift_ref, out = refs[count:]
    out[...] = low(residual_ref[...] + (kept_ref[...] + wide(stacked(refs[:count]))) + shift_ref[...])


def final_result(kept, got, residual, shift, run):
    args = (kept, *got, residual, shift[None])
    return run("result", functools.partial(result_kernel, len(got)), args, (shape(low_type, *kept.shape),))[0]


def settle_back_kernel(count, scalars, kept_ref, *refs):
    grad_ref, residual_ref, gain_ref, grad_out, shared_out = refs[count : count + 5]
    grad_normed = kept_ref[...] + wide(stacked(refs[:count]))
    grad_own = wide(grad_ref[...])
    residual = wide(residual_ref[...])
    centered = residual - jnp.mean(residual, -1, keepdims=True)
    inverse_std = lax.rsqrt(jnp.mean(centered * centered, -1, keepdims=True) + epsilon)
    unit_rows = centered * inverse_std
    grad_unit = grad_normed * gain_ref[...]
    pulled = grad_unit - jnp.mean(grad_unit, -1, keepdims=True)
    pulled = pulled - unit_rows * jnp.mean(grad_unit * unit_rows, -1, keepdims=True)
    grad_input = grad_own + inverse_std * pulled
    grad_out[...] = grad_input
    put_pieces(refs[count + 5 :], low(grad_input))
    shared_out[0:1] = jnp.sum(grad_normed * unit_rows, 0, keepdims=True)
    shared_out[1:2] = jnp.sum(grad_normed, 0, keepdims=True)
    shared_out[2:3] = jnp.sum(grad_own, 0, keepdims=True)


def settle_back(kept, got, grad_own, residual, gain, run, count=PIECES):
    args = (kept, *got, grad_own, residual, gain[None])
    outs = [shape(wide_type, *kept.shape), shape(wide_type, 3, kept.shape[1])]
    kernel = functools.partial(settle_back_kernel, len(got))
    grad, shared, *lows = run("settle_back", kernel, args, outs + piece_shapes(low_type, *kept.shape, count))
    return (grad, lows, shared)


def gelu_and_slope(u):
    root = math.sqrt(2.0 / math.pi)
    square = u * u
    bend = jnp.tanh(root * u * (1.0 + 0.044715 * square))
    half = 0.5 * (1.0 + bend)
    slope = half + 0.5 * u * (1.0 - bend * bend) * (root * (1.0 + 3.0 * 0.044715 * square))
    return (u * half, slope)


def project_kernel(with_back, count, scalars, *refs):
    slots = slots_of(refs[:count])
    wq_ref, wk_ref, wv_ref, wu_ref, bu_ref, cos_ref, even_ref, odd_ref = refs[count : count + 8]
    refs = refs[count + 8 :]
    if with_back:
        back_ref, full_out, q_out, k_out, v_out, hidden_out, slope_out, sum_out = refs
    else:
        full_out, q_out, k_out, v_out, hidden_out, slope_out = refs
    c = scalars[1]
    tile = slots[0].shape[0]
    shift = half(bu_ref, 1, c)
    for i, rows in enumerate(slots):
        here = slice(i * tile, (i + 1) * tile)
        full_out[here] = rows
        turns = (cos_ref[here], even_ref[here], odd_ref[here])
        for w_ref, out in ((wq_ref, q_out), (wk_ref, k_out)):
            product = dot(rows, half(w_ref, 1, c))
            for at in range(0, product.shape[1], 128):
                out[here, at : at + 128] = low(turn_lanes(product[:, at : at + 128], *turns))
        v_out[here] = low(dot(rows, half(wv_ref, 1, c)))
        preact = dot(rows, half(wu_ref, 1, c)) + shift
        hidden, slope = gelu_and_slope(preact)
        hidden_out[here] = low(hidden)
        if with_back:
            grad = wide(back_ref[here]) * slope
            slope_out[here] = low(grad)
            column = jnp.sum(grad, 0, keepdims=True)
            sum_out[...] = column if i == 0 else sum_out[...] + column
        else:
            slope_out[here] = low(slope)


def project_row(pieces, params, turns, run, back=None):
    w_query, w_key, w_value, w_up, b_up = (params[i] for i in (2, 3, 4, 6, 7))
    pieces = flat(pieces)
    rows, width = sum(piece.shape[0] for piece in pieces), pieces[0].shape[1]
    heads, units = w_query.shape[1] // 2, w_up.shape[1] // 2
    outs = [shape(low_type, rows, width)] + [shape(low_type, rows, heads)] * 3 + [shape(low_type, rows, units)] * 2
    args = (*pieces, w_query, w_key, w_value, w_up, b_up[None], *turns)
    if back is not None:
        args += (back,)
        outs.append(shape(wide_type, 1, units))
    return run("project", functools.partial(project_kernel, back is not None, len(pieces)), args, outs, 7.5)


def attend_kernel(sub, scalars, q_ref, k_ref, v_ref, c_out, log_out):
    scaling = 1.0 / math.sqrt(HDIM)
    size = SLOTS * sub
    allowed = block_allowed(scalars[0], size, sub)
    lane = lax.broadcasted_iota(jnp.int32, (1, 128), 1)
    for group in range(q_ref.shape[1] // 128):
        queries = [take_block(q_ref, block, sub, group) for block in range(BLOCKS)]
        keys = [take_block(k_ref, block, sub, group) for block in range(BLOCKS)]
        values = [take_block(v_ref, block, sub, group).T for block in range(BLOCKS)]
        for j in range(BLOCKS):
            contexts = []
            for head in range(128 // HDIM):
                of_head = lane // HDIM == head
                query = jnp.where(of_head, queries[j], jnp.zeros_like(queries[j]))
                scores = [dot(keys[i], query, NT) for i in range(j + 1)]
                scores[j] = jnp.where(allowed, scores[j], negative)
                tops = [jnp.max(s, 0, keepdims=True) for s in scores]
                top = functools.reduce(jnp.maximum, tops)
                weights = [jnp.exp((s - top) * scaling) for s in scores]
                total = functools.reduce(jnp.add, [jnp.sum(w, 0, keepdims=True) for w in weights])
                context = None
                for i in range(j + 1):
                    rows = values[i][head * HDIM : (head + 1) * HDIM]
                    context = add(context, dot(rows, low(weights[i])))
                contexts.append(context * (1.0 / total))
                log_row = group * (128 // HDIM) + head
                log_out[log_row : log_row + 1, j * size : (j + 1) * size] = top * scaling + jnp.log(total)
            put_block(c_out, j, sub, group, low(jnp.concatenate(contexts, 0).T))


def attend(queries, keys, values, run):
    rows, width = queries.shape
    kernel = functools.partial(attend_kernel, rows // (BLOCKS * SLOTS))
    outs = (shape(low_type, rows, width), shape(wide_type, width // HDIM, rows))
    return run("attend", kernel, (queries, keys, values), outs, 7.5)


def attend_back_kernel(
    sub, scalars, q_ref, k_ref, v_ref, g_ref, log_ref, cos_ref, even_ref, odd_ref, dq_out, dk_out, dv_out
):
    scaling = 1.0 / math.sqrt(HDIM)
    size = SLOTS * sub
    allowed = block_allowed(scalars[0], size, sub)
    lane = lax.broadcasted_iota(jnp.int32, (1, 128), 1)
    turns = []
    for block in range(BLOCKS):
        cosines, to_even, to_odd = [take_block(ref, block, sub, 0) for ref in (cos_ref, even_ref, odd_ref)]
        turns.append((cosines, -to_even, -to_odd))
    for group in range(q_ref.shape[1] // 128):
        queries, keys, values, grads = [
            [take_block(ref, block, sub, group) for block in range(BLOCKS)] for ref in (q_ref, k_ref, v_ref, g_ref)
        ]
        flat_keys = [k.T for k in keys]
        grad_keys = [None] * BLOCKS
        grad_values = [None] * BLOCKS
        for j in range(BLOCKS):
            grad_query = []
            for head in range(128 // HDIM):
                of_head = lane // HDIM == head
                query = jnp.where(of_head, queries[j], jnp.zeros_like(queries[j]))
                grad = jnp.where(of_head, grads[j], jnp.zeros_like(grads[j]))
                log_row = group * (128 // HDIM) + head
                log_total = log_ref[log_row : log_row + 1, j * size : (j + 1) * size]
                probs, grad_probs, delta = [], [], None
                for i in range(j + 1):
                    weights = jnp.exp(dot(keys[i], query, NT) * scaling - log_total)
                    if i == j:
                        weights = jnp.where(allowed, weights, 0.0)
                    back = dot(values[i], grad, NT)
                    delta = add(delta, jnp.sum(weights * back, 0, keepdims=True))
                    probs.append(weights)
                    grad_probs.append(back)
                flat = None
                for i in range(j + 1):
                    grad_scores = low(probs[i] * (grad_probs[i] - delta))
                    grad_values[i] = add(grad_values[i], dot(low(probs[i]), grad))
                    grad_keys[i] = add(grad_keys[i], dot(grad_scores, query))
                    flat = add(flat, dot(flat_keys[i][head * HDIM : (head + 1) * HDIM], grad_scores))
                grad_query.append(flat)
            turned = jnp.concatenate(grad_query, 0).T * scaling
            put_block(dq_out, j, sub, group, low(turn_lanes(turned, *turns[j])))
        for i in range(BLOCKS):
            put_block(dk_out, i, sub, group, low(turn_lanes(grad_keys[i] * scaling, *turns[i])))
            put_block(dv_out, i, sub, group, low(grad_values[i]))


def attend_back_call(queries, keys, values, grad_context, logs, turns, run):
    rows, width = queries.shape
    kernel = functools.partial(attend_back_kernel, rows // (BLOCKS * SLOTS))
    args = (queries, keys, values, grad_context, logs, *turns)
    return run("attend_back", kernel, args, [shape(low_type, rows, width)] * 3, 0, limit=16)


def products(terms, weights, axis, c, start, stop):
    total = None
    for a_ref, w_ref in zip(terms, weights, strict=True):
        total = add(total, dot(a_ref[start:stop], half(w_ref, axis, c), NT if axis else NN))
    return total


def sent_kernel(axis, count, scalars, *refs):
    rows = refs[0].shape[0]
    put_pieces(refs[2 * count :], low(products(refs[:count], refs[count : 2 * count], axis, scalars[1], rows // 2, rows)))


def kept_kernel(axis, count, pieces, scalars, *refs):
    rows = refs[0].shape[0]
    tile = rows // SLOTS
    got_refs, (kept_out, *sent_outs) = refs[2 * count : 2 * count + pieces], refs[2 * count + pieces :]
    total = products(refs[:count], refs[count : 2 * count], axis, scalars[1], 0, rows // 2)
    put_pieces(sent_outs, low(total[tile:] + wide(stacked(got_refs[pieces // 2 :]))))
    kept_out[...] = total[:tile] + wide(stacked(got_refs[: pieces // 2]))


def send_part(terms, weights, axis, run):
    rows, width = terms[0].shape[0], weights[0].shape[1 - axis]
    kernel = functools.partial(sent_kernel, axis, len(terms))
    outs = piece_shapes(low_type, rows // 2, width, 2 * PIECES)
    return [swap_c(sent) for sent in run("sent", kernel, (*terms, *weights), outs, 2.5)]


def keep_part(terms, weights, axis, got, run, count=1):
    rows, width = terms[0].shape[0] // SLOTS, weights[0].shape[1 - axis]
    kernel = functools.partial(kept_kernel, axis, len(terms), len(got))
    outs = [shape(wide_type, rows, width)] + piece_shapes(low_type, rows, width, count)
    kept, *sent = run("kept", kernel, (*terms, *weights, *got), outs, 2.5)
    return (kept, [swap_x(piece) for piece in sent])


def raw_back_kernel(count, scalars, *refs):
    slots = slots_of(refs[:count])
    wo_ref, wd_ref, full_out, context_out, raw_out = refs[count:]
    tile = slots[0].shape[0]
    for i, rows in enumerate(slots):
        here = slice(i * tile, (i + 1) * tile)
        full_out[here] = rows
        context_out[here] = low(dot(rows, half(wo_ref, 0, scalars[1]), NT))
        raw_out[here] = low(dot(rows, half(wd_ref, 0, scalars[1]), NT))


def raw_back(pieces, params, run):
    w_out, w_down = params[5], params[8]
    pieces = flat(pieces)
    rows, width = sum(piece.shape[0] for piece in pieces), pieces[0].shape[1]
    outs = [shape(low_type, rows, n) for n in (width, w_out.shape[0] // 2, w_down.shape[0] // 2)]
    return run("raw_back", functools.partial(raw_back_kernel, len(pieces)), (*pieces, w_out, w_down), outs, 3.5)


def slopes_kernel(count, scalars, *refs):
    slots = slots_of(refs[:count])
    wo_ref, wd_ref, slope_ref, full_out, context_out, hidden_out, sum_out = refs[count:]
    tile = slots[0].shape[0]
    for i, rows in enumerate(slots):
        here = slice(i * tile, (i + 1) * tile)
        full_out[here] = rows
        context_out[here] = low(dot(rows, half(wo_ref, 0, scalars[1]), NT))
        grad = dot(rows, half(wd_ref, 0, scalars[1]), NT) * wide(slope_ref[here])
        hidden_out[here] = low(grad)
        column = jnp.sum(grad, 0, keepdims=True)
        sum_out[...] = column if i == 0 else sum_out[...] + column


def slopes(pieces, params, slope, run):
    w_out, w_down = params[5], params[8]
    pieces = flat(pieces)
    rows, width = sum(piece.shape[0] for piece in pieces), pieces[0].shape[1]
    units = w_down.shape[0] // 2
    outs = [shape(low_type, rows, n) for n in (width, w_out.shape[0] // 2, units)] + [shape(wide_type, 1, units)]
    return run("slopes", functools.partial(slopes_kernel, len(pieces)), (*pieces, w_out, w_down, slope), outs, 3.5)


def outer_kernel(counts, scalars, *refs):
    c, y, z = scalars[1], scalars[2], scalars[3]
    kept_out, sent_out = refs[-2:]
    at = 0
    refs = list(refs[:-2])
    for count in counts:
        left_ref = refs.pop(0)
        rights = [refs.pop(0) for _ in range(count)]
        tile = left_ref.shape[1] // 4
        piece = tile // 4
        total = sum(right.shape[1] for right in rights)
        for i in range(4):
            block = ((i >> 1) ^ (z & 1)) + 2 * ((i & 1) ^ (z >> 1))
            left = left_ref[:, pl.ds(pl.multiple_of(block * tile, tile), tile)]
            start = at
            for right_ref in rights:
                columns = slice(start, start + right_ref.shape[1])
                value = low(dot(left, right_ref[...], TN))
                a, b, d, e = [value[k * piece : (k + 1) * piece] for k in range(4)]
                a, b = jnp.where(c == 0, a, b), jnp.where(c == 0, b, a)
                d, e = jnp.where(c == 0, d, e), jnp.where(c == 0, e, d)
                for k, (upper, lower) in enumerate(((a, d), (b, e))):
                    rows = slice((2 * i + k) * piece, (2 * i + k + 1) * piece)
                    kept_out[rows, columns] = jnp.where(y == 0, upper, lower)
                    sent_out[rows, columns] = jnp.where(y == 0, lower, upper)
                start += right_ref.shape[1]
        at += total


class Reduction:
    hops = (swap_y, lambda v: swap_z(v, 1), lambda v: swap_z(v, 2), swap_c)

    def __init__(self, pairs, run):
        self.run = run
        self.at = 0
        total = sum(right.shape[1] for _, rights in pairs for right in rights)
        out = shape(low_type, pairs[0][0].shape[1] // 2, total)
        kernel = functools.partial(outer_kernel, [len(rights) for _, rights in pairs])
        args = [v for left, rights in pairs for v in (left, *rights)]
        self.kept, sent = run("outer", kernel, args, (out, out), 3 * total / 1024)
        self.got = self.hops[0](sent)

    def hop(self):
        out = shape(low_type, self.kept.shape[0] // 2, self.kept.shape[1])
        self.kept, sent = self.run("fold", fold_kernel, (self.kept, self.got), (out, out), 6)
        self.at += 1
        self.got = self.hops[self.at](sent)

    def finish(self, cuts, outs):
        kernel = functools.partial(finish_kernel, cuts)
        return self.run("finish", kernel, (self.kept, self.got), [shape(wide_type, *dims) for dims in outs])


def finish_kernel(cuts, scalars, kept_ref, got_ref, *outs):
    first = scalars[1] == 0
    start = 0
    for stop, out in zip(cuts, outs, strict=True):
        own, other = wide(kept_ref[:, start:stop]), wide(got_ref[:, start:stop])
        rows = own.shape[0]
        if out.shape[0] == rows and out.shape[1] == own.shape[1]:
            out[...] = own + other
        else:
            both = jnp.concatenate([jnp.where(first, own, other), jnp.where(first, other, own)], 1)
            out[...] = both
        start = stop


def fold_kernel(scalars, kept_ref, got_ref, kept_out, sent_out):
    half = kept_out.shape[0]
    kept_out[...] = low(wide(kept_ref[:half]) + wide(got_ref[:half]))
    sent_out[...] = low(wide(kept_ref[half:]) + wide(got_ref[half:]))


def small_kernel(scalars, shared_ref, *refs):
    out = refs[-1]
    first = scalars[1] == 0
    rows = [shared_ref[...]]
    for ref in refs[:-1]:
        sums = ref[...]
        for start in (0, 64):
            cuts = [sums[:, at + start : at + start + 64] for at in range(0, sums.shape[1], 128)]
            mine = jnp.concatenate(cuts, 1)
            none = jnp.zeros_like(mine)
            rows.append(jnp.where(first, jnp.concatenate([mine, none], 1), jnp.concatenate([none, mine], 1)))
    used = sum(row.shape[0] for row in rows)
    rows.append(jnp.zeros((out.shape[0] - used, out.shape[1]), wide_type))
    out[...] = low(jnp.concatenate(rows, 0))


def small_rows(shared, hidden_sums, run):
    return run("small", small_kernel, (shared, *hidden_sums), (shape(low_type, 16, shared.shape[1]),))[0]


def wait_kernel(scalars, *refs):
    pass


def split_kernel(scalars, ref, *outs):
    put_pieces(outs, ref[...])


def in_pieces(v, run):
    return run("split", split_kernel, (v,), piece_shapes(v.dtype, *v.shape))


def hold(run, *arrays):
    run("wait", wait_kernel, arrays, (), 0.5, ANYWHERE)


def quad_body(inputs, *rest):
    cotangent = rest[-1]
    r = lax.axis_index("rows")
    place = (lax.axis_index("tp"), r % 2, r // 2, lax.axis_index("seq"))
    x, c, y, z = place
    owner = 2 * x + c
    sub = inputs.shape[1] // SLOTS
    run = Chain(jnp.stack([owner, c, y, z, x]).astype(jnp.int32))
    one, two = rest[:10], rest[10:20]

    mine = across_part(inputs, x)
    start = own_tokens(core_rows(pick(mine, c, 1), pick(mine, 1 - c, 1), c), place)
    turns = lane_tables(row_positions(owner, sub))
    normed, cot_kept, cot_sent = first_norm(start, one, across_part(cotangent, x), run)
    pieces = row_pieces(normed)
    cot_own = own_tokens(core_rows(cot_kept, cot_sent, c), place)
    full_one, q1, k1, v1, hidden_one, slope_one = project_row(pieces, one, turns, run)
    cot_parts = in_pieces(cot_own, run)
    context_one, logs_one = attend(q1, k1, v1, run)
    cot_pieces = row_pieces(cot_parts)
    branch = ((context_one, hidden_one), (one[5], one[8]), 0)
    got = send_part(*branch, run)
    hold(run, *flat(cot_pieces))
    kept, got = keep_part(*branch, got, run)
    cot_full, grad_context, raw = raw_back(cot_pieces, two, run)
    middle, normed = settle(kept, got, start, one[9], two[0], two[1], run)

    full_two, q2, k2, v2, hidden_two, grad_hidden, sums_two = project_row(row_pieces(normed), two, turns, run, raw)
    run.weight = 0.28e9
    units_two = Reduction([(cot_full, (hidden_two,)), (full_two, (grad_hidden,))], run)
    context_two, logs_two = attend(q2, k2, v2, run)
    grads = attend_back_call(q2, k2, v2, grad_context, logs_two, turns, run)
    back = ((*grads, grad_hidden), (*two[2:5], two[6]), 1)
    got = send_part(*back, run)
    heads_two = Reduction([(cot_full, (context_two,)), (full_two, grads)], run)
    kept, got = keep_part(*back, got, run)
    branch = ((context_two, hidden_two), (two[5], two[8]), 0)
    res_got = send_part(*branch, run)
    grad_middle, grad_low, shared_two = settle_back(kept, got, cot_own, middle, two[0], run)
    pieces = row_pieces(grad_low)
    units_two.hop()
    res_kept, res_got = keep_part(*branch, res_got, run)

    grad_full, grad_context, grad_hidden, sums_one = slopes(pieces, one, slope_one, run)
    heads_two.hop()
    units_one = Reduction([(grad_full, (hidden_one,)), (full_one, (grad_hidden,))], run)
    result = final_result(res_kept, res_got, middle, two[9], run)
    out_rows = rows_over_z(result, place)
    grads = attend_back_call(q1, k1, v1, grad_context, logs_one, turns, run)
    back = ((*grads, grad_hidden), (*one[2:5], one[6]), 1)
    got = send_part(*back, run)
    hold(run, out_rows)
    units_two.hop()
    kept, got = keep_part(*back, got, run)
    heads_one = Reduction([(grad_full, (context_one,)), (full_one, grads)], run)
    heads_two.hop()
    grad_start, start_low, shared_one = settle_back(kept, got, grad_middle, start, one[0], run, 1)
    in_rows = rows_over_z(start_low[0], place)
    outputs = local_rows(out_rows, place, run)
    units_one.hop()
    units_two.hop()
    shared = jnp.concatenate([shared_one, shared_two], 0)
    shared = shared + swap_x(shared)
    heads_two.hop()
    small = small_rows(shared, [sums_one, sums_two], run)
    last = Reduction([(small, (jnp.eye(16, 128, dtype=low_type),))], run)
    width, units = q1.shape[1], hidden_one.shape[1]
    head_cut = [width, 2 * width, 3 * width, 4 * width]
    head_dims = (sub, 2 * width)
    wd_two, wu_two = units_two.finish([units, 2 * units], [(sub, 2 * units)] * 2)
    hold(run, in_rows)
    input_grad = local_rows(in_rows, place, run)
    wo_two, wq_two, wk_two, wv_two = heads_two.finish(head_cut, [head_dims] * 4)
    outputs = outputs()
    heads_one.hop()
    units_one.hop()
    last.hop()
    input_grad = input_grad()
    heads_one.hop()
    last.hop()
    units_one.hop()
    heads_one.hop()
    last.hop()
    wd_one, wu_one = units_one.finish([units, 2 * units], [(sub, 2 * units)] * 2)
    wo_one, wq_one, wk_one, wv_one = heads_one.finish(head_cut, [head_dims] * 4)
    (tail,) = last.finish([128], [(sub, 128)])
    columns = tail.T
    hidden_one, hidden_two = (columns[i : i + 2].reshape(-1) for i in (6, 8))
    return (
        outputs, input_grad,
        columns[0], columns[1], wq_one, wk_one, wv_one, wo_one.T, wu_one, hidden_one, wd_one.T, columns[2],
        columns[3], columns[4], wq_two, wk_two, wv_two, wo_two.T, wu_two, hidden_two, wd_two.T, columns[5],
    )


def solution(mesh):
    in_specs = (
        P("rows", "seq", None),
        P(),
        P(),
        P(None, "tp"),
        P(None, "tp"),
        P(None, "tp"),
        P("tp", None),
        P(None, "tp"),
        P("tp"),
        P("tp", None),
        P(),
        P(),
        P(),
        P(None, "tp"),
        P(None, "tp"),
        P(None, "tp"),
        P("tp", None),
        P(None, "tp"),
        P("tp"),
        P("tp", None),
        P(),
        P("rows", "seq", None),
    )
    out_specs = (
        P("rows", "seq", None),
        P("rows", "seq", None),
        P(("seq", "rows")),
        P(("seq", "rows")),
        P(("seq", "rows"), "tp"),
        P(("seq", "rows"), "tp"),
        P(("seq", "rows"), "tp"),
        P("tp", ("seq", "rows")),
        P(("seq", "rows"), "tp"),
        P(("tp", "seq", "rows")),
        P("tp", ("seq", "rows")),
        P(("seq", "rows")),
        P(("seq", "rows")),
        P(("seq", "rows")),
        P(("seq", "rows"), "tp"),
        P(("seq", "rows"), "tp"),
        P(("seq", "rows"), "tp"),
        P("tp", ("seq", "rows")),
        P(("seq", "rows"), "tp"),
        P(("tp", "seq", "rows")),
        P("tp", ("seq", "rows")),
        P(("seq", "rows")),
    )
    fits = (mesh.shape["seq"], mesh.shape["tp"], mesh.shape["rows"]) == (4, 2, 4)
    body = quad_body if fits else general_body
    return jax.shard_map(body, mesh=mesh, in_specs=in_specs, out_specs=out_specs, check_vma=False)
```

```python
import functools
import math

import jax
import jax.numpy as jnp
from jax import lax
from jax.experimental import pallas as pl
from jax.experimental.pallas import tpu as pltpu
from jax.sharding import PartitionSpec as P

HDIM = 64
ROT = 32


epsilon = 1e-05
negative = -1e30


def tables(position, length):
    positions = (position + jnp.arange(length, dtype=jnp.int32)).astype(jnp.float32)
    ladder = jnp.arange(ROT // 2, dtype=jnp.float32)
    frequency = jnp.exp(ladder * (-2.0 * math.log(10000.0) / ROT))
    angles = positions[:, None] * frequency[None, :]
    return (jnp.cos(angles), jnp.sin(angles))


def rotate(flat_rows, cos_table, sin_table):
    old_shape = flat_rows.shape
    headed = flat_rows.reshape(old_shape[:-1] + (old_shape[-1] // HDIM, HDIM))
    turned = headed[..., :ROT].reshape(headed.shape[:-1] + (ROT // 2, 2))
    even_part = turned[..., 0]
    odd_part = turned[..., 1]
    cos_wide = cos_table[:, None, :]
    sin_wide = sin_table[:, None, :]
    new_even = even_part * cos_wide - odd_part * sin_wide
    new_odd = odd_part * cos_wide + even_part * sin_wide
    joined = jnp.stack([new_even, new_odd], -1).reshape(headed.shape[:-1] + (ROT,))
    return jnp.concatenate([joined, headed[..., ROT:]], -1).reshape(old_shape)


def normalize(residual, gain, bias):
    centered = residual - jnp.mean(residual, -1, keepdims=True)
    inverse_std = lax.rsqrt(jnp.mean(centered * centered, -1, keepdims=True) + epsilon)
    unit_rows = centered * inverse_std
    return (unit_rows * gain + bias, unit_rows, inverse_std)


def normed_rows(residual, gain, bias):
    normed, unit_rows, inverse_std = normalize(residual, gain, bias)
    normed_low = normed.astype(jnp.bfloat16)
    return (normed_low, unit_rows, inverse_std)


def project(operand, weight):
    return jnp.dot(operand, weight, preferred_element_type=jnp.float32)


def back_project(operand, weight):
    return lax.dot_general(
        operand, weight, (((2,), (1,)), ((), ())), preferred_element_type=jnp.float32
    )


def outer(left_rows, right_rows):
    return lax.dot_general(
        left_rows, right_rows, (((0, 1), (0, 1)), ((), ())), preferred_element_type=jnp.float32
    )


def token_sum(operand):
    return jnp.sum(operand, axis=(0, 1))


def gelu_tanh(argument):
    return jax.nn.gelu(argument, approximate=True)


def headed_view(flat_rows):
    return flat_rows.reshape(flat_rows.shape[:-1] + (flat_rows.shape[-1] // HDIM, HDIM))


def allowed_mask(position, query_count, key_start, key_count):
    query_places = position + jnp.arange(query_count, dtype=jnp.int32)
    key_places = key_start + jnp.arange(key_count, dtype=jnp.int32)
    return query_places[:, None] >= key_places[None, :]


def block_scores(queries, key_rows, position, key_start):
    scaling = 1.0 / math.sqrt(HDIM)
    scores = (
        jnp.einsum(
            "bqhd,bkhd->bhqk",
            headed_view(queries),
            headed_view(key_rows),
            preferred_element_type=jnp.float32,
        )
        * scaling
    )
    allowed = allowed_mask(position, queries.shape[1], key_start, key_rows.shape[1])
    return (jnp.where(allowed, scores, negative), allowed)


def start_stats(queries):
    batch, query_count, width = queries.shape
    head_count = width // HDIM
    highest = jnp.full((batch, head_count, query_count), negative, jnp.float32)
    summed = jnp.zeros((batch, head_count, query_count), jnp.float32)
    return (highest, summed)


def start_values(queries):
    batch, query_count, width = queries.shape
    return jnp.zeros((batch, query_count, width // HDIM, HDIM), jnp.float32)


def stats_block(running, pieces, key_start, queries, position):
    highest, summed = running
    masked, allowed = block_scores(queries, pieces[0], position, key_start)
    new_high = jnp.maximum(highest, jnp.max(masked, -1))
    expo = jnp.where(allowed, jnp.exp(masked - new_high[..., None]), 0.0)
    summed = jnp.sum(expo, -1)
    return (new_high, summed)


def value_block(pieces, key_start, queries, position, log_total):
    masked, allowed = block_scores(queries, pieces[0], position, key_start)
    attn_low = jnp.where(allowed, jnp.exp(masked - log_total[..., None]), 0.0).astype(jnp.bfloat16)
    return jnp.einsum(
        "bhqk,bkhd->bqhd", attn_low, headed_view(pieces[1]), preferred_element_type=jnp.float32
    )


def fold_history(key_rows, value_rows, fold_fn, initial):
    return fold_fn(
        initial,
        (
            lax.all_gather(key_rows, "seq", axis=1, tiled=True),
            lax.all_gather(value_rows, "seq", axis=1, tiled=True),
        ),
        jnp.int32(0),
    )


def attend_fold(queries, key_rows, value_rows, position):

    def stats_piece(running, pieces, key_start):
        return stats_block(running, pieces, key_start, queries, position)

    highest, summed = fold_history(key_rows, value_rows, stats_piece, start_stats(queries))
    log_total = highest + jnp.log(summed)

    def value_piece(accumulated, pieces, key_start):
        return value_block(pieces, key_start, queries, position, log_total)

    accumulated = fold_history(key_rows, value_rows, value_piece, start_values(queries))
    return (accumulated.reshape(queries.shape), log_total)


def attend_back(queries, grad_context, log_total, row_delta, key_all, value_all, position):
    batch, block_size, width = queries.shape
    head_count = width // HDIM
    block_count = key_all.shape[1] // block_size
    scaling = 1.0 / math.sqrt(HDIM)
    headed_q = headed_view(queries)
    headed_g = headed_view(grad_context)

    def back_block(grad_query, block_index):
        offset = block_index * block_size
        key_rows = headed_view(lax.dynamic_slice_in_dim(key_all, offset, block_size, 1))
        value_rows = headed_view(lax.dynamic_slice_in_dim(value_all, offset, block_size, 1))
        scores = (
            jnp.einsum("bqhd,bkhd->bhqk", headed_q, key_rows, preferred_element_type=jnp.float32)
            * scaling
        )
        allowed = allowed_mask(position, block_size, offset, block_size)
        masked = jnp.where(allowed, scores, negative)
        attn_weights = jnp.where(allowed, jnp.exp(masked - log_total[..., None]), 0.0)
        grad_weights = jnp.einsum(
            "bqhd,bkhd->bhqk", headed_g, value_rows, preferred_element_type=jnp.float32
        )
        grad_score = (attn_weights * (grad_weights - row_delta[..., None])).astype(jnp.bfloat16)
        grad_query = (
            grad_query
            + jnp.einsum(
                "bhqk,bkhd->bqhd", grad_score, key_rows, preferred_element_type=jnp.float32
            )
            * scaling
        )
        grad_key = (
            jnp.einsum("bhqk,bqhd->bkhd", grad_score, headed_q, preferred_element_type=jnp.float32)
            * scaling
        )
        grad_value = jnp.einsum(
            "bhqk,bqhd->bkhd",
            attn_weights.astype(jnp.bfloat16),
            headed_g,
            preferred_element_type=jnp.float32,
        )
        return (
            grad_query,
            (
                grad_key.reshape(batch, block_size, width),
                grad_value.reshape(batch, block_size, width),
            ),
        )

    initial = jnp.zeros((batch, block_size, head_count, HDIM), jnp.float32)
    grad_query, key_terms = lax.scan(back_block, initial, jnp.arange(block_count, dtype=jnp.int32))
    return (grad_query.reshape(batch, block_size, width), key_terms)


def layer_forward(residual, params, cos_table, sin_table, position):
    norm_gain, norm_bias, w_query, w_key, w_value, w_out, w_up, b_up, w_down, b_down = params
    normed_low, unit_rows, inverse_std = normed_rows(residual, norm_gain, norm_bias)
    queries = rotate(project(normed_low, w_query), cos_table, sin_table).astype(jnp.bfloat16)
    key_rows = rotate(project(normed_low, w_key), cos_table, sin_table).astype(jnp.bfloat16)
    value_rows = project(normed_low, w_value).astype(jnp.bfloat16)
    context, log_total = attend_fold(queries, key_rows, value_rows, position)
    attn_branch = project(context.astype(jnp.bfloat16), w_out)
    preact = project(normed_low, w_up) + b_up
    hidden_low = gelu_tanh(preact).astype(jnp.bfloat16)
    branches = attn_branch + project(hidden_low, w_down)
    combined = lax.psum(branches, "tp")
    return (residual + combined + b_down, (context, log_total, None))


def layer_backward(residual, params, cos_table, sin_table, position, stashed, grad_out, grad_low):
    norm_gain, norm_bias, w_query, w_key, w_value, w_out, w_up, b_up, w_down, b_down = params
    context, log_total, gathered = stashed
    normed_low, unit_rows, inverse_std = normed_rows(residual, norm_gain, norm_bias)
    queries = rotate(project(normed_low, w_query), cos_table, sin_table).astype(jnp.bfloat16)
    key_rows = rotate(project(normed_low, w_key), cos_table, sin_table).astype(jnp.bfloat16)
    value_rows = project(normed_low, w_value).astype(jnp.bfloat16)
    key_all, value_all = (
        lax.all_gather(key_rows, "seq", axis=1, tiled=True),
        lax.all_gather(value_rows, "seq", axis=1, tiled=True),
    )
    grad_context = back_project(grad_low, w_out).astype(jnp.bfloat16)
    batch, block_size, width = queries.shape
    products = (grad_context.astype(jnp.float32) * context).reshape(
        batch, block_size, width // HDIM, HDIM
    )
    row_delta = jnp.transpose(jnp.sum(products, -1), (0, 2, 1))
    grad_query, key_terms = attend_back(
        queries, grad_context, log_total, row_delta, key_all, value_all, position
    )
    summed_keys, summed_values = (
        lax.psum_scatter(key_terms[0], "seq", scatter_dimension=0, tiled=True),
        lax.psum_scatter(key_terms[1], "seq", scatter_dimension=0, tiled=True),
    )
    own_keys = summed_keys[0]
    own_values = summed_values[0]
    grad_query_low = rotate(grad_query, cos_table, -sin_table).astype(jnp.bfloat16)
    grad_key_low = rotate(own_keys, cos_table, -sin_table).astype(jnp.bfloat16)
    grad_value_low = own_values.astype(jnp.bfloat16)
    preact = project(normed_low, w_up) + b_up
    hidden, gelu_pull = jax.vjp(gelu_tanh, preact)
    hidden_low = hidden.astype(jnp.bfloat16)
    grad_preact = gelu_pull(back_project(grad_low, w_down))[0]
    grad_preact_low = grad_preact.astype(jnp.bfloat16)
    partial_value = back_project(grad_query_low, w_query) + back_project(grad_key_low, w_key)
    partial_value = (
        partial_value + back_project(grad_value_low, w_value) + back_project(grad_preact_low, w_up)
    )
    grad_normed = lax.psum(partial_value, "tp")
    grad_unit = grad_normed * norm_gain
    centered_grad = grad_unit - jnp.mean(grad_unit, -1, keepdims=True)
    centered_grad = centered_grad - unit_rows * jnp.mean(grad_unit * unit_rows, -1, keepdims=True)
    grad_input = grad_out + inverse_std * centered_grad
    small = (token_sum(grad_normed * unit_rows), token_sum(grad_normed), token_sum(grad_out))
    gradients = (
        small[0],
        small[1],
        outer(normed_low, grad_query_low),
        outer(normed_low, grad_key_low),
        outer(normed_low, grad_value_low),
        outer(context.astype(jnp.bfloat16), grad_low),
        outer(normed_low, grad_preact_low),
        token_sum(grad_preact),
        outer(hidden_low, grad_low),
        small[2],
    )
    return (grad_input, gradients)


def general_body(
    inputs,
    norm_gain_one,
    norm_bias_one,
    query_one,
    key_one,
    value_one,
    output_one,
    up_one,
    up_bias_one,
    down_one,
    down_bias_one,
    norm_gain_two,
    norm_bias_two,
    query_two,
    key_two,
    value_two,
    output_two,
    up_two,
    up_bias_two,
    down_two,
    down_bias_two,
    cotangent,
):
    first_params = (
        norm_gain_one,
        norm_bias_one,
        query_one,
        key_one,
        value_one,
        output_one,
        up_one,
        up_bias_one,
        down_one,
        down_bias_one,
    )
    second_params = (
        norm_gain_two,
        norm_bias_two,
        query_two,
        key_two,
        value_two,
        output_two,
        up_two,
        up_bias_two,
        down_two,
        down_bias_two,
    )
    block_size = inputs.shape[1]
    position = lax.axis_index("seq") * block_size
    cos_table, sin_table = tables(position, block_size)
    start_rows = inputs.astype(jnp.float32)
    cot_rows = cotangent.astype(jnp.float32)
    middle, first_stash = layer_forward(start_rows, first_params, cos_table, sin_table, position)
    result, second_stash = layer_forward(middle, second_params, cos_table, sin_table, position)
    result_low = result.astype(jnp.bfloat16)
    middle_grad, second_grads = layer_backward(
        middle, second_params, cos_table, sin_table, position, second_stash, cot_rows, cotangent
    )
    middle_low = middle_grad.astype(jnp.bfloat16)
    start_grad, first_grads = layer_backward(
        start_rows,
        first_params,
        cos_table,
        sin_table,
        position,
        first_stash,
        middle_grad,
        middle_low,
    )
    start_low = start_grad.astype(jnp.bfloat16)
    everything = (
        lax.psum_scatter(first_grads[0], ("seq", "rows"), scatter_dimension=0, tiled=True),
        lax.psum_scatter(first_grads[1], ("seq", "rows"), scatter_dimension=0, tiled=True),
        lax.psum_scatter(first_grads[2], ("seq", "rows"), scatter_dimension=0, tiled=True),
        lax.psum_scatter(first_grads[3], ("seq", "rows"), scatter_dimension=0, tiled=True),
        lax.psum_scatter(first_grads[4], ("seq", "rows"), scatter_dimension=0, tiled=True),
        lax.psum_scatter(first_grads[5], ("seq", "rows"), scatter_dimension=1, tiled=True),
        lax.psum_scatter(first_grads[6], ("seq", "rows"), scatter_dimension=0, tiled=True),
        lax.psum_scatter(first_grads[7], ("seq", "rows"), scatter_dimension=0, tiled=True),
        lax.psum_scatter(first_grads[8], ("seq", "rows"), scatter_dimension=1, tiled=True),
        lax.psum_scatter(first_grads[9], ("seq", "rows"), scatter_dimension=0, tiled=True),
        lax.psum_scatter(second_grads[0], ("seq", "rows"), scatter_dimension=0, tiled=True),
        lax.psum_scatter(second_grads[1], ("seq", "rows"), scatter_dimension=0, tiled=True),
        lax.psum_scatter(second_grads[2], ("seq", "rows"), scatter_dimension=0, tiled=True),
        lax.psum_scatter(second_grads[3], ("seq", "rows"), scatter_dimension=0, tiled=True),
        lax.psum_scatter(second_grads[4], ("seq", "rows"), scatter_dimension=0, tiled=True),
        lax.psum_scatter(second_grads[5], ("seq", "rows"), scatter_dimension=1, tiled=True),
        lax.psum_scatter(second_grads[6], ("seq", "rows"), scatter_dimension=0, tiled=True),
        lax.psum_scatter(second_grads[7], ("seq", "rows"), scatter_dimension=0, tiled=True),
        lax.psum_scatter(second_grads[8], ("seq", "rows"), scatter_dimension=1, tiled=True),
        lax.psum_scatter(second_grads[9], ("seq", "rows"), scatter_dimension=0, tiled=True),
    )
    return (result_low, start_low) + tuple(everything)


BLOCKS = 4
SLOTS = 4
low_type = jnp.bfloat16
wide_type = jnp.float32
NT = (((1,), (1,)), ((), ()))
NN = (((1,), (0,)), ((), ()))
TN = (((0,), (0,)), ((), ()))
SCALARS = pl.BlockSpec(memory_space=pltpu.SMEM)
HERE = pl.BlockSpec(memory_space=pltpu.VMEM)
ANYWHERE = pl.BlockSpec(memory_space=pl.ANY)


def swap_x(v):
    return lax.ppermute(v, "tp", [(0, 1), (1, 0)])


def swap_c(v):
    return lax.ppermute(v, "rows", [(0, 1), (1, 0), (2, 3), (3, 2)])


def swap_y(v):
    return lax.ppermute(v, "rows", [(0, 2), (2, 0), (1, 3), (3, 1)])


def swap_z(v, k):
    return lax.ppermute(v, "seq", [(i, i ^ k) for i in range(4)])


def low(v):
    return v.astype(low_type)


def wide(v):
    return v.astype(wide_type)


def shape(kind, *dims):
    return jax.ShapeDtypeStruct(dims, kind)


def dot(a, b, dims=NN):
    return lax.dot_general(a, b, dims, preferred_element_type=wide_type)


def add(a, b):
    return b if a is None else a + b


def pick(v, index, axis=0):
    return lax.dynamic_index_in_dim(v, index, axis, keepdims=False)


def part(v, index, count, axis):
    size = v.shape[axis] // count
    return lax.dynamic_slice_in_dim(v, index * size, size, axis)


def in_order(first, a, b, axis):
    return jnp.where(first, jnp.concatenate([a, b], axis), jnp.concatenate([b, a], axis))


def xor_order(pieces, z):
    odd = (z & 1) == 1
    high = (z & 2) == 2
    a, b, c, d = pieces
    a, b, c, d = jnp.where(odd, b, a), jnp.where(odd, a, b), jnp.where(odd, d, c), jnp.where(odd, c, d)
    a, b, c, d = jnp.where(high, c, a), jnp.where(high, d, b), jnp.where(high, a, c), jnp.where(high, b, d)
    return jnp.stack([a, b, c, d])


class Chain:
    def __init__(self, scalars):
        self.scalars = scalars
        self.token = None
        self.weight = 1.1e9

    def __call__(self, name, kernel, args, outs, us=1, spec=HERE, limit=8):
        before = () if self.token is None else (self.token,)
        count = len(args)

        def with_token(*refs):
            outs_at = 1 + count + len(before)
            refs[outs_at][...] = jnp.zeros((8, 128), wide_type)
            kernel(*refs[: 1 + count], *refs[outs_at + 1 :])

        made = pl.pallas_call(
            with_token,
            in_specs=[SCALARS] + [spec] * count + [HERE] * len(before),
            out_specs=[HERE] * (1 + len(outs)),
            out_shape=[shape(wide_type, 8, 128), *outs],
            compiler_params=pltpu.CompilerParams(vmem_limit_bytes=limit * 2**20),
            cost_estimate=pl.CostEstimate(flops=int(us * self.weight), bytes_accessed=1000, transcendentals=0),
            name=name,
        )(self.scalars, *args, *before)
        self.token = made[0]
        return made[1:]


def across_part(local, x):
    rows, tokens, width = local.shape
    return part(local.reshape(rows, SLOTS, tokens // SLOTS, width), x, 2, 1)


def core_rows(kept, sent, c):
    return in_order(c == 0, kept, swap_c(sent), 0)


def own_tokens(whole, place):
    z = place[3]
    pieces = [pick(whole, z)] + [swap_z(pick(whole, z ^ k), k) for k in (1, 2, 3)]
    return xor_order(pieces, z).reshape(-1, whole.shape[2])


def rows_over_z(own, place):
    z = place[3]
    blocks = own.reshape(BLOCKS, own.shape[0] // BLOCKS, own.shape[1])
    pieces = [pick(blocks, z)] + [swap_z(pick(blocks, z ^ k), k) for k in (1, 2, 3)]
    return xor_order(pieces, z)


def place_kernel(scalars, own_ref, core_ref, across_ref, last_ref, out):
    owner = scalars[0]
    for i, ref in enumerate((own_ref, core_ref, across_ref, last_ref)):
        out[:, owner ^ i] = ref[...]


def local_rows(rows, place, run):
    x, c, y, z = place
    own = part(rows, c, 2, 0)
    across = swap_x(own)
    core = swap_c(part(rows, 1 - c, 2, 0))
    last = swap_x(core)

    def assemble():
        count, sub, width = own.shape
        (full,) = run("place", place_kernel, (own, core, across, last), (shape(rows.dtype, count, SLOTS, sub, width),))
        return full.reshape(count, SLOTS * sub, width)

    return assemble


def row_pieces(own):
    across = [swap_x(piece) for piece in own]
    return [list(own), across, [swap_c(piece) for piece in own], [swap_c(piece) for piece in across]]


def flat(pieces):
    return [piece for slot in pieces for piece in slot]


def stacked(refs):
    return refs[0][...] if len(refs) == 1 else jnp.concatenate([ref[...] for ref in refs], 0)


def slots_of(refs):
    count = len(refs) // SLOTS
    return [stacked(refs[i * count : (i + 1) * count]) for i in range(SLOTS)]


def put_pieces(refs, value):
    rows = refs[0].shape[0]
    for i, ref in enumerate(refs):
        ref[...] = value[i * rows : (i + 1) * rows]


PIECES = 2


def piece_shapes(kind, rows, width, count=PIECES):
    return [shape(kind, rows // count, width)] * count


def half(ref, axis, c):
    size = ref.shape[axis] // 2
    at = pl.ds(pl.multiple_of(c * size, size), size)
    return ref[at, :] if axis == 0 else ref[:, at]


def slot_places(owner, index, sub):
    slot = index // sub
    return (owner ^ (((slot & 1) << 1) | (slot >> 1))) * sub + (index - slot * sub)


def row_positions(owner, sub):
    index = jnp.arange(SLOTS * BLOCKS * sub, dtype=jnp.int32)
    slot = index // (BLOCKS * sub)
    block = (index // sub) % BLOCKS
    own_place = (owner ^ (((slot & 1) << 1) | (slot >> 1))) * sub
    return block * SLOTS * sub + own_place + index % sub


def lane_tables(positions):
    lane = jnp.arange(128, dtype=jnp.int32) % HDIM
    frequency = jnp.exp((lane // 2).astype(wide_type) * (-2.0 * math.log(10000.0) / ROT))
    angles = positions.astype(wide_type)[:, None] * frequency[None, :]
    turned = (lane < ROT)[None, :]
    even = (lane % 2 == 0)[None, :]
    sines = jnp.sin(angles)
    return (
        jnp.where(turned, jnp.cos(angles), 1.0),
        jnp.where(turned & even, -sines, 0.0),
        jnp.where(turned & ~even, sines, 0.0),
    )


def turn_lanes(v, cosines, to_even, to_odd):
    return v * cosines + pltpu.roll(v, 127, 1) * to_even + pltpu.roll(v, 1, 1) * to_odd


def take_block(ref, block, sub, group):
    starts = [(slot * BLOCKS + block) * sub for slot in range(SLOTS)]
    return jnp.concatenate([ref[at : at + sub, group * 128 : (group + 1) * 128] for at in starts], 0)


def put_block(ref, block, sub, group, value):
    for slot in range(SLOTS):
        at = (slot * BLOCKS + block) * sub
        ref[at : at + sub, group * 128 : (group + 1) * 128] = value[slot * sub : (slot + 1) * sub]


def block_allowed(owner, size, sub):
    key_place = slot_places(owner, lax.broadcasted_iota(jnp.int32, (size, size), 0), sub)
    query_place = slot_places(owner, lax.broadcasted_iota(jnp.int32, (size, size), 1), sub)
    return query_place >= key_place


def normed_of(residual, gain_ref, bias_ref):
    centered = residual - jnp.mean(residual, -1, keepdims=True)
    inverse_std = lax.rsqrt(jnp.mean(centered * centered, -1, keepdims=True) + epsilon)
    return low(centered * inverse_std * gain_ref[...] + bias_ref[...])


def first_kernel(scalars, own_ref, gain_ref, bias_ref, cot_ref, kept_out, sent_out, *normed_outs):
    put_pieces(normed_outs, normed_of(wide(own_ref[...]), gain_ref, bias_ref))
    kept_out[...] = cot_ref[:, scalars[1]]
    sent_out[...] = cot_ref[:, 1 - scalars[1]]


def first_norm(own, params, cot, run):
    args = (own, params[0][None], params[1][None], cot)
    half_cot = shape(cot.dtype, cot.shape[0], *cot.shape[2:])
    kept, sent, *normed = run("first_norm", first_kernel, args, [half_cot] * 2 + piece_shapes(low_type, *own.shape))
    return (normed, kept, sent)


def settle_kernel(count, scalars, kept_ref, *refs):
    residual_ref, shift_ref, gain_ref, bias_ref, middle_out = refs[count : count + 5]
    middle = wide(residual_ref[...]) + (kept_ref[...] + wide(stacked(refs[:count]))) + shift_ref[...]
    middle_out[...] = middle
    put_pieces(refs[count + 5 :], normed_of(middle, gain_ref, bias_ref))


def settle(kept, got, residual, shift, gain, bias, run):
    args = (kept, *got, residual, shift[None], gain[None], bias[None])
    outs = [shape(wide_type, *kept.shape)] + piece_shapes(low_type, *kept.shape)
    middle, *normed = run("settle", functools.partial(settle_kernel, len(got)), args, outs)
    return (middle, normed)


def result_kernel(count, scalars, kept_ref, *refs):
    residual_ref, shift_ref, out = refs[count:]
    out[...] = low(residual_ref[...] + (kept_ref[...] + wide(stacked(refs[:count]))) + shift_ref[...])


def final_result(kept, got, residual, shift, run):
    args = (kept, *got, residual, shift[None])
    return run("result", functools.partial(result_kernel, len(got)), args, (shape(low_type, *kept.shape),))[0]


def settle_back_kernel(count, scalars, kept_ref, *refs):
    grad_ref, residual_ref, gain_ref, grad_out, shared_out = refs[count : count + 5]
    grad_normed = kept_ref[...] + wide(stacked(refs[:count]))
    grad_own = wide(grad_ref[...])
    residual = wide(residual_ref[...])
    centered = residual - jnp.mean(residual, -1, keepdims=True)
    inverse_std = lax.rsqrt(jnp.mean(centered * centered, -1, keepdims=True) + epsilon)
    unit_rows = centered * inverse_std
    grad_unit = grad_normed * gain_ref[...]
    pulled = grad_unit - jnp.mean(grad_unit, -1, keepdims=True)
    pulled = pulled - unit_rows * jnp.mean(grad_unit * unit_rows, -1, keepdims=True)
    grad_input = grad_own + inverse_std * pulled
    grad_out[...] = grad_input
    put_pieces(refs[count + 5 :], low(grad_input))
    shared_out[0:1] = jnp.sum(grad_normed * unit_rows, 0, keepdims=True)
    shared_out[1:2] = jnp.sum(grad_normed, 0, keepdims=True)
    shared_out[2:3] = jnp.sum(grad_own, 0, keepdims=True)


def settle_back(kept, got, grad_own, residual, gain, run, count=PIECES):
    args = (kept, *got, grad_own, residual, gain[None])
    outs = [shape(wide_type, *kept.shape), shape(wide_type, 3, kept.shape[1])]
    kernel = functools.partial(settle_back_kernel, len(got))
    grad, shared, *lows = run("settle_back", kernel, args, outs + piece_shapes(low_type, *kept.shape, count))
    return (grad, lows, shared)


def gelu_and_slope(u):
    root = math.sqrt(2.0 / math.pi)
    square = u * u
    bend = jnp.tanh(root * u * (1.0 + 0.044715 * square))
    half = 0.5 * (1.0 + bend)
    slope = half + 0.5 * u * (1.0 - bend * bend) * (root * (1.0 + 3.0 * 0.044715 * square))
    return (u * half, slope)


def project_kernel(with_back, count, scalars, *refs):
    slots = slots_of(refs[:count])
    wq_ref, wk_ref, wv_ref, wu_ref, bu_ref, cos_ref, even_ref, odd_ref = refs[count : count + 8]
    refs = refs[count + 8 :]
    if with_back:
        back_ref, full_out, q_out, k_out, v_out, hidden_out, slope_out, sum_out = refs
    else:
        full_out, q_out, k_out, v_out, hidden_out, slope_out = refs
    c = scalars[1]
    tile = slots[0].shape[0]
    shift = half(bu_ref, 1, c)
    for i, rows in enumerate(slots):
        here = slice(i * tile, (i + 1) * tile)
        full_out[here] = rows
        turns = (cos_ref[here], even_ref[here], odd_ref[here])
        for w_ref, out in ((wq_ref, q_out), (wk_ref, k_out)):
            product = dot(rows, half(w_ref, 1, c))
            for at in range(0, product.shape[1], 128):
                out[here, at : at + 128] = low(turn_lanes(product[:, at : at + 128], *turns))
        v_out[here] = low(dot(rows, half(wv_ref, 1, c)))
        preact = dot(rows, half(wu_ref, 1, c)) + shift
        hidden, slope = gelu_and_slope(preact)
        hidden_out[here] = low(hidden)
        if with_back:
            grad = wide(back_ref[here]) * slope
            slope_out[here] = low(grad)
            column = jnp.sum(grad, 0, keepdims=True)
            sum_out[...] = column if i == 0 else sum_out[...] + column
        else:
            slope_out[here] = low(slope)


def project_row(pieces, params, turns, run, back=None):
    w_query, w_key, w_value, w_up, b_up = (params[i] for i in (2, 3, 4, 6, 7))
    pieces = flat(pieces)
    rows, width = sum(piece.shape[0] for piece in pieces), pieces[0].shape[1]
    heads, units = w_query.shape[1] // 2, w_up.shape[1] // 2
    outs = [shape(low_type, rows, width)] + [shape(low_type, rows, heads)] * 3 + [shape(low_type, rows, units)] * 2
    args = (*pieces, w_query, w_key, w_value, w_up, b_up[None], *turns)
    if back is not None:
        args += (back,)
        outs.append(shape(wide_type, 1, units))
    return run("project", functools.partial(project_kernel, back is not None, len(pieces)), args, outs, 7.5)


def attend_kernel(sub, scalars, q_ref, k_ref, v_ref, c_out, log_out):
    scaling = 1.0 / math.sqrt(HDIM)
    size = SLOTS * sub
    allowed = block_allowed(scalars[0], size, sub)
    lane = lax.broadcasted_iota(jnp.int32, (1, 128), 1)
    for group in range(q_ref.shape[1] // 128):
        queries = [take_block(q_ref, block, sub, group) for block in range(BLOCKS)]
        keys = [take_block(k_ref, block, sub, group) for block in range(BLOCKS)]
        values = [take_block(v_ref, block, sub, group).T for block in range(BLOCKS)]
        for j in range(BLOCKS):
            contexts = []
            for head in range(128 // HDIM):
                of_head = lane // HDIM == head
                query = jnp.where(of_head, queries[j], jnp.zeros_like(queries[j]))
                scores = [dot(keys[i], query, NT) for i in range(j + 1)]
                scores[j] = jnp.where(allowed, scores[j], negative)
                tops = [jnp.max(s, 0, keepdims=True) for s in scores]
                top = functools.reduce(jnp.maximum, tops)
                weights = [jnp.exp2((s - top) * (scaling * math.log2(math.e))) for s in scores]
                total = functools.reduce(jnp.add, [jnp.sum(w, 0, keepdims=True) for w in weights])
                context = None
                for i in range(j + 1):
                    rows = values[i][head * HDIM : (head + 1) * HDIM]
                    context = add(context, dot(rows, low(weights[i])))
                contexts.append(context * (1.0 / total))
                log_row = group * (128 // HDIM) + head
                log_out[log_row : log_row + 1, j * size : (j + 1) * size] = top * scaling + jnp.log(total)
            put_block(c_out, j, sub, group, low(jnp.concatenate(contexts, 0).T))


def attend(queries, keys, values, run):
    rows, width = queries.shape
    kernel = functools.partial(attend_kernel, rows // (BLOCKS * SLOTS))
    outs = (shape(low_type, rows, width), shape(wide_type, width // HDIM, rows))
    return run("attend", kernel, (queries, keys, values), outs, 7.5)


def attend_back_kernel(
    sub, scalars, q_ref, k_ref, v_ref, g_ref, log_ref, cos_ref, even_ref, odd_ref, dq_out, dk_out, dv_out
):
    scaling = 1.0 / math.sqrt(HDIM)
    size = SLOTS * sub
    allowed = block_allowed(scalars[0], size, sub)
    lane = lax.broadcasted_iota(jnp.int32, (1, 128), 1)
    turns = []
    for block in range(BLOCKS):
        cosines, to_even, to_odd = [take_block(ref, block, sub, 0) for ref in (cos_ref, even_ref, odd_ref)]
        turns.append((cosines, -to_even, -to_odd))
    for group in range(q_ref.shape[1] // 128):
        queries, keys, values, grads = [
            [take_block(ref, block, sub, group) for block in range(BLOCKS)] for ref in (q_ref, k_ref, v_ref, g_ref)
        ]
        flat_keys = [k.T for k in keys]
        grad_keys = [None] * BLOCKS
        grad_values = [None] * BLOCKS
        for j in range(BLOCKS):
            grad_query = []
            for head in range(128 // HDIM):
                of_head = lane // HDIM == head
                query = jnp.where(of_head, queries[j], jnp.zeros_like(queries[j]))
                grad = jnp.where(of_head, grads[j], jnp.zeros_like(grads[j]))
                log_row = group * (128 // HDIM) + head
                log_total = log_ref[log_row : log_row + 1, j * size : (j + 1) * size] * math.log2(math.e)
                probs, grad_probs, delta = [], [], None
                for i in range(j + 1):
                    weights = jnp.exp2(dot(keys[i], query, NT) * (scaling * math.log2(math.e)) - log_total)
                    if i == j:
                        weights = jnp.where(allowed, weights, 0.0)
                    back = dot(values[i], grad, NT)
                    delta = add(delta, jnp.sum(weights * back, 0, keepdims=True))
                    probs.append(weights)
                    grad_probs.append(back)
                flat = None
                for i in range(j + 1):
                    grad_scores = low(probs[i] * (grad_probs[i] - delta))
                    grad_values[i] = add(grad_values[i], dot(low(probs[i]), grad))
                    grad_keys[i] = add(grad_keys[i], dot(grad_scores, query))
                    flat = add(flat, dot(flat_keys[i][head * HDIM : (head + 1) * HDIM], grad_scores))
                grad_query.append(flat)
            turned = jnp.concatenate(grad_query, 0).T * scaling
            put_block(dq_out, j, sub, group, low(turn_lanes(turned, *turns[j])))
        for i in range(BLOCKS):
            put_block(dk_out, i, sub, group, low(turn_lanes(grad_keys[i] * scaling, *turns[i])))
            put_block(dv_out, i, sub, group, low(grad_values[i]))


def attend_back_call(queries, keys, values, grad_context, logs, turns, run):
    rows, width = queries.shape
    kernel = functools.partial(attend_back_kernel, rows // (BLOCKS * SLOTS))
    args = (queries, keys, values, grad_context, logs, *turns)
    return run("attend_back", kernel, args, [shape(low_type, rows, width)] * 3, 0, limit=16)


def products(terms, weights, axis, c, start, stop):
    total = None
    for a_ref, w_ref in zip(terms, weights, strict=True):
        total = add(total, dot(a_ref[start:stop], half(w_ref, axis, c), NT if axis else NN))
    return total


def sent_kernel(axis, count, scalars, *refs):
    rows = refs[0].shape[0]
    put_pieces(refs[2 * count :], low(products(refs[:count], refs[count : 2 * count], axis, scalars[1], rows // 2, rows)))


def kept_kernel(axis, count, pieces, scalars, *refs):
    rows = refs[0].shape[0]
    tile = rows // SLOTS
    got_refs, (kept_out, *sent_outs) = refs[2 * count : 2 * count + pieces], refs[2 * count + pieces :]
    total = products(refs[:count], refs[count : 2 * count], axis, scalars[1], 0, rows // 2)
    put_pieces(sent_outs, low(total[tile:] + wide(stacked(got_refs[pieces // 2 :]))))
    kept_out[...] = total[:tile] + wide(stacked(got_refs[: pieces // 2]))


def send_part(terms, weights, axis, run):
    rows, width = terms[0].shape[0], weights[0].shape[1 - axis]
    kernel = functools.partial(sent_kernel, axis, len(terms))
    outs = piece_shapes(low_type, rows // 2, width, 2 * PIECES)
    return [swap_c(sent) for sent in run("sent", kernel, (*terms, *weights), outs, 2.5)]


def keep_part(terms, weights, axis, got, run, count=1):
    rows, width = terms[0].shape[0] // SLOTS, weights[0].shape[1 - axis]
    kernel = functools.partial(kept_kernel, axis, len(terms), len(got))
    outs = [shape(wide_type, rows, width)] + piece_shapes(low_type, rows, width, count)
    kept, *sent = run("kept", kernel, (*terms, *weights, *got), outs, 2.5)
    return (kept, [swap_x(piece) for piece in sent])


def raw_back_kernel(count, scalars, *refs):
    slots = slots_of(refs[:count])
    wo_ref, wd_ref, full_out, context_out, raw_out = refs[count:]
    tile = slots[0].shape[0]
    for i, rows in enumerate(slots):
        here = slice(i * tile, (i + 1) * tile)
        full_out[here] = rows
        context_out[here] = low(dot(rows, half(wo_ref, 0, scalars[1]), NT))
        raw_out[here] = low(dot(rows, half(wd_ref, 0, scalars[1]), NT))


def raw_back(pieces, params, run):
    w_out, w_down = params[5], params[8]
    pieces = flat(pieces)
    rows, width = sum(piece.shape[0] for piece in pieces), pieces[0].shape[1]
    outs = [shape(low_type, rows, n) for n in (width, w_out.shape[0] // 2, w_down.shape[0] // 2)]
    return run("raw_back", functools.partial(raw_back_kernel, len(pieces)), (*pieces, w_out, w_down), outs, 3.5)


def slopes_kernel(count, scalars, *refs):
    slots = slots_of(refs[:count])
    wo_ref, wd_ref, slope_ref, full_out, context_out, hidden_out, sum_out = refs[count:]
    tile = slots[0].shape[0]
    for i, rows in enumerate(slots):
        here = slice(i * tile, (i + 1) * tile)
        full_out[here] = rows
        context_out[here] = low(dot(rows, half(wo_ref, 0, scalars[1]), NT))
        grad = dot(rows, half(wd_ref, 0, scalars[1]), NT) * wide(slope_ref[here])
        hidden_out[here] = low(grad)
        column = jnp.sum(grad, 0, keepdims=True)
        sum_out[...] = column if i == 0 else sum_out[...] + column


def slopes(pieces, params, slope, run):
    w_out, w_down = params[5], params[8]
    pieces = flat(pieces)
    rows, width = sum(piece.shape[0] for piece in pieces), pieces[0].shape[1]
    units = w_down.shape[0] // 2
    outs = [shape(low_type, rows, n) for n in (width, w_out.shape[0] // 2, units)] + [shape(wide_type, 1, units)]
    return run("slopes", functools.partial(slopes_kernel, len(pieces)), (*pieces, w_out, w_down, slope), outs, 3.5)


def outer_kernel(counts, scalars, *refs):
    c, y, z = scalars[1], scalars[2], scalars[3]
    kept_out, sent_out = refs[-2:]
    at = 0
    refs = list(refs[:-2])
    for count in counts:
        left_ref = refs.pop(0)
        rights = [refs.pop(0) for _ in range(count)]
        tile = left_ref.shape[1] // 4
        piece = tile // 4
        total = sum(right.shape[1] for right in rights)
        for i in range(4):
            block = ((i >> 1) ^ (z & 1)) + 2 * ((i & 1) ^ (z >> 1))
            left = left_ref[:, pl.ds(pl.multiple_of(block * tile, tile), tile)]
            start = at
            for right_ref in rights:
                columns = slice(start, start + right_ref.shape[1])
                value = low(dot(left, right_ref[...], TN))
                a, b, d, e = [value[k * piece : (k + 1) * piece] for k in range(4)]
                a, b = jnp.where(c == 0, a, b), jnp.where(c == 0, b, a)
                d, e = jnp.where(c == 0, d, e), jnp.where(c == 0, e, d)
                for k, (upper, lower) in enumerate(((a, d), (b, e))):
                    rows = slice((2 * i + k) * piece, (2 * i + k + 1) * piece)
                    kept_out[rows, columns] = jnp.where(y == 0, upper, lower)
                    sent_out[rows, columns] = jnp.where(y == 0, lower, upper)
                start += right_ref.shape[1]
        at += total


class Reduction:
    hops = (swap_y, lambda v: swap_z(v, 1), lambda v: swap_z(v, 2), swap_c)

    def __init__(self, pairs, run):
        self.run = run
        self.at = 0
        total = sum(right.shape[1] for _, rights in pairs for right in rights)
        out = shape(low_type, pairs[0][0].shape[1] // 2, total)
        kernel = functools.partial(outer_kernel, [len(rights) for _, rights in pairs])
        args = [v for left, rights in pairs for v in (left, *rights)]
        self.kept, sent = run("outer", kernel, args, (out, out), 3 * total / 1024)
        self.got = self.hops[0](sent)

    def hop(self):
        out = shape(low_type, self.kept.shape[0] // 2, self.kept.shape[1])
        self.kept, sent = self.run("fold", fold_kernel, (self.kept, self.got), (out, out), 6)
        self.at += 1
        self.got = self.hops[self.at](sent)

    def finish(self, cuts, outs):
        kernel = functools.partial(finish_kernel, cuts)
        return self.run("finish", kernel, (self.kept, self.got), [shape(wide_type, *dims) for dims in outs])


def finish_kernel(cuts, scalars, kept_ref, got_ref, *outs):
    first = scalars[1] == 0
    start = 0
    for stop, out in zip(cuts, outs, strict=True):
        own, other = wide(kept_ref[:, start:stop]), wide(got_ref[:, start:stop])
        rows = own.shape[0]
        if out.shape[0] == rows and out.shape[1] == own.shape[1]:
            out[...] = own + other
        else:
            both = jnp.concatenate([jnp.where(first, own, other), jnp.where(first, other, own)], 1)
            out[...] = both
        start = stop


def fold_kernel(scalars, kept_ref, got_ref, kept_out, sent_out):
    half = kept_out.shape[0]
    kept_out[...] = low(wide(kept_ref[:half]) + wide(got_ref[:half]))
    sent_out[...] = low(wide(kept_ref[half:]) + wide(got_ref[half:]))


def small_kernel(scalars, shared_ref, *refs):
    out = refs[-1]
    first = scalars[1] == 0
    rows = [shared_ref[...]]
    for ref in refs[:-1]:
        sums = ref[...]
        for start in (0, 64):
            cuts = [sums[:, at + start : at + start + 64] for at in range(0, sums.shape[1], 128)]
            mine = jnp.concatenate(cuts, 1)
            none = jnp.zeros_like(mine)
            rows.append(jnp.where(first, jnp.concatenate([mine, none], 1), jnp.concatenate([none, mine], 1)))
    used = sum(row.shape[0] for row in rows)
    rows.append(jnp.zeros((out.shape[0] - used, out.shape[1]), wide_type))
    out[...] = low(jnp.concatenate(rows, 0))


def small_rows(shared, hidden_sums, run):
    return run("small", small_kernel, (shared, *hidden_sums), (shape(low_type, 16, shared.shape[1]),))[0]


def wait_kernel(scalars, *refs):
    pass


def split_kernel(scalars, ref, *outs):
    put_pieces(outs, ref[...])


def in_pieces(v, run):
    return run("split", split_kernel, (v,), piece_shapes(v.dtype, *v.shape))


def hold(run, *arrays):
    run("wait", wait_kernel, arrays, (), 0.5, ANYWHERE)


def quad_body(inputs, *rest):
    cotangent = rest[-1]
    r = lax.axis_index("rows")
    place = (lax.axis_index("tp"), r % 2, r // 2, lax.axis_index("seq"))
    x, c, y, z = place
    owner = 2 * x + c
    sub = inputs.shape[1] // SLOTS
    run = Chain(jnp.stack([owner, c, y, z, x]).astype(jnp.int32))
    one, two = rest[:10], rest[10:20]

    mine = across_part(inputs, x)
    start = own_tokens(core_rows(pick(mine, c, 1), pick(mine, 1 - c, 1), c), place)
    turns = lane_tables(row_positions(owner, sub))
    normed, cot_kept, cot_sent = first_norm(start, one, across_part(cotangent, x), run)
    pieces = row_pieces(normed)
    cot_own = own_tokens(core_rows(cot_kept, cot_sent, c), place)
    full_one, q1, k1, v1, hidden_one, slope_one = project_row(pieces, one, turns, run)
    cot_parts = in_pieces(cot_own, run)
    context_one, logs_one = attend(q1, k1, v1, run)
    cot_pieces = row_pieces(cot_parts)
    branch = ((context_one, hidden_one), (one[5], one[8]), 0)
    got = send_part(*branch, run)
    hold(run, *flat(cot_pieces))
    kept, got = keep_part(*branch, got, run)
    cot_full, grad_context, raw = raw_back(cot_pieces, two, run)
    middle, normed = settle(kept, got, start, one[9], two[0], two[1], run)

    full_two, q2, k2, v2, hidden_two, grad_hidden, sums_two = project_row(row_pieces(normed), two, turns, run, raw)
    run.weight = 0.28e9
    units_two = Reduction([(cot_full, (hidden_two,)), (full_two, (grad_hidden,))], run)
    context_two, logs_two = attend(q2, k2, v2, run)
    grads = attend_back_call(q2, k2, v2, grad_context, logs_two, turns, run)
    back = ((*grads, grad_hidden), (*two[2:5], two[6]), 1)
    got = send_part(*back, run)
    heads_two = Reduction([(cot_full, (context_two,)), (full_two, grads)], run)
    kept, got = keep_part(*back, got, run)
    branch = ((context_two, hidden_two), (two[5], two[8]), 0)
    res_got = send_part(*branch, run)
    width, units = q1.shape[1], hidden_one.shape[1]
    head_cut = [width, 2 * width, 3 * width, 4 * width]
    head_dims = (sub, 2 * width)
    grad_middle, grad_low, shared_two = settle_back(kept, got, cot_own, middle, two[0], run)
    pieces = row_pieces(grad_low)
    res_kept, res_got = keep_part(*branch, res_got, run)
    units_two.hop()
    grad_full, grad_context, grad_hidden, sums_one = slopes(pieces, one, slope_one, run)
    heads_two.hop()
    units_one = Reduction([(grad_full, (hidden_one,)), (full_one, (grad_hidden,))], run)
    result = final_result(res_kept, res_got, middle, two[9], run)
    out_rows = rows_over_z(result, place)
    outputs = local_rows(out_rows, place, run)
    grads = attend_back_call(q1, k1, v1, grad_context, logs_one, turns, run)
    back = ((*grads, grad_hidden), (*one[2:5], one[6]), 1)
    got = send_part(*back, run)
    hold(run, out_rows)
    units_two.hop()
    kept, got = keep_part(*back, got, run)
    heads_one = Reduction([(grad_full, (context_one,)), (full_one, grads)], run)
    heads_two.hop()
    grad_start, start_low, shared_one = settle_back(kept, got, grad_middle, start, one[0], run, 1)
    in_rows = rows_over_z(start_low[0], place)
    shared = jnp.concatenate([shared_one, shared_two], 0)
    shared = shared + swap_x(shared)
    input_grad = local_rows(in_rows, place, run)
    units_one.hop()
    small = small_rows(shared, [sums_one, sums_two], run)
    units_two.hop()
    heads_two.hop()
    last = Reduction([(small, (jnp.eye(16, 128, dtype=low_type),))], run)
    wd_two, wu_two = units_two.finish([units, 2 * units], [(sub, 2 * units)] * 2)
    hold(run, in_rows)
    wo_two, wq_two, wk_two, wv_two = heads_two.finish(head_cut, [head_dims] * 4)
    outputs = outputs()
    heads_one.hop()
    units_one.hop()
    last.hop()
    input_grad = input_grad()
    heads_one.hop()
    last.hop()
    units_one.hop()
    heads_one.hop()
    last.hop()
    wo_one, wq_one, wk_one, wv_one = heads_one.finish(head_cut, [head_dims] * 4)
    (tail,) = last.finish([128], [(sub, 128)])
    wd_one, wu_one = units_one.finish([units, 2 * units], [(sub, 2 * units)] * 2)
    columns = tail.T
    hidden_one, hidden_two = (columns[i : i + 2].reshape(-1) for i in (6, 8))
    return (
        outputs, input_grad,
        columns[0], columns[1], wq_one, wk_one, wv_one, wo_one.T, wu_one, hidden_one, wd_one.T, columns[2],
        columns[3], columns[4], wq_two, wk_two, wv_two, wo_two.T, wu_two, hidden_two, wd_two.T, columns[5],
    )


def solution(mesh):
    in_specs = (
        P("rows", "seq", None),
        P(),
        P(),
        P(None, "tp"),
        P(None, "tp"),
        P(None, "tp"),
        P("tp", None),
        P(None, "tp"),
        P("tp"),
        P("tp", None),
        P(),
        P(),
        P(),
        P(None, "tp"),
        P(None, "tp"),
        P(None, "tp"),
        P("tp", None),
        P(None, "tp"),
        P("tp"),
        P("tp", None),
        P(),
        P("rows", "seq", None),
    )
    out_specs = (
        P("rows", "seq", None),
        P("rows", "seq", None),
        P(("seq", "rows")),
        P(("seq", "rows")),
        P(("seq", "rows"), "tp"),
        P(("seq", "rows"), "tp"),
        P(("seq", "rows"), "tp"),
        P("tp", ("seq", "rows")),
        P(("seq", "rows"), "tp"),
        P(("tp", "seq", "rows")),
        P("tp", ("seq", "rows")),
        P(("seq", "rows")),
        P(("seq", "rows")),
        P(("seq", "rows")),
        P(("seq", "rows"), "tp"),
        P(("seq", "rows"), "tp"),
        P(("seq", "rows"), "tp"),
        P("tp", ("seq", "rows")),
        P(("seq", "rows"), "tp"),
        P(("tp", "seq", "rows")),
        P("tp", ("seq", "rows")),
        P(("seq", "rows")),
    )
    fits = (mesh.shape["seq"], mesh.shape["tp"], mesh.shape["rows"]) == (4, 2, 4)
    body = quad_body if fits else general_body
    return jax.shard_map(body, mesh=mesh, in_specs=in_specs, out_specs=out_specs, check_vma=False)
```

```python
import functools
import math

import jax
import jax.numpy as jnp
from jax import lax
from jax.experimental import pallas as pl
from jax.experimental.pallas import tpu as pltpu
from jax.sharding import PartitionSpec as P

HDIM = 64
ROT = 32


epsilon = 1e-05
negative = -1e30


def tables(position, length):
    positions = (position + jnp.arange(length, dtype=jnp.int32)).astype(jnp.float32)
    ladder = jnp.arange(ROT // 2, dtype=jnp.float32)
    frequency = jnp.exp(ladder * (-2.0 * math.log(10000.0) / ROT))
    angles = positions[:, None] * frequency[None, :]
    return (jnp.cos(angles), jnp.sin(angles))


def rotate(flat_rows, cos_table, sin_table):
    old_shape = flat_rows.shape
    headed = flat_rows.reshape(old_shape[:-1] + (old_shape[-1] // HDIM, HDIM))
    turned = headed[..., :ROT].reshape(headed.shape[:-1] + (ROT // 2, 2))
    even_part = turned[..., 0]
    odd_part = turned[..., 1]
    cos_wide = cos_table[:, None, :]
    sin_wide = sin_table[:, None, :]
    new_even = even_part * cos_wide - odd_part * sin_wide
    new_odd = odd_part * cos_wide + even_part * sin_wide
    joined = jnp.stack([new_even, new_odd], -1).reshape(headed.shape[:-1] + (ROT,))
    return jnp.concatenate([joined, headed[..., ROT:]], -1).reshape(old_shape)


def normalize(residual, gain, bias):
    centered = residual - jnp.mean(residual, -1, keepdims=True)
    inverse_std = lax.rsqrt(jnp.mean(centered * centered, -1, keepdims=True) + epsilon)
    unit_rows = centered * inverse_std
    return (unit_rows * gain + bias, unit_rows, inverse_std)


def normed_rows(residual, gain, bias):
    normed, unit_rows, inverse_std = normalize(residual, gain, bias)
    normed_low = normed.astype(jnp.bfloat16)
    return (normed_low, unit_rows, inverse_std)


def project(operand, weight):
    return jnp.dot(operand, weight, preferred_element_type=jnp.float32)


def back_project(operand, weight):
    return lax.dot_general(
        operand, weight, (((2,), (1,)), ((), ())), preferred_element_type=jnp.float32
    )


def outer(left_rows, right_rows):
    return lax.dot_general(
        left_rows, right_rows, (((0, 1), (0, 1)), ((), ())), preferred_element_type=jnp.float32
    )


def token_sum(operand):
    return jnp.sum(operand, axis=(0, 1))


def gelu_tanh(argument):
    return jax.nn.gelu(argument, approximate=True)


def headed_view(flat_rows):
    return flat_rows.reshape(flat_rows.shape[:-1] + (flat_rows.shape[-1] // HDIM, HDIM))


def allowed_mask(position, query_count, key_start, key_count):
    query_places = position + jnp.arange(query_count, dtype=jnp.int32)
    key_places = key_start + jnp.arange(key_count, dtype=jnp.int32)
    return query_places[:, None] >= key_places[None, :]


def block_scores(queries, key_rows, position, key_start):
    scaling = 1.0 / math.sqrt(HDIM)
    scores = (
        jnp.einsum(
            "bqhd,bkhd->bhqk",
            headed_view(queries),
            headed_view(key_rows),
            preferred_element_type=jnp.float32,
        )
        * scaling
    )
    allowed = allowed_mask(position, queries.shape[1], key_start, key_rows.shape[1])
    return (jnp.where(allowed, scores, negative), allowed)


def start_stats(queries):
    batch, query_count, width = queries.shape
    head_count = width // HDIM
    highest = jnp.full((batch, head_count, query_count), negative, jnp.float32)
    summed = jnp.zeros((batch, head_count, query_count), jnp.float32)
    return (highest, summed)


def start_values(queries):
    batch, query_count, width = queries.shape
    return jnp.zeros((batch, query_count, width // HDIM, HDIM), jnp.float32)


def stats_block(running, pieces, key_start, queries, position):
    highest, summed = running
    masked, allowed = block_scores(queries, pieces[0], position, key_start)
    new_high = jnp.maximum(highest, jnp.max(masked, -1))
    expo = jnp.where(allowed, jnp.exp(masked - new_high[..., None]), 0.0)
    summed = jnp.sum(expo, -1)
    return (new_high, summed)


def value_block(pieces, key_start, queries, position, log_total):
    masked, allowed = block_scores(queries, pieces[0], position, key_start)
    attn_low = jnp.where(allowed, jnp.exp(masked - log_total[..., None]), 0.0).astype(jnp.bfloat16)
    return jnp.einsum(
        "bhqk,bkhd->bqhd", attn_low, headed_view(pieces[1]), preferred_element_type=jnp.float32
    )


def fold_history(key_rows, value_rows, fold_fn, initial):
    return fold_fn(
        initial,
        (
            lax.all_gather(key_rows, "seq", axis=1, tiled=True),
            lax.all_gather(value_rows, "seq", axis=1, tiled=True),
        ),
        jnp.int32(0),
    )


def attend_fold(queries, key_rows, value_rows, position):

    def stats_piece(running, pieces, key_start):
        return stats_block(running, pieces, key_start, queries, position)

    highest, summed = fold_history(key_rows, value_rows, stats_piece, start_stats(queries))
    log_total = highest + jnp.log(summed)

    def value_piece(accumulated, pieces, key_start):
        return value_block(pieces, key_start, queries, position, log_total)

    accumulated = fold_history(key_rows, value_rows, value_piece, start_values(queries))
    return (accumulated.reshape(queries.shape), log_total)


def attend_back(queries, grad_context, log_total, row_delta, key_all, value_all, position):
    batch, block_size, width = queries.shape
    head_count = width // HDIM
    block_count = key_all.shape[1] // block_size
    scaling = 1.0 / math.sqrt(HDIM)
    headed_q = headed_view(queries)
    headed_g = headed_view(grad_context)

    def back_block(grad_query, block_index):
        offset = block_index * block_size
        key_rows = headed_view(lax.dynamic_slice_in_dim(key_all, offset, block_size, 1))
        value_rows = headed_view(lax.dynamic_slice_in_dim(value_all, offset, block_size, 1))
        scores = (
            jnp.einsum("bqhd,bkhd->bhqk", headed_q, key_rows, preferred_element_type=jnp.float32)
            * scaling
        )
        allowed = allowed_mask(position, block_size, offset, block_size)
        masked = jnp.where(allowed, scores, negative)
        attn_weights = jnp.where(allowed, jnp.exp(masked - log_total[..., None]), 0.0)
        grad_weights = jnp.einsum(
            "bqhd,bkhd->bhqk", headed_g, value_rows, preferred_element_type=jnp.float32
        )
        grad_score = (attn_weights * (grad_weights - row_delta[..., None])).astype(jnp.bfloat16)
        grad_query = (
            grad_query
            + jnp.einsum(
                "bhqk,bkhd->bqhd", grad_score, key_rows, preferred_element_type=jnp.float32
            )
            * scaling
        )
        grad_key = (
            jnp.einsum("bhqk,bqhd->bkhd", grad_score, headed_q, preferred_element_type=jnp.float32)
            * scaling
        )
        grad_value = jnp.einsum(
            "bhqk,bqhd->bkhd",
            attn_weights.astype(jnp.bfloat16),
            headed_g,
            preferred_element_type=jnp.float32,
        )
        return (
            grad_query,
            (
                grad_key.reshape(batch, block_size, width),
                grad_value.reshape(batch, block_size, width),
            ),
        )

    initial = jnp.zeros((batch, block_size, head_count, HDIM), jnp.float32)
    grad_query, key_terms = lax.scan(back_block, initial, jnp.arange(block_count, dtype=jnp.int32))
    return (grad_query.reshape(batch, block_size, width), key_terms)


def layer_forward(residual, params, cos_table, sin_table, position):
    norm_gain, norm_bias, w_query, w_key, w_value, w_out, w_up, b_up, w_down, b_down = params
    normed_low, unit_rows, inverse_std = normed_rows(residual, norm_gain, norm_bias)
    queries = rotate(project(normed_low, w_query), cos_table, sin_table).astype(jnp.bfloat16)
    key_rows = rotate(project(normed_low, w_key), cos_table, sin_table).astype(jnp.bfloat16)
    value_rows = project(normed_low, w_value).astype(jnp.bfloat16)
    context, log_total = attend_fold(queries, key_rows, value_rows, position)
    attn_branch = project(context.astype(jnp.bfloat16), w_out)
    preact = project(normed_low, w_up) + b_up
    hidden_low = gelu_tanh(preact).astype(jnp.bfloat16)
    branches = attn_branch + project(hidden_low, w_down)
    combined = lax.psum(branches, "tp")
    return (residual + combined + b_down, (context, log_total, None))


def layer_backward(residual, params, cos_table, sin_table, position, stashed, grad_out, grad_low):
    norm_gain, norm_bias, w_query, w_key, w_value, w_out, w_up, b_up, w_down, b_down = params
    context, log_total, gathered = stashed
    normed_low, unit_rows, inverse_std = normed_rows(residual, norm_gain, norm_bias)
    queries = rotate(project(normed_low, w_query), cos_table, sin_table).astype(jnp.bfloat16)
    key_rows = rotate(project(normed_low, w_key), cos_table, sin_table).astype(jnp.bfloat16)
    value_rows = project(normed_low, w_value).astype(jnp.bfloat16)
    key_all, value_all = (
        lax.all_gather(key_rows, "seq", axis=1, tiled=True),
        lax.all_gather(value_rows, "seq", axis=1, tiled=True),
    )
    grad_context = back_project(grad_low, w_out).astype(jnp.bfloat16)
    batch, block_size, width = queries.shape
    products = (grad_context.astype(jnp.float32) * context).reshape(
        batch, block_size, width // HDIM, HDIM
    )
    row_delta = jnp.transpose(jnp.sum(products, -1), (0, 2, 1))
    grad_query, key_terms = attend_back(
        queries, grad_context, log_total, row_delta, key_all, value_all, position
    )
    summed_keys, summed_values = (
        lax.psum_scatter(key_terms[0], "seq", scatter_dimension=0, tiled=True),
        lax.psum_scatter(key_terms[1], "seq", scatter_dimension=0, tiled=True),
    )
    own_keys = summed_keys[0]
    own_values = summed_values[0]
    grad_query_low = rotate(grad_query, cos_table, -sin_table).astype(jnp.bfloat16)
    grad_key_low = rotate(own_keys, cos_table, -sin_table).astype(jnp.bfloat16)
    grad_value_low = own_values.astype(jnp.bfloat16)
    preact = project(normed_low, w_up) + b_up
    hidden, gelu_pull = jax.vjp(gelu_tanh, preact)
    hidden_low = hidden.astype(jnp.bfloat16)
    grad_preact = gelu_pull(back_project(grad_low, w_down))[0]
    grad_preact_low = grad_preact.astype(jnp.bfloat16)
    partial_value = back_project(grad_query_low, w_query) + back_project(grad_key_low, w_key)
    partial_value = (
        partial_value + back_project(grad_value_low, w_value) + back_project(grad_preact_low, w_up)
    )
    grad_normed = lax.psum(partial_value, "tp")
    grad_unit = grad_normed * norm_gain
    centered_grad = grad_unit - jnp.mean(grad_unit, -1, keepdims=True)
    centered_grad = centered_grad - unit_rows * jnp.mean(grad_unit * unit_rows, -1, keepdims=True)
    grad_input = grad_out + inverse_std * centered_grad
    small = (token_sum(grad_normed * unit_rows), token_sum(grad_normed), token_sum(grad_out))
    gradients = (
        small[0],
        small[1],
        outer(normed_low, grad_query_low),
        outer(normed_low, grad_key_low),
        outer(normed_low, grad_value_low),
        outer(context.astype(jnp.bfloat16), grad_low),
        outer(normed_low, grad_preact_low),
        token_sum(grad_preact),
        outer(hidden_low, grad_low),
        small[2],
    )
    return (grad_input, gradients)


def general_body(
    inputs,
    norm_gain_one,
    norm_bias_one,
    query_one,
    key_one,
    value_one,
    output_one,
    up_one,
    up_bias_one,
    down_one,
    down_bias_one,
    norm_gain_two,
    norm_bias_two,
    query_two,
    key_two,
    value_two,
    output_two,
    up_two,
    up_bias_two,
    down_two,
    down_bias_two,
    cotangent,
):
    first_params = (
        norm_gain_one,
        norm_bias_one,
        query_one,
        key_one,
        value_one,
        output_one,
        up_one,
        up_bias_one,
        down_one,
        down_bias_one,
    )
    second_params = (
        norm_gain_two,
        norm_bias_two,
        query_two,
        key_two,
        value_two,
        output_two,
        up_two,
        up_bias_two,
        down_two,
        down_bias_two,
    )
    block_size = inputs.shape[1]
    position = lax.axis_index("seq") * block_size
    cos_table, sin_table = tables(position, block_size)
    start_rows = inputs.astype(jnp.float32)
    cot_rows = cotangent.astype(jnp.float32)
    middle, first_stash = layer_forward(start_rows, first_params, cos_table, sin_table, position)
    result, second_stash = layer_forward(middle, second_params, cos_table, sin_table, position)
    result_low = result.astype(jnp.bfloat16)
    middle_grad, second_grads = layer_backward(
        middle, second_params, cos_table, sin_table, position, second_stash, cot_rows, cotangent
    )
    middle_low = middle_grad.astype(jnp.bfloat16)
    start_grad, first_grads = layer_backward(
        start_rows,
        first_params,
        cos_table,
        sin_table,
        position,
        first_stash,
        middle_grad,
        middle_low,
    )
    start_low = start_grad.astype(jnp.bfloat16)
    everything = (
        lax.psum_scatter(first_grads[0], ("seq", "rows"), scatter_dimension=0, tiled=True),
        lax.psum_scatter(first_grads[1], ("seq", "rows"), scatter_dimension=0, tiled=True),
        lax.psum_scatter(first_grads[2], ("seq", "rows"), scatter_dimension=0, tiled=True),
        lax.psum_scatter(first_grads[3], ("seq", "rows"), scatter_dimension=0, tiled=True),
        lax.psum_scatter(first_grads[4], ("seq", "rows"), scatter_dimension=0, tiled=True),
        lax.psum_scatter(first_grads[5], ("seq", "rows"), scatter_dimension=1, tiled=True),
        lax.psum_scatter(first_grads[6], ("seq", "rows"), scatter_dimension=0, tiled=True),
        lax.psum_scatter(first_grads[7], ("seq", "rows"), scatter_dimension=0, tiled=True),
        lax.psum_scatter(first_grads[8], ("seq", "rows"), scatter_dimension=1, tiled=True),
        lax.psum_scatter(first_grads[9], ("seq", "rows"), scatter_dimension=0, tiled=True),
        lax.psum_scatter(second_grads[0], ("seq", "rows"), scatter_dimension=0, tiled=True),
        lax.psum_scatter(second_grads[1], ("seq", "rows"), scatter_dimension=0, tiled=True),
        lax.psum_scatter(second_grads[2], ("seq", "rows"), scatter_dimension=0, tiled=True),
        lax.psum_scatter(second_grads[3], ("seq", "rows"), scatter_dimension=0, tiled=True),
        lax.psum_scatter(second_grads[4], ("seq", "rows"), scatter_dimension=0, tiled=True),
        lax.psum_scatter(second_grads[5], ("seq", "rows"), scatter_dimension=1, tiled=True),
        lax.psum_scatter(second_grads[6], ("seq", "rows"), scatter_dimension=0, tiled=True),
        lax.psum_scatter(second_grads[7], ("seq", "rows"), scatter_dimension=0, tiled=True),
        lax.psum_scatter(second_grads[8], ("seq", "rows"), scatter_dimension=1, tiled=True),
        lax.psum_scatter(second_grads[9], ("seq", "rows"), scatter_dimension=0, tiled=True),
    )
    return (result_low, start_low) + tuple(everything)


BLOCKS = 4
SLOTS = 4
low_type = jnp.bfloat16
wide_type = jnp.float32
NT = (((1,), (1,)), ((), ()))
NN = (((1,), (0,)), ((), ()))
TN = (((0,), (0,)), ((), ()))
SCALARS = pl.BlockSpec(memory_space=pltpu.SMEM)
HERE = pl.BlockSpec(memory_space=pltpu.VMEM)
ANYWHERE = pl.BlockSpec(memory_space=pl.ANY)


def swap_x(v):
    return lax.ppermute(v, "tp", [(0, 1), (1, 0)])


def swap_c(v):
    return lax.ppermute(v, "rows", [(0, 1), (1, 0), (2, 3), (3, 2)])


def swap_y(v):
    return lax.ppermute(v, "rows", [(0, 2), (2, 0), (1, 3), (3, 1)])


def swap_z(v, k):
    return lax.ppermute(v, "seq", [(i, i ^ k) for i in range(4)])


def low(v):
    return v.astype(low_type)


def wide(v):
    return v.astype(wide_type)


def shape(kind, *dims):
    return jax.ShapeDtypeStruct(dims, kind)


def dot(a, b, dims=NN):
    return lax.dot_general(a, b, dims, preferred_element_type=wide_type)


def add(a, b):
    return b if a is None else a + b


def pick(v, index, axis=0):
    return lax.dynamic_index_in_dim(v, index, axis, keepdims=False)


def part(v, index, count, axis):
    size = v.shape[axis] // count
    return lax.dynamic_slice_in_dim(v, index * size, size, axis)


def in_order(first, a, b, axis):
    return jnp.where(first, jnp.concatenate([a, b], axis), jnp.concatenate([b, a], axis))


def xor_order(pieces, z):
    odd = (z & 1) == 1
    high = (z & 2) == 2
    a, b, c, d = pieces
    a, b, c, d = jnp.where(odd, b, a), jnp.where(odd, a, b), jnp.where(odd, d, c), jnp.where(odd, c, d)
    a, b, c, d = jnp.where(high, c, a), jnp.where(high, d, b), jnp.where(high, a, c), jnp.where(high, b, d)
    return jnp.stack([a, b, c, d])


class Chain:
    def __init__(self, scalars):
        self.scalars = scalars
        self.token = None
        self.weight = 1.1e9

    def __call__(self, name, kernel, args, outs, us=1, spec=HERE, limit=8):
        before = () if self.token is None else (self.token,)
        count = len(args)

        def with_token(*refs):
            outs_at = 1 + count + len(before)
            refs[outs_at][...] = jnp.zeros((8, 128), wide_type)
            kernel(*refs[: 1 + count], *refs[outs_at + 1 :])

        made = pl.pallas_call(
            with_token,
            in_specs=[SCALARS] + [spec] * count + [HERE] * len(before),
            out_specs=[HERE] * (1 + len(outs)),
            out_shape=[shape(wide_type, 8, 128), *outs],
            compiler_params=pltpu.CompilerParams(vmem_limit_bytes=limit * 2**20),
            cost_estimate=pl.CostEstimate(flops=int(us * self.weight), bytes_accessed=1000, transcendentals=0),
            name=name,
        )(self.scalars, *args, *before)
        self.token = made[0]
        return made[1:]


def across_part(local, x):
    rows, tokens, width = local.shape
    return part(local.reshape(rows, SLOTS, tokens // SLOTS, width), x, 2, 1)


def core_rows(kept, sent, c):
    return in_order(c == 0, kept, swap_c(sent), 0)


def own_tokens(whole, place):
    z = place[3]
    pieces = [pick(whole, z)] + [swap_z(pick(whole, z ^ k), k) for k in (1, 2, 3)]
    return xor_order(pieces, z).reshape(-1, whole.shape[2])


def rows_over_z(own, place):
    z = place[3]
    blocks = own.reshape(BLOCKS, own.shape[0] // BLOCKS, own.shape[1])
    pieces = [pick(blocks, z)] + [swap_z(pick(blocks, z ^ k), k) for k in (1, 2, 3)]
    return xor_order(pieces, z)


def place_kernel(scalars, own_ref, core_ref, across_ref, last_ref, out):
    owner = scalars[0]
    for i, ref in enumerate((own_ref, core_ref, across_ref, last_ref)):
        out[:, owner ^ i] = ref[...]


def local_rows(rows, place, run):
    x, c, y, z = place
    own = part(rows, c, 2, 0)
    across = swap_x(own)
    core = swap_c(part(rows, 1 - c, 2, 0))
    last = swap_x(core)

    def assemble():
        count, sub, width = own.shape
        (full,) = run("place", place_kernel, (own, core, across, last), (shape(rows.dtype, count, SLOTS, sub, width),))
        return full.reshape(count, SLOTS * sub, width)

    return assemble


def row_pieces(own):
    across = [swap_x(piece) for piece in own]
    return [list(own), across, [swap_c(piece) for piece in own], [swap_c(piece) for piece in across]]


def flat(pieces):
    return [piece for slot in pieces for piece in slot]


def stacked(refs):
    return refs[0][...] if len(refs) == 1 else jnp.concatenate([ref[...] for ref in refs], 0)


def slots_of(refs):
    count = len(refs) // SLOTS
    return [stacked(refs[i * count : (i + 1) * count]) for i in range(SLOTS)]


def put_pieces(refs, value):
    rows = refs[0].shape[0]
    for i, ref in enumerate(refs):
        ref[...] = value[i * rows : (i + 1) * rows]


PIECES = 2


def piece_shapes(kind, rows, width, count=PIECES):
    return [shape(kind, rows // count, width)] * count


def half(ref, axis, c):
    size = ref.shape[axis] // 2
    at = pl.ds(pl.multiple_of(c * size, size), size)
    return ref[at, :] if axis == 0 else ref[:, at]


def slot_places(owner, index, sub):
    slot = index // sub
    return (owner ^ (((slot & 1) << 1) | (slot >> 1))) * sub + (index - slot * sub)


def row_positions(owner, sub):
    index = jnp.arange(SLOTS * BLOCKS * sub, dtype=jnp.int32)
    slot = index // (BLOCKS * sub)
    block = (index // sub) % BLOCKS
    own_place = (owner ^ (((slot & 1) << 1) | (slot >> 1))) * sub
    return block * SLOTS * sub + own_place + index % sub


def lane_tables(positions):
    lane = jnp.arange(128, dtype=jnp.int32) % HDIM
    frequency = jnp.exp((lane // 2).astype(wide_type) * (-2.0 * math.log(10000.0) / ROT))
    angles = positions.astype(wide_type)[:, None] * frequency[None, :]
    turned = (lane < ROT)[None, :]
    even = (lane % 2 == 0)[None, :]
    sines = jnp.sin(angles)
    return (
        jnp.where(turned, jnp.cos(angles), 1.0),
        jnp.where(turned & even, -sines, 0.0),
        jnp.where(turned & ~even, sines, 0.0),
    )


def turn_lanes(v, cosines, to_even, to_odd):
    return v * cosines + pltpu.roll(v, 127, 1) * to_even + pltpu.roll(v, 1, 1) * to_odd


def take_block(ref, block, sub, group):
    starts = [(slot * BLOCKS + block) * sub for slot in range(SLOTS)]
    return jnp.concatenate([ref[at : at + sub, group * 128 : (group + 1) * 128] for at in starts], 0)


def put_block(ref, block, sub, group, value):
    for slot in range(SLOTS):
        at = (slot * BLOCKS + block) * sub
        ref[at : at + sub, group * 128 : (group + 1) * 128] = value[slot * sub : (slot + 1) * sub]


def block_allowed(owner, size, sub):
    key_place = slot_places(owner, lax.broadcasted_iota(jnp.int32, (size, size), 0), sub)
    query_place = slot_places(owner, lax.broadcasted_iota(jnp.int32, (size, size), 1), sub)
    return query_place >= key_place


def normed_of(residual, gain_ref, bias_ref):
    centered = residual - jnp.mean(residual, -1, keepdims=True)
    inverse_std = lax.rsqrt(jnp.mean(centered * centered, -1, keepdims=True) + epsilon)
    return low(centered * inverse_std * gain_ref[...] + bias_ref[...])


def first_kernel(scalars, own_ref, gain_ref, bias_ref, cot_ref, kept_out, sent_out, *normed_outs):
    put_pieces(normed_outs, normed_of(wide(own_ref[...]), gain_ref, bias_ref))
    kept_out[...] = cot_ref[:, scalars[1]]
    sent_out[...] = cot_ref[:, 1 - scalars[1]]


def first_norm(own, params, cot, run):
    args = (own, params[0][None], params[1][None], cot)
    half_cot = shape(cot.dtype, cot.shape[0], *cot.shape[2:])
    kept, sent, *normed = run("first_norm", first_kernel, args, [half_cot] * 2 + piece_shapes(low_type, *own.shape))
    return (normed, kept, sent)


def settle_kernel(count, scalars, kept_ref, *refs):
    residual_ref, shift_ref, gain_ref, bias_ref, middle_out = refs[count : count + 5]
    middle = wide(residual_ref[...]) + (kept_ref[...] + wide(stacked(refs[:count]))) + shift_ref[...]
    middle_out[...] = middle
    put_pieces(refs[count + 5 :], normed_of(middle, gain_ref, bias_ref))


def settle(kept, got, residual, shift, gain, bias, run):
    args = (kept, *got, residual, shift[None], gain[None], bias[None])
    outs = [shape(wide_type, *kept.shape)] + piece_shapes(low_type, *kept.shape)
    middle, *normed = run("settle", functools.partial(settle_kernel, len(got)), args, outs)
    return (middle, normed)


def result_kernel(count, scalars, kept_ref, *refs):
    residual_ref, shift_ref, out = refs[count:]
    out[...] = low(residual_ref[...] + (kept_ref[...] + wide(stacked(refs[:count]))) + shift_ref[...])


def final_result(kept, got, residual, shift, run):
    args = (kept, *got, residual, shift[None])
    return run("result", functools.partial(result_kernel, len(got)), args, (shape(low_type, *kept.shape),))[0]


def settle_back_kernel(count, scalars, kept_ref, *refs):
    grad_ref, residual_ref, gain_ref, grad_out, shared_out = refs[count : count + 5]
    grad_normed = kept_ref[...] + wide(stacked(refs[:count]))
    grad_own = wide(grad_ref[...])
    residual = wide(residual_ref[...])
    centered = residual - jnp.mean(residual, -1, keepdims=True)
    inverse_std = lax.rsqrt(jnp.mean(centered * centered, -1, keepdims=True) + epsilon)
    unit_rows = centered * inverse_std
    grad_unit = grad_normed * gain_ref[...]
    pulled = grad_unit - jnp.mean(grad_unit, -1, keepdims=True)
    pulled = pulled - unit_rows * jnp.mean(grad_unit * unit_rows, -1, keepdims=True)
    grad_input = grad_own + inverse_std * pulled
    grad_out[...] = grad_input
    put_pieces(refs[count + 5 :], low(grad_input))
    shared_out[0:1] = jnp.sum(grad_normed * unit_rows, 0, keepdims=True)
    shared_out[1:2] = jnp.sum(grad_normed, 0, keepdims=True)
    shared_out[2:3] = jnp.sum(grad_own, 0, keepdims=True)


def settle_back(kept, got, grad_own, residual, gain, run, count=PIECES):
    args = (kept, *got, grad_own, residual, gain[None])
    outs = [shape(wide_type, *kept.shape), shape(wide_type, 3, kept.shape[1])]
    kernel = functools.partial(settle_back_kernel, len(got))
    grad, shared, *lows = run("settle_back", kernel, args, outs + piece_shapes(low_type, *kept.shape, count))
    return (grad, lows, shared)


def gelu_and_slope(u):
    root = math.sqrt(2.0 / math.pi)
    square = u * u
    bend = jnp.tanh(root * u * (1.0 + 0.044715 * square))
    half = 0.5 * (1.0 + bend)
    slope = half + 0.5 * u * (1.0 - bend * bend) * (root * (1.0 + 3.0 * 0.044715 * square))
    return (u * half, slope)


def project_kernel(with_back, count, scalars, *refs):
    slots = slots_of(refs[:count])
    wq_ref, wk_ref, wv_ref, wu_ref, bu_ref, cos_ref, even_ref, odd_ref = refs[count : count + 8]
    refs = refs[count + 8 :]
    if with_back:
        back_ref, full_out, q_out, k_out, v_out, hidden_out, slope_out, sum_out = refs
    else:
        full_out, q_out, k_out, v_out, hidden_out, slope_out = refs
    c = scalars[1]
    tile = slots[0].shape[0]
    shift = half(bu_ref, 1, c)
    for i, rows in enumerate(slots):
        here = slice(i * tile, (i + 1) * tile)
        full_out[here] = rows
        turns = (cos_ref[here], even_ref[here], odd_ref[here])
        for w_ref, out in ((wq_ref, q_out), (wk_ref, k_out)):
            product = dot(rows, half(w_ref, 1, c))
            for at in range(0, product.shape[1], 128):
                out[here, at : at + 128] = low(turn_lanes(product[:, at : at + 128], *turns))
        v_out[here] = low(dot(rows, half(wv_ref, 1, c)))
        preact = dot(rows, half(wu_ref, 1, c)) + shift
        hidden, slope = gelu_and_slope(preact)
        hidden_out[here] = low(hidden)
        if with_back:
            grad = wide(back_ref[here]) * slope
            slope_out[here] = low(grad)
            column = jnp.sum(grad, 0, keepdims=True)
            sum_out[...] = column if i == 0 else sum_out[...] + column
        else:
            slope_out[here] = low(slope)


def project_row(pieces, params, turns, run, back=None):
    w_query, w_key, w_value, w_up, b_up = (params[i] for i in (2, 3, 4, 6, 7))
    pieces = flat(pieces)
    rows, width = sum(piece.shape[0] for piece in pieces), pieces[0].shape[1]
    heads, units = w_query.shape[1] // 2, w_up.shape[1] // 2
    outs = [shape(low_type, rows, width)] + [shape(low_type, rows, heads)] * 3 + [shape(low_type, rows, units)] * 2
    args = (*pieces, w_query, w_key, w_value, w_up, b_up[None], *turns)
    if back is not None:
        args += (back,)
        outs.append(shape(wide_type, 1, units))
    return run("project", functools.partial(project_kernel, back is not None, len(pieces)), args, outs, 7.5)


def attend_kernel(sub, scalars, q_ref, k_ref, v_ref, c_out, log_out):
    scaling = 1.0 / math.sqrt(HDIM)
    size = SLOTS * sub
    allowed = block_allowed(scalars[0], size, sub)
    lane = lax.broadcasted_iota(jnp.int32, (1, 128), 1)
    for group in range(q_ref.shape[1] // 128):
        queries = [take_block(q_ref, block, sub, group) for block in range(BLOCKS)]
        keys = [take_block(k_ref, block, sub, group) for block in range(BLOCKS)]
        values = [take_block(v_ref, block, sub, group).T for block in range(BLOCKS)]
        for j in range(BLOCKS):
            contexts = []
            for head in range(128 // HDIM):
                of_head = lane // HDIM == head
                query = jnp.where(of_head, queries[j], jnp.zeros_like(queries[j]))
                scores = [dot(keys[i], query, NT) for i in range(j + 1)]
                scores[j] = jnp.where(allowed, scores[j], negative)
                tops = [jnp.max(s, 0, keepdims=True) for s in scores]
                top = functools.reduce(jnp.maximum, tops)
                weights = [jnp.exp2((s - top) * (scaling * math.log2(math.e))) for s in scores]
                total = functools.reduce(jnp.add, [jnp.sum(w, 0, keepdims=True) for w in weights])
                context = None
                for i in range(j + 1):
                    rows = values[i][head * HDIM : (head + 1) * HDIM]
                    context = add(context, dot(rows, low(weights[i])))
                contexts.append(context * (1.0 / total))
                log_row = group * (128 // HDIM) + head
                log_out[log_row : log_row + 1, j * size : (j + 1) * size] = top * scaling + jnp.log(total)
            put_block(c_out, j, sub, group, low(jnp.concatenate(contexts, 0).T))


def attend(queries, keys, values, run):
    rows, width = queries.shape
    kernel = functools.partial(attend_kernel, rows // (BLOCKS * SLOTS))
    outs = (shape(low_type, rows, width), shape(wide_type, width // HDIM, rows))
    return run("attend", kernel, (queries, keys, values), outs, 7.5)


def attend_back_kernel(
    sub, scalars, q_ref, k_ref, v_ref, g_ref, log_ref, cos_ref, even_ref, odd_ref, dq_out, dk_out, dv_out
):
    scaling = 1.0 / math.sqrt(HDIM)
    size = SLOTS * sub
    allowed = block_allowed(scalars[0], size, sub)
    lane = lax.broadcasted_iota(jnp.int32, (1, 128), 1)
    turns = []
    for block in range(BLOCKS):
        cosines, to_even, to_odd = [take_block(ref, block, sub, 0) for ref in (cos_ref, even_ref, odd_ref)]
        turns.append((cosines, -to_even, -to_odd))
    for group in range(q_ref.shape[1] // 128):
        queries, keys, values, grads = [
            [take_block(ref, block, sub, group) for block in range(BLOCKS)] for ref in (q_ref, k_ref, v_ref, g_ref)
        ]
        flat_keys = [k.T for k in keys]
        grad_keys = [None] * BLOCKS
        grad_values = [None] * BLOCKS
        for j in range(BLOCKS):
            grad_query = []
            for head in range(128 // HDIM):
                of_head = lane // HDIM == head
                query = jnp.where(of_head, queries[j], jnp.zeros_like(queries[j]))
                grad = jnp.where(of_head, grads[j], jnp.zeros_like(grads[j]))
                log_row = group * (128 // HDIM) + head
                log_total = log_ref[log_row : log_row + 1, j * size : (j + 1) * size] * math.log2(math.e)
                probs, grad_probs, delta = [], [], None
                for i in range(j + 1):
                    weights = jnp.exp2(dot(keys[i], query, NT) * (scaling * math.log2(math.e)) - log_total)
                    if i == j:
                        weights = jnp.where(allowed, weights, 0.0)
                    back = dot(values[i], grad, NT)
                    delta = add(delta, jnp.sum(weights * back, 0, keepdims=True))
                    probs.append(weights)
                    grad_probs.append(back)
                flat = None
                for i in range(j + 1):
                    grad_scores = low(probs[i] * (grad_probs[i] - delta))
                    grad_values[i] = add(grad_values[i], dot(low(probs[i]), grad))
                    grad_keys[i] = add(grad_keys[i], dot(grad_scores, query))
                    flat = add(flat, dot(flat_keys[i][head * HDIM : (head + 1) * HDIM], grad_scores))
                grad_query.append(flat)
            turned = jnp.concatenate(grad_query, 0).T * scaling
            put_block(dq_out, j, sub, group, low(turn_lanes(turned, *turns[j])))
        for i in range(BLOCKS):
            put_block(dk_out, i, sub, group, low(turn_lanes(grad_keys[i] * scaling, *turns[i])))
            put_block(dv_out, i, sub, group, low(grad_values[i]))


def attend_back_call(queries, keys, values, grad_context, logs, turns, run):
    rows, width = queries.shape
    kernel = functools.partial(attend_back_kernel, rows // (BLOCKS * SLOTS))
    args = (queries, keys, values, grad_context, logs, *turns)
    return run("attend_back", kernel, args, [shape(low_type, rows, width)] * 3, 0, limit=16)


def products(terms, weights, axis, c, start, stop):
    total = None
    for a_ref, w_ref in zip(terms, weights, strict=True):
        total = add(total, dot(a_ref[start:stop], half(w_ref, axis, c), NT if axis else NN))
    return total


def sent_kernel(axis, count, scalars, *refs):
    rows = refs[0].shape[0]
    put_pieces(refs[2 * count :], low(products(refs[:count], refs[count : 2 * count], axis, scalars[1], rows // 2, rows)))


def kept_kernel(axis, count, pieces, scalars, *refs):
    rows = refs[0].shape[0]
    tile = rows // SLOTS
    got_refs, (kept_out, *sent_outs) = refs[2 * count : 2 * count + pieces], refs[2 * count + pieces :]
    total = products(refs[:count], refs[count : 2 * count], axis, scalars[1], 0, rows // 2)
    put_pieces(sent_outs, low(total[tile:] + wide(stacked(got_refs[pieces // 2 :]))))
    kept_out[...] = total[:tile] + wide(stacked(got_refs[: pieces // 2]))


def send_part(terms, weights, axis, run):
    rows, width = terms[0].shape[0], weights[0].shape[1 - axis]
    kernel = functools.partial(sent_kernel, axis, len(terms))
    outs = piece_shapes(low_type, rows // 2, width, 2 * PIECES)
    return [swap_c(sent) for sent in run("sent", kernel, (*terms, *weights), outs, 2.5)]


def keep_part(terms, weights, axis, got, run, count=1):
    rows, width = terms[0].shape[0] // SLOTS, weights[0].shape[1 - axis]
    kernel = functools.partial(kept_kernel, axis, len(terms), len(got))
    outs = [shape(wide_type, rows, width)] + piece_shapes(low_type, rows, width, count)
    kept, *sent = run("kept", kernel, (*terms, *weights, *got), outs, 2.5)
    return (kept, [swap_x(piece) for piece in sent])


def raw_back_kernel(count, scalars, *refs):
    slots = slots_of(refs[:count])
    wo_ref, wd_ref, full_out, context_out, raw_out = refs[count:]
    tile = slots[0].shape[0]
    for i, rows in enumerate(slots):
        here = slice(i * tile, (i + 1) * tile)
        full_out[here] = rows
        context_out[here] = low(dot(rows, half(wo_ref, 0, scalars[1]), NT))
        raw_out[here] = low(dot(rows, half(wd_ref, 0, scalars[1]), NT))


def raw_back(pieces, params, run):
    w_out, w_down = params[5], params[8]
    pieces = flat(pieces)
    rows, width = sum(piece.shape[0] for piece in pieces), pieces[0].shape[1]
    outs = [shape(low_type, rows, n) for n in (width, w_out.shape[0] // 2, w_down.shape[0] // 2)]
    return run("raw_back", functools.partial(raw_back_kernel, len(pieces)), (*pieces, w_out, w_down), outs, 3.5)


def slopes_kernel(count, scalars, *refs):
    slots = slots_of(refs[:count])
    wo_ref, wd_ref, slope_ref, full_out, context_out, hidden_out, sum_out = refs[count:]
    tile = slots[0].shape[0]
    for i, rows in enumerate(slots):
        here = slice(i * tile, (i + 1) * tile)
        full_out[here] = rows
        context_out[here] = low(dot(rows, half(wo_ref, 0, scalars[1]), NT))
        grad = dot(rows, half(wd_ref, 0, scalars[1]), NT) * wide(slope_ref[here])
        hidden_out[here] = low(grad)
        column = jnp.sum(grad, 0, keepdims=True)
        sum_out[...] = column if i == 0 else sum_out[...] + column


def slopes(pieces, params, slope, run):
    w_out, w_down = params[5], params[8]
    pieces = flat(pieces)
    rows, width = sum(piece.shape[0] for piece in pieces), pieces[0].shape[1]
    units = w_down.shape[0] // 2
    outs = [shape(low_type, rows, n) for n in (width, w_out.shape[0] // 2, units)] + [shape(wide_type, 1, units)]
    return run("slopes", functools.partial(slopes_kernel, len(pieces)), (*pieces, w_out, w_down, slope), outs, 3.5)


def outer_kernel(counts, scalars, *refs):
    c, y, z = scalars[1], scalars[2], scalars[3]
    kept_out, sent_out = refs[-2:]
    at = 0
    refs = list(refs[:-2])
    for count in counts:
        left_ref = refs.pop(0)
        rights = [refs.pop(0) for _ in range(count)]
        tile = left_ref.shape[1] // 4
        piece = tile // 4
        total = sum(right.shape[1] for right in rights)
        for i in range(4):
            block = ((i >> 1) ^ (z & 1)) + 2 * ((i & 1) ^ (z >> 1))
            left = left_ref[:, pl.ds(pl.multiple_of(block * tile, tile), tile)]
            start = at
            for right_ref in rights:
                columns = slice(start, start + right_ref.shape[1])
                value = low(dot(left, right_ref[...], TN))
                a, b, d, e = [value[k * piece : (k + 1) * piece] for k in range(4)]
                a, b = jnp.where(c == 0, a, b), jnp.where(c == 0, b, a)
                d, e = jnp.where(c == 0, d, e), jnp.where(c == 0, e, d)
                for k, (upper, lower) in enumerate(((a, d), (b, e))):
                    rows = slice((2 * i + k) * piece, (2 * i + k + 1) * piece)
                    kept_out[rows, columns] = jnp.where(y == 0, upper, lower)
                    sent_out[rows, columns] = jnp.where(y == 0, lower, upper)
                start += right_ref.shape[1]
        at += total


class Reduction:
    hops = (swap_y, lambda v: swap_z(v, 1), lambda v: swap_z(v, 2), swap_c)

    def __init__(self, pairs, run):
        self.run = run
        self.at = 0
        total = sum(right.shape[1] for _, rights in pairs for right in rights)
        out = shape(low_type, pairs[0][0].shape[1] // 2, total)
        kernel = functools.partial(outer_kernel, [len(rights) for _, rights in pairs])
        args = [v for left, rights in pairs for v in (left, *rights)]
        self.kept, sent = run("outer", kernel, args, (out, out), 3 * total / 1024)
        self.got = self.hops[0](sent)

    def hop(self):
        out = shape(low_type, self.kept.shape[0] // 2, self.kept.shape[1])
        self.kept, sent = self.run("fold", fold_kernel, (self.kept, self.got), (out, out), 6)
        self.at += 1
        self.got = self.hops[self.at](sent)

    def finish(self, cuts, outs):
        kernel = functools.partial(finish_kernel, cuts)
        return self.run("finish", kernel, (self.kept, self.got), [shape(wide_type, *dims) for dims in outs])


def finish_kernel(cuts, scalars, kept_ref, got_ref, *outs):
    first = scalars[1] == 0
    start = 0
    for stop, out in zip(cuts, outs, strict=True):
        own, other = wide(kept_ref[:, start:stop]), wide(got_ref[:, start:stop])
        rows = own.shape[0]
        if out.shape[0] == rows and out.shape[1] == own.shape[1]:
            out[...] = own + other
        else:
            both = jnp.concatenate([jnp.where(first, own, other), jnp.where(first, other, own)], 1)
            out[...] = both
        start = stop


def fold_kernel(scalars, kept_ref, got_ref, kept_out, sent_out):
    half = kept_out.shape[0]
    kept_out[...] = low(wide(kept_ref[:half]) + wide(got_ref[:half]))
    sent_out[...] = low(wide(kept_ref[half:]) + wide(got_ref[half:]))


def small_kernel(scalars, shared_ref, *refs):
    out = refs[-1]
    first = scalars[1] == 0
    rows = [shared_ref[...]]
    for ref in refs[:-1]:
        sums = ref[...]
        for start in (0, 64):
            cuts = [sums[:, at + start : at + start + 64] for at in range(0, sums.shape[1], 128)]
            mine = jnp.concatenate(cuts, 1)
            none = jnp.zeros_like(mine)
            rows.append(jnp.where(first, jnp.concatenate([mine, none], 1), jnp.concatenate([none, mine], 1)))
    used = sum(row.shape[0] for row in rows)
    rows.append(jnp.zeros((out.shape[0] - used, out.shape[1]), wide_type))
    out[...] = low(jnp.concatenate(rows, 0))


def small_rows(shared, hidden_sums, run):
    return run("small", small_kernel, (shared, *hidden_sums), (shape(low_type, 16, shared.shape[1]),))[0]


def wait_kernel(scalars, *refs):
    pass


def split_kernel(scalars, ref, *outs):
    put_pieces(outs, ref[...])


def in_pieces(v, run):
    return run("split", split_kernel, (v,), piece_shapes(v.dtype, *v.shape))


def hold(run, *arrays):
    run("wait", wait_kernel, arrays, (), 0.5, ANYWHERE)


def quad_body(inputs, *rest):
    cotangent = rest[-1]
    r = lax.axis_index("rows")
    place = (lax.axis_index("tp"), r % 2, r // 2, lax.axis_index("seq"))
    x, c, y, z = place
    owner = 2 * x + c
    sub = inputs.shape[1] // SLOTS
    run = Chain(jnp.stack([owner, c, y, z, x]).astype(jnp.int32))
    one, two = rest[:10], rest[10:20]

    mine = across_part(inputs, x)
    start = own_tokens(core_rows(pick(mine, c, 1), pick(mine, 1 - c, 1), c), place)
    turns = lane_tables(row_positions(owner, sub))
    normed, cot_kept, cot_sent = first_norm(start, one, across_part(cotangent, x), run)
    pieces = row_pieces(normed)
    cot_own = own_tokens(core_rows(cot_kept, cot_sent, c), place)
    full_one, q1, k1, v1, hidden_one, slope_one = project_row(pieces, one, turns, run)
    cot_parts = in_pieces(cot_own, run)
    context_one, logs_one = attend(q1, k1, v1, run)
    cot_pieces = row_pieces(cot_parts)
    branch = ((context_one, hidden_one), (one[5], one[8]), 0)
    got = send_part(*branch, run)
    hold(run, *flat(cot_pieces))
    kept, got = keep_part(*branch, got, run)
    cot_full, grad_context, raw = raw_back(cot_pieces, two, run)
    middle, normed = settle(kept, got, start, one[9], two[0], two[1], run)

    full_two, q2, k2, v2, hidden_two, grad_hidden, sums_two = project_row(row_pieces(normed), two, turns, run, raw)
    run.weight = 0.28e9
    units_two = Reduction([(cot_full, (hidden_two,)), (full_two, (grad_hidden,))], run)
    context_two, logs_two = attend(q2, k2, v2, run)
    grads = attend_back_call(q2, k2, v2, grad_context, logs_two, turns, run)
    back = ((*grads, grad_hidden), (*two[2:5], two[6]), 1)
    got = send_part(*back, run)
    heads_two = Reduction([(cot_full, (context_two,)), (full_two, grads)], run)
    kept, got = keep_part(*back, got, run)
    branch = ((context_two, hidden_two), (two[5], two[8]), 0)
    res_got = send_part(*branch, run)
    width, units = q1.shape[1], hidden_one.shape[1]
    head_cut = [width, 2 * width, 3 * width, 4 * width]
    head_dims = (sub, 2 * width)
    grad_middle, grad_low, shared_two = settle_back(kept, got, cot_own, middle, two[0], run)
    pieces = row_pieces(grad_low)
    res_kept, res_got = keep_part(*branch, res_got, run)
    units_two.hop()
    grad_full, grad_context, grad_hidden, sums_one = slopes(pieces, one, slope_one, run)
    heads_two.hop()
    units_one = Reduction([(grad_full, (hidden_one,)), (full_one, (grad_hidden,))], run)
    result = final_result(res_kept, res_got, middle, two[9], run)
    out_rows = rows_over_z(result, place)
    outputs = local_rows(out_rows, place, run)
    grads = attend_back_call(q1, k1, v1, grad_context, logs_one, turns, run)
    back = ((*grads, grad_hidden), (*one[2:5], one[6]), 1)
    got = send_part(*back, run)
    hold(run, out_rows)
    units_two.hop()
    kept, got = keep_part(*back, got, run)
    heads_one = Reduction([(grad_full, (context_one,)), (full_one, grads)], run)
    heads_two.hop()
    grad_start, start_low, shared_one = settle_back(kept, got, grad_middle, start, one[0], run, 1)
    in_rows = rows_over_z(start_low[0], place)
    shared = jnp.concatenate([shared_one, shared_two], 0)
    shared = shared + swap_x(shared)
    input_grad = local_rows(in_rows, place, run)
    units_one.hop()
    small = small_rows(shared, [sums_one, sums_two], run)
    units_two.hop()
    heads_two.hop()
    last = Reduction([(small, (jnp.eye(16, 128, dtype=low_type),))], run)
    wd_two, wu_two = units_two.finish([units, 2 * units], [(sub, 2 * units)] * 2)
    hold(run, in_rows)
    wo_two, wq_two, wk_two, wv_two = heads_two.finish(head_cut, [head_dims] * 4)
    outputs = outputs()
    heads_one.hop()
    units_one.hop()
    last.hop()
    input_grad = input_grad()
    heads_one.hop()
    last.hop()
    units_one.hop()
    heads_one.hop()
    wd_one, wu_one = units_one.finish([units, 2 * units], [(sub, 2 * units)] * 2)
    last.hop()
    wo_one, wq_one, wk_one, wv_one = heads_one.finish(head_cut, [head_dims] * 4)
    (tail,) = last.finish([128], [(sub, 128)])
    columns = tail.T
    hidden_one, hidden_two = (columns[i : i + 2].reshape(-1) for i in (6, 8))
    return (
        outputs, input_grad,
        columns[0], columns[1], wq_one, wk_one, wv_one, wo_one.T, wu_one, hidden_one, wd_one.T, columns[2],
        columns[3], columns[4], wq_two, wk_two, wv_two, wo_two.T, wu_two, hidden_two, wd_two.T, columns[5],
    )


def solution(mesh):
    in_specs = (
        P("rows", "seq", None),
        P(),
        P(),
        P(None, "tp"),
        P(None, "tp"),
        P(None, "tp"),
        P("tp", None),
        P(None, "tp"),
        P("tp"),
        P("tp", None),
        P(),
        P(),
        P(),
        P(None, "tp"),
        P(None, "tp"),
        P(None, "tp"),
        P("tp", None),
        P(None, "tp"),
        P("tp"),
        P("tp", None),
        P(),
        P("rows", "seq", None),
    )
    out_specs = (
        P("rows", "seq", None),
        P("rows", "seq", None),
        P(("seq", "rows")),
        P(("seq", "rows")),
        P(("seq", "rows"), "tp"),
        P(("seq", "rows"), "tp"),
        P(("seq", "rows"), "tp"),
        P("tp", ("seq", "rows")),
        P(("seq", "rows"), "tp"),
        P(("tp", "seq", "rows")),
        P("tp", ("seq", "rows")),
        P(("seq", "rows")),
        P(("seq", "rows")),
        P(("seq", "rows")),
        P(("seq", "rows"), "tp"),
        P(("seq", "rows"), "tp"),
        P(("seq", "rows"), "tp"),
        P("tp", ("seq", "rows")),
        P(("seq", "rows"), "tp"),
        P(("tp", "seq", "rows")),
        P("tp", ("seq", "rows")),
        P(("seq", "rows")),
    )
    fits = (mesh.shape["seq"], mesh.shape["tp"], mesh.shape["rows"]) == (4, 2, 4)
    body = quad_body if fits else general_body
    return jax.shard_map(body, mesh=mesh, in_specs=in_specs, out_specs=out_specs, check_vma=False)
```
